256 devices in a mesh: section: 8 (over x, y_hi), tensor: 32 (over z, y_lo, core).
Axes of the slice: x: 4, y: 4 (y_hi: 2, y_lo: 2; y = y_hi * 2 + y_lo), z: 8, core: 2. Of those that a mesh axis runs over, the one named last changes fastest.
Arguments:
- latent_noise: bfloat16 [128, 8, 2432], P(None, 'section'), may hold values from -6 to 6
- score_noise: bfloat16 [128, 8, 2432], P(None, 'section'), may hold values from -6 to 6
- gen_time: int32 [8], replicated, may hold values from 0 to 999
- score_time: int32 [8], replicated, may hold values from 20 to 979
- w_mod: bfloat16 [3, 256, 7296], P(None, None, 'tensor'), may hold values from -0.375 to 0.375
- w_up: bfloat16 [3, 2432, 9728], P(None, None, 'tensor'), may hold values from -0.125 to 0.125
- b_up: float32 [3, 9728], P(None, 'tensor'), may hold values from -3 to 3
- w_down: bfloat16 [3, 9728, 2432], P(None, 'tensor'), may hold values from -0.0625 to 0.0625
- b_down: float32 [3, 2432], replicated, may hold values from -3 to 3
Outputs:
- grad_w1: float32 [2432, 9728], P('section', 'tensor')
- grad_w2: float32 [9728, 2432], P('tensor', 'section')
The draws below stay inside these ranges and needn't reach their ends.
All inputs are finite; a program needn't handle non-finite values.
Results may differ from the reference program's by a relative error of at most 0.014.
Values may be sent and summed in bfloat16 or wider, within the bound.
A program may use at most 64 MiB of HBM per device.

```python
import math
import jax
import jax.numpy as jnp
from jax import lax

D = 2432
FF = 9728
EMB = 256
TRAIN_STEPS = 1000
TOK_WIN = 128
SAMPLES = 8


def place_ends(entries, stream_key, smallest, top_value):
    shape = entries.shape
    spot = [jax.random.randint(jax.random.fold_in(stream_key, axis), (), 0, shape[axis]) for axis in range(len(shape))]
    entries = entries.at[tuple(spot)].set(smallest)
    longest = shape.index(max(shape))
    spot[longest] = (spot[longest] + 1) % shape[longest]
    return entries.at[tuple(spot)].set(top_value)


def strengthened(drawn, stream_key, source, target, shards_of, factor):
    owner, partner = [(jnp.arange(drawn.shape[position]) // (drawn.shape[position] // shards_of)).reshape([-1 if axis == position else 1 for axis in range(drawn.ndim)]) for position in (source, target)]
    chosen = jax.random.permutation(stream_key, shards_of)[partner]
    strong = (owner == chosen) | (owner == (partner + shards_of // 2) % shards_of)
    return jnp.where(strong, factor * drawn, drawn)


def levels(rng, shape, cuts, smallest, high):
    level = 1.0
    for dim, parts in cuts:
        steps = jax.random.uniform(jax.random.fold_in(jax.random.fold_in(rng, 6), dim), (parts,), jnp.float32, smallest / len(cuts), high / len(cuts))
        level = level * jnp.repeat(jnp.exp(steps), shape[dim] // parts).reshape((-1,) + (1,) * (len(shape) - 1 - dim))
    return level


def gaussian(stream_key, extent, width, limit, shards=(), kind=jnp.bfloat16):
    array = jax.random.normal(stream_key, extent, jnp.float32) * width
    if len(shards) > 0:
        array = levels(stream_key, extent, shards, -0.22, 0.18) * array
    return jnp.clip(array, min=-limit, max=limit).astype(kind)


def heavy_noise(key, shape, scale, most, split, heavy, dtype=jnp.bfloat16):
    drawn = scale * jax.random.normal(key, shape, jnp.float32)
    if split:
        drawn = drawn * levels(key, shape, split, -0.22, 0.18)
    return jnp.clip(strengthened(drawn, jax.random.fold_in(key, 3), *heavy), -most, most).astype(dtype)


def setup_inputs(seed: int = 0) -> dict:
    streams_of = jax.random.split(jax.random.key(seed), 10)
    latent_noise = heavy_noise(streams_of[0], (TOK_WIN, SAMPLES, D), 1.0, 6.0, ((1, 8),), (1, 2, 8, 2.0))
    score_noise = gaussian(streams_of[1], (TOK_WIN, SAMPLES, D), 1.0, 6.0, ((1, 8),))
    gen_time = place_ends(jax.random.randint(streams_of[2], (SAMPLES,), 0, TRAIN_STEPS), jax.random.fold_in(streams_of[2], 1), 0, TRAIN_STEPS - 1).astype(jnp.int32)
    score_time = place_ends(jax.random.randint(streams_of[3], (SAMPLES,), 20, TRAIN_STEPS - 20), jax.random.fold_in(streams_of[3], 1), 20, (TRAIN_STEPS - 20) - 1).astype(jnp.int32)
    w_mod = gaussian(streams_of[4], (3, EMB, 3 * D), EMB ** -0.5, 0.375, ((2, 32),))
    w_up = gaussian(streams_of[5], (3, D, FF), D ** -0.5, 0.125, ((2, 32),))
    b_up = gaussian(streams_of[6], (3, FF), 0.5, 3.0, ((1, 32),), jnp.float32)
    w_down = gaussian(streams_of[7], (3, FF, D), FF ** -0.5, 0.0625, ((1, 32),))
    b_down = gaussian(streams_of[8], (3, D), 0.5, 3.0, (), jnp.float32)
    return {"latent_noise": latent_noise, "score_noise": score_noise, "gen_time": gen_time, "score_time": score_time, "w_mod": w_mod, "w_up": w_up, "b_up": b_up, "w_down": w_down, "b_down": b_down}


tanh_scale = math.sqrt(2.0 / math.pi)
cubic_term = 0.044715

def smooth_gate(values):
    argument = tanh_scale * (values + cubic_term * values * values * values)
    return 0.5 * values * (1.0 + jnp.tanh(argument))

def smooth_slope(values):
    argument = tanh_scale * (values + cubic_term * values * values * values)
    bent = jnp.tanh(argument)
    return 0.5 * (1.0 + bent) + 0.5 * values * (1.0 - bent * bent) * tanh_scale * (1.0 + 3.0 * cubic_term * values * values)

def embed_times(stamps, emb_width):
    half_width = emb_width // 2
    indices = jnp.arange(half_width).astype(jnp.float32)
    frequency = jnp.exp(indices * (-math.log(10000.0) / half_width))
    angles = stamps.astype(jnp.float32)[:, None] * frequency[None, :]
    return jnp.concatenate([jnp.cos(angles), jnp.sin(angles)], axis=1).astype(jnp.bfloat16)

def modulate(activations, shift_vec, scale_vec):
    values = activations.astype(jnp.float32)
    average = lax.optimization_barrier(jnp.mean(values, axis=-1, keepdims=True))
    centred = values - average
    variance = lax.optimization_barrier(jnp.mean(centred * centred, axis=-1, keepdims=True))
    normed = centred * lax.rsqrt(variance + 1e-06)
    return (normed * (1.0 + scale_vec) + shift_vec).astype(jnp.bfloat16)

def split_three(modulation, model_width):
    return (modulation[:, :model_width], modulation[:, model_width:2 * model_width], modulation[:, 2 * model_width:])

def reference(latent_noise, score_noise, gen_time, score_time, w_mod, w_up, b_up, w_down, b_down):
    layout = latent_noise.shape
    model_width = layout[2]
    emb_gen = embed_times(gen_time, EMB)
    emb_score = embed_times(score_time, EMB)
    gen_shift, gen_scale, gen_gate = split_three(jnp.dot(emb_gen, w_mod[0], preferred_element_type=jnp.float32), model_width)
    real_shift, real_scale, real_gate = split_three(jnp.dot(emb_score, w_mod[1], preferred_element_type=jnp.float32), model_width)
    fake_shift, fake_scale, fake_gate = split_three(jnp.dot(emb_score, w_mod[2], preferred_element_type=jnp.float32), model_width)
    gen_inputs = modulate(latent_noise, gen_shift, gen_scale).reshape(-1, model_width)
    gen_preact = jnp.dot(gen_inputs, w_up[0], preferred_element_type=jnp.float32) + b_up[0]
    hidden_gen = smooth_gate(gen_preact).astype(jnp.bfloat16)
    gen_sum = jnp.dot(hidden_gen, w_down[0], preferred_element_type=jnp.float32).reshape(layout)
    generated = latent_noise.astype(jnp.float32) + gen_gate * (gen_sum + b_down[0])
    noise_level = (score_time.astype(jnp.float32) / TRAIN_STEPS)[None, :, None]
    noised = ((1.0 - noise_level) * generated + noise_level * score_noise.astype(jnp.float32)).astype(jnp.bfloat16)

    def score_update(network, shift_vec, scale_vec, gate_vec):
        inputs = modulate(noised, shift_vec, scale_vec).reshape(-1, model_width)
        preact = jnp.dot(inputs, w_up[network], preferred_element_type=jnp.float32) + b_up[network]
        hidden = smooth_gate(preact).astype(jnp.bfloat16)
        summed = jnp.dot(hidden, w_down[network], preferred_element_type=jnp.float32).reshape(layout)
        return gate_vec * (summed + b_down[network])
    contrast = score_update(2, fake_shift, fake_scale, fake_gate) - score_update(1, real_shift, real_scale, real_gate)
    cotangent = contrast / math.sqrt(SAMPLES * TOK_WIN)
    output_grad = (cotangent * gen_gate).astype(jnp.bfloat16).reshape(-1, model_width)
    hidden_grad = jnp.dot(output_grad, w_down[0].T, preferred_element_type=jnp.float32)
    preact_grad = (hidden_grad * smooth_slope(gen_preact)).astype(jnp.bfloat16)
    grad_w2 = jnp.dot(hidden_gen.T, output_grad, preferred_element_type=jnp.float32)
    grad_w1 = jnp.dot(gen_inputs.T, preact_grad, preferred_element_type=jnp.float32)
    return (grad_w1, grad_w2)
```

```python
import functools
import math

import jax
import jax.numpy as jnp
from jax import lax
from jax.experimental import pallas as pl
from jax.experimental.pallas import tpu as pltpu
from jax.sharding import PartitionSpec as P

TRAIN_STEPS = 1000
MESH = pl.DeviceIdType.MESH
f32 = jnp.float32
bf16 = jnp.bfloat16

NT = (((1,), (1,)), ((), ()))
NN = (((1,), (0,)), ((), ()))

tanh_scale = math.sqrt(2.0 / math.pi)
cubic_term = 0.044715

TOK = 128
D = 2432
DP = 2560
F = 304
MODC = 228
WIDTHS = (384, 256)
BASES = tuple(4 * sum(WIDTHS[:j]) for j in range(len(WIDTHS)))
NCH = len(WIDTHS)

CHIPS = [
    (dz, dy) for dz in (4, 3, 5, 2, 6, 1, 7, 0) for dy in (1, 0) if (dz, dy) != (0, 0)
]
SECTS = [(2, 1), (1, 1), (3, 1), (2, 0), (0, 1), (1, 0), (3, 0)]


def mul(value, factor):
    return pl.multiple_of(value * factor, factor)


def dot(a, b, dims):
    return lax.dot_general(a, b, dims, preferred_element_type=f32)


def gelu(v):
    return 0.5 * v * (1.0 + jnp.tanh(tanh_scale * (v + cubic_term * v * v * v)))


def slope(v):
    bent = jnp.tanh(tanh_scale * (v + cubic_term * v * v * v))
    return 0.5 * (1.0 + bent) + 0.5 * v * (1.0 - bent * bent) * tanh_scale * (
        1.0 + 3.0 * cubic_term * v * v
    )


class Sems:
    def __init__(self):
        self.count = 0

    def take(self, n):
        first = self.count
        self.count += n
        return first


SEMS = Sems()
LOAD = SEMS.take(16)
MX_S, MX_R = SEMS.take(1), SEMS.take(1)
MA_S, MA_R = SEMS.take(15), SEMS.take(15)
CX_S, CX_R = SEMS.take(4 * NCH), SEMS.take(4 * NCH)
RS_S, RS_R = SEMS.take(30 * NCH), SEMS.take(30 * NCH)
AG_S, AG_R = SEMS.take(30 * NCH), SEMS.take(30 * NCH)
FW_S, FW_R = SEMS.take(32 * NCH), SEMS.take(32 * NCH)
SX_S, SX_R = SEMS.take(28), SEMS.take(28)


def kernel(
    lat, noi, gt, st, wmod, wup, bup, wdn, bdn, o1, o2,
    latv, noiv, wmodv, wupv, wdnv, bupv, bdnv,
    mblk, mpart, mcomb, mall, modv,
    xn, xm, hid, prev, slope_t,
    psend, precv, csum, rsrecv, nbuf, gbuf,
    gen_t, og_t, g_all, h_all, p_all, o_all, pg, hid_t, res,
    sem,
):
    s = lax.axis_index("section")
    t = lax.axis_index("tensor")
    x, yh = s // 2, s % 2
    z, yl, c = t // 4, (t // 2) % 2, t % 2
    q = yl * 2 + c

    def chip_at(dz, dy):
        return lax.rem(z + dz, 8), lax.rem(yl + dy, 2)

    def chip_dev(dz, dy):
        z2, y2 = chip_at(dz, dy)
        return (s, z2 * 4 + y2 * 2 + c)

    def sect_at(dx, dy):
        return lax.rem(x + dx, 4) * 2 + lax.rem(yh + dy, 2)

    partner = (s, z * 4 + yl * 2 + (1 - c))

    def remote(src, dst, ssem, rsem, dev):
        return pltpu.make_async_remote_copy(
            src_ref=src, dst_ref=dst, send_sem=sem.at[ssem], recv_sem=sem.at[rsem],
            device_id=dev, device_id_type=MESH,
        )

    def load(k, src, dst):
        copy = pltpu.make_async_copy(src, dst, sem.at[LOAD + k])
        copy.start()
        return copy

    ld_wmod = load(0, wmod, wmodv)
    ld_lat = load(1, lat, latv.at[:, 0:D])
    ld_up = [load(2, wup.at[0], wupv.at[0])]
    ld_bup = load(3, bup, bupv)
    ld_dn = [load(4, wdn.at[0], wdnv.at[0])]
    ld_bdn = load(5, bdn, bdnv.at[:, 0:D])
    ld_noi = load(6, noi, noiv.at[:, 0:D])
    for n in (1, 2):
        ld_up.append(load(5 + 2 * n, wup.at[n], wupv.at[n]))
        ld_dn.append(load(6 + 2 * n, wdn.at[n], wdnv.at[n]))

    barrier = pltpu.get_barrier_semaphore()
    for dz, dy in CHIPS:
        pl.semaphore_signal(barrier, inc=1, device_id=chip_dev(dz, dy), device_id_type=MESH)
    for dx, dy in SECTS:
        pl.semaphore_signal(barrier, inc=1, device_id=(sect_at(dx, dy), t), device_id_type=MESH)
    pl.semaphore_signal(barrier, inc=1, device_id=partner, device_id_type=MESH)

    lane = lax.broadcasted_iota(jnp.int32, (8, 128), 1).astype(f32)
    freq = jnp.exp(lane * (-math.log(10000.0) / 128))

    def embed(stamp):
        angle = stamp.astype(f32) * freq
        return jnp.concatenate([jnp.cos(angle), jnp.sin(angle)], axis=1).astype(bf16)

    emb_gen = embed(gt[s])
    emb_score = embed(st[s])
    sigma = st[s].astype(f32) / TRAIN_STEPS
    ld_wmod.wait()
    row = lax.broadcasted_iota(jnp.int32, (8, MODC), 0)
    m0 = dot(emb_gen, wmodv[0], NT)
    m1 = dot(emb_score, wmodv[1], NT)
    m2 = dot(emb_score, wmodv[2], NT)
    mblk[...] = jnp.zeros_like(mblk)
    mblk[:, 0:MODC] = jnp.where(
        row % 4 == 0, m0, jnp.where(row % 4 == 1, m1, jnp.where(row % 4 == 2, m2, 0.0))
    )
    modv[...] = jnp.zeros_like(modv)
    pl.semaphore_wait(barrier, 23)

    mx = remote(mblk, mpart, MX_S, MX_R, partner)
    mx.start()
    mx.wait_recv()
    row8 = lax.broadcasted_iota(jnp.int32, (8, 256), 0)
    mcomb[...] = jnp.where((row8 < 4) == (c == 0), mblk[...], mpart[...])
    chip = z * 2 + yl
    ma = []
    for k, (dz, dy) in enumerate(CHIPS):
        copy = remote(mcomb, mall.at[chip], MA_S + k, MA_R + k, chip_dev(dz, dy))
        copy.start()
        ma.append(copy)
    mall[chip] = mcomb[...]

    latv[:, D:DP] = jnp.zeros((TOK, DP - D), bf16)
    noiv[:, D:DP] = jnp.zeros((TOK, DP - D), bf16)
    bdnv[:, D:DP] = jnp.zeros((3, DP - D), f32)
    ld_lat.wait()

    def norm_rows(values):
        mean = jnp.mean(values, axis=1, keepdims=True)
        centred = values - mean
        var = jnp.mean(centred * centred, axis=1, keepdims=True)
        return centred * lax.rsqrt(var + 1e-06)

    def norm_body(i, _):
        rows = pl.ds(mul(i, 16), 16)
        xn[rows, :] = norm_rows(latv[rows, 0:D].astype(f32))
        return 0

    lax.fori_loop(0, 8, norm_body, 0)
    for copy in ma:
        copy.wait_recv()
    for k in range(32):
        modv[0:3, MODC * k : MODC * (k + 1)] = mall[k // 2, 4 * (k % 2) : 4 * (k % 2) + 3, 0:MODC]

    def gen_body(i, _):
        rows = pl.ds(mul(i, 16), 16)
        xm[0, rows, :] = (xn[rows, :] * (1.0 + modv[0:1, D : 2 * D]) + modv[0:1, 0:D]).astype(bf16)
        return 0

    lax.fori_loop(0, 8, gen_body, 0)
    ld_up[0].wait()
    ld_bup.wait()
    pre = dot(xm[0], wupv[0], NT) + bupv[0:1, :]
    prev[:, 0:F] = pre
    hid[0] = gelu(pre).astype(bf16)
    ld_dn[0].wait()

    def chunk_cols(j):
        return BASES[j], min(BASES[j] + 4 * WIDTHS[j], D)

    def all_reduce(a, produce, finish, out, between):
        def core_copy(j, i):
            col = mul(BASES[j] // 128 + (i * 2 + 1 - c) * (WIDTHS[j] // 128), 128)
            k = (a * NCH + j) * 2 + i
            return remote(
                psend.at[a, :, pl.ds(col, WIDTHS[j])], precv[a][j].at[i], CX_S + k, CX_R + k, partner
            )

        def scatter(j, k):
            z2, y2 = chip_at(*CHIPS[k])
            i = (a * NCH + j) * 15 + k
            return remote(
                csum[a][j].at[y2, pl.ds(mul(z2, 16), 16), :], rsrecv[a][j].at[k],
                RS_S + i, RS_R + i, chip_dev(*CHIPS[k]),
            )

        def piece(ref, j, z2, y2):
            col = mul(BASES[j] // 128 + (y2 * 2 + c) * (WIDTHS[j] // 128), 128)
            return ref.at[pl.ds(mul(z2, 16), 16), pl.ds(col, WIDTHS[j])]

        def gather(j, k):
            own = piece(out, j, z, yl)
            i = (a * NCH + j) * 15 + k
            return remote(own, own, AG_S + i, AG_R + i, chip_dev(*CHIPS[k]))

        def forward(j, k):
            dz, dy = CHIPS[k] if k < 15 else (0, 0)
            z2, y2 = chip_at((8 - dz) % 8, dy)
            part = piece(out, j, z2, y2)
            i = (a * NCH + j) * 16 + k
            return remote(part, part, FW_S + i, FW_R + i, partner)

        def send_chunk(j):
            for i in range(2):
                core_copy(j, i).wait_recv()
            for i in range(2):
                col = mul(BASES[j] // 128 + (i * 2 + c) * (WIDTHS[j] // 128), 128)
                csum[a][j][i] = (
                    psend[a, :, pl.ds(col, WIDTHS[j])].astype(f32) + precv[a][j][i].astype(f32)
                ).astype(bf16)
            for k in range(15):
                scatter(j, k).start()

        for j in range(NCH):
            produce(j)
            for i in range(2):
                core_copy(j, i).start()
            if j >= 1:
                send_chunk(j - 1)
        send_chunk(NCH - 1)
        between()
        for j in range(NCH):
            total = csum[a][j][yl, pl.ds(mul(z, 16), 16), :].astype(f32)
            for k in reversed(range(15)):
                scatter(j, k).wait_recv()
                total = total + rsrecv[a][j][k].astype(f32)
            col = mul(BASES[j] // 128 + q * (WIDTHS[j] // 128), 128)
            piece(out, j, z, yl)[...] = finish(total, pl.ds(mul(z, 16), 16), col, WIDTHS[j])
            for k in range(15):
                gather(j, k).start()
            forward(j, 15).start()
        for j in range(NCH):
            for k in reversed(range(15)):
                gather(j, k).wait_recv()
                forward(j, k).start()
        for j in range(NCH):
            for k in reversed(range(16)):
                forward(j, k).wait_recv()

        def drain():
            for j in range(NCH):
                for i in range(2):
                    core_copy(j, i).wait_send()
                for k in range(15):
                    scatter(j, k).wait_send()
                    gather(j, k).wait_send()
                for k in range(16):
                    forward(j, k).wait_send()

        return drain

    def produce_gen(j):
        lo, hi = chunk_cols(j)
        psend[0, :, lo:hi] = dot(hid[0], wdnv[0, :, lo:hi], NN).astype(bf16)
        if hi < BASES[j] + 4 * WIDTHS[j]:
            psend[0, :, hi:DP] = jnp.zeros((TOK, DP - hi), bf16)

    def finish_gen(total, rows, col, width):
        cols = pl.ds(col, width)
        gate = modv[0:1, pl.ds(pl.multiple_of(2 * D + col, 128), width)]
        generated = latv[rows, cols].astype(f32) + gate * (total + bdnv[0:1, cols])
        return (
            (1.0 - sigma) * generated + sigma * noiv[rows, cols].astype(f32)
        ).astype(bf16)

    def sect_copy(part, k):
        dev = (sect_at(*SECTS[k]), t)
        i = part * 7 + k
        rows = pl.ds(mul(dev[0], F // 16 * 16), F)
        src = (gen_t.at[rows, :], hid_t, pg, og_t.at[rows, :])[part]
        dst = (g_all, h_all, p_all, o_all)[part].at[:, pl.ds(mul(s, 128), 128)]
        return remote(src, dst, SX_S + i, SX_R + i, dev)

    def transposed(value):
        return value.astype(f32).T

    def early_sends():
        ld_bdn.wait()
        ld_noi.wait()
        for b in range(19):
            cols = slice(128 * b, 128 * b + 128)
            gen_t[cols, :] = transposed(xm[0, :, cols]).astype(bf16)
        for k in range(7):
            sect_copy(0, k).start()
        g_all[:, pl.ds(mul(s, 128), 128)] = gen_t[pl.ds(mul(s, F), F), :]
        prev[:, F:384] = jnp.zeros((TOK, 384 - F), f32)
        for b in range(3):
            height = min(128, F - 128 * b)
            block = prev[:, 128 * b : 128 * b + 128].T
            slope_t[128 * b : 128 * b + height, :] = slope(block)[0:height]
            hid_t[128 * b : 128 * b + height, :] = gelu(block)[0:height].astype(bf16)
        for k in range(7):
            sect_copy(1, k).start()
        h_all[:, pl.ds(mul(s, 128), 128)] = hid_t[...]

    drain_gen = all_reduce(0, produce_gen, finish_gen, nbuf, early_sends)

    def score_body(i, _):
        rows = pl.ds(mul(i, 16), 16)
        normed = norm_rows(nbuf[rows, 0:D].astype(f32))
        for n in (1, 2):
            xm[n, rows, :] = (normed * (1.0 + modv[n : n + 1, D : 2 * D]) + modv[n : n + 1, 0:D]).astype(bf16)
        return 0

    lax.fori_loop(0, 8, score_body, 0)
    for n in (1, 2):
        ld_up[n].wait()
        hid[n] = gelu(dot(xm[n], wupv[n], NT) + bupv[n : n + 1, :]).astype(bf16)
    for n in (1, 2):
        ld_dn[n].wait()

    def produce_gap(j):
        lo, hi = chunk_cols(j)
        real = dot(hid[1], wdnv[1, :, lo:hi], NN) * modv[1:2, 2 * D + lo : 2 * D + hi]
        fake = dot(hid[2], wdnv[2, :, lo:hi], NN) * modv[2:3, 2 * D + lo : 2 * D + hi]
        psend[1, :, lo:hi] = (fake - real).astype(bf16)
        if hi < BASES[j] + 4 * WIDTHS[j]:
            psend[1, :, hi:DP] = jnp.zeros((TOK, DP - hi), bf16)

    def finish_gap(total, rows, col, width):
        cols = pl.ds(col, width)
        gates = modv[0:3, pl.ds(pl.multiple_of(2 * D + col, 128), width)]
        bias = gates[2:3] * bdnv[2:3, cols] - gates[1:2] * bdnv[1:2, cols]
        return ((total + bias) / 32.0 * gates[0:1]).astype(bf16)

    def drain_first():
        mx.wait_send()
        for copy in ma:
            copy.wait_send()
        drain_gen()
        for part in (0, 1):
            for k in range(7):
                sect_copy(part, k).wait_send()

    drain_gap = all_reduce(1, produce_gap, finish_gap, gbuf, drain_first)

    pg[...] = (dot(wdnv[0], gbuf[:, 0:D], NT) * slope_t[...]).astype(bf16)
    for k in range(7):
        sect_copy(2, k).start()
    p_all[:, pl.ds(mul(s, 128), 128)] = pg[...]
    for b in range(19):
        cols = slice(128 * b, 128 * b + 128)
        og_t[cols, :] = transposed(gbuf[:, cols]).astype(bf16)
    for k in range(7):
        sect_copy(3, k).start()
    o_all[:, pl.ds(mul(s, 128), 128)] = og_t[pl.ds(mul(s, F), F), :]
    drain_gap()
    for part in (0, 2):
        for k in reversed(range(7)):
            sect_copy(part, k).wait_recv()
    res[0] = dot(g_all[...], p_all[...], NT)
    out1 = pltpu.make_async_copy(res.at[0], o1, sem.at[LOAD + 12])
    out1.start()
    for part in (1, 3):
        for k in reversed(range(7)):
            sect_copy(part, k).wait_recv()
    res[1] = dot(h_all[...], o_all[...], NT)
    out2 = pltpu.make_async_copy(res.at[1], o2, sem.at[LOAD + 13])
    out2.start()
    for part in (2, 3):
        for k in range(7):
            sect_copy(part, k).wait_send()
    out1.wait()
    out2.wait()


def shards(latent_noise, score_noise, gen_time, score_time, w_mod, w_up, b_up, w_down, b_down):
    anywhere = pl.BlockSpec(memory_space=pl.ANY)
    scalars = pl.BlockSpec(memory_space=pltpu.SMEM)
    vm = pltpu.VMEM
    per_chunk = lambda lead: [[vm((lead, TOK, w), bf16) for w in WIDTHS] for _ in range(2)]
    scratch = [
        vm((TOK, DP), bf16), vm((TOK, DP), bf16), vm((3, MODC, 256), bf16),
        vm((3, F, D), bf16), vm((3, F, D), bf16), vm((3, F), f32), vm((3, DP), f32),
        vm((8, 256), f32), vm((8, 256), f32), vm((8, 256), f32), vm((16, 8, 256), f32),
        vm((8, 7424), f32),
        vm((TOK, D), f32), vm((3, TOK, D), bf16), vm((3, TOK, F), bf16), vm((TOK, 384), f32),
        vm((F, TOK), f32),
        vm((2, TOK, DP), bf16), per_chunk(2), per_chunk(2),
        [[vm((15, 16, w), bf16) for w in WIDTHS] for _ in range(2)],
        vm((TOK, DP), bf16), vm((TOK, DP), bf16),
        vm((D, TOK), bf16), vm((D, TOK), bf16),
        vm((F, 1024), bf16), vm((F, 1024), bf16), vm((F, 1024), bf16), vm((F, 1024), bf16),
        vm((F, TOK), bf16), vm((F, TOK), bf16), vm((2, F, F), f32),
        pltpu.SemaphoreType.DMA((SEMS.count,)),
    ]
    out = jax.ShapeDtypeStruct((F, F), f32)
    return pl.pallas_call(
        kernel,
        out_shape=(out, out),
        in_specs=[anywhere, anywhere, scalars, scalars] + [anywhere] * 5,
        out_specs=(anywhere, anywhere),
        scratch_shapes=scratch,
        cost_estimate=pl.CostEstimate(flops=1_700_000_000, bytes_accessed=11_000_000, transcendentals=300_000),
        compiler_params=pltpu.CompilerParams(
            collective_id=0, has_side_effects=True, vmem_limit_bytes=56 * 2**20
        ),
    )(
        latent_noise.reshape(TOK, D), score_noise.reshape(TOK, D), gen_time, score_time,
        w_mod.transpose(0, 2, 1), w_up.transpose(0, 2, 1), b_up, w_down, b_down,
    )


def solution(mesh):
    placed = (
        P(None, "section", None),
        P(None, "section", None),
        P(),
        P(),
        P(None, None, "tensor"),
        P(None, None, "tensor"),
        P(None, "tensor"),
        P(None, "tensor", None),
        P(),
    )
    return jax.shard_map(
        shards,
        mesh=mesh,
        in_specs=placed,
        out_specs=(P("section", "tensor"), P("tensor", "section")),
        check_vma=False,
    )
```

```python
import functools
import math

import jax
import jax.numpy as jnp
from jax import lax
from jax.experimental import pallas as pl
from jax.experimental.pallas import tpu as pltpu
from jax.sharding import PartitionSpec as P

TRAIN_STEPS = 1000
MESH = pl.DeviceIdType.MESH
f32 = jnp.float32
bf16 = jnp.bfloat16

NT = (((1,), (1,)), ((), ()))
NN = (((1,), (0,)), ((), ()))

tanh_scale = math.sqrt(2.0 / math.pi)
cubic_term = 0.044715

TOK = 128
D = 2432
DP = 2560
F = 304
MODC = 228
WIDTHS = (384, 256)
BASES = tuple(4 * sum(WIDTHS[:j]) for j in range(len(WIDTHS)))
NCH = len(WIDTHS)
STOP = 99
COPY_OUT = 0
BG = 1
LATE = 0
GRAD = bf16 if COPY_OUT else f32

DISTANCES = (0, 1, 7, 2, 6, 3, 5, 4)
CORES = [(dz, dy, dc) for dz in reversed(DISTANCES) for dy in (1, 0) for dc in (0, 1) if (dz, dy, dc) != (0, 0, 0)]
CHIPS = [(dz, dy) for dz in reversed(DISTANCES) for dy in (1, 0) if (dz, dy) != (0, 0)]
SECTS = [(2, 1), (1, 1), (3, 1), (2, 0), (0, 1), (1, 0), (3, 0)]


def mul(value, factor):
    return pl.multiple_of(value * factor, factor)


def dot(a, b, dims):
    return lax.dot_general(a, b, dims, preferred_element_type=f32)


def gelu(v):
    return 0.5 * v * (1.0 + jnp.tanh(tanh_scale * (v + cubic_term * v * v * v)))


def slope(v):
    bent = jnp.tanh(tanh_scale * (v + cubic_term * v * v * v))
    return 0.5 * (1.0 + bent) + 0.5 * v * (1.0 - bent * bent) * tanh_scale * (
        1.0 + 3.0 * cubic_term * v * v
    )


class Sems:
    def __init__(self):
        self.count = 0

    def take(self, n):
        first = self.count
        self.count += n
        return first


SEMS = Sems()
LOAD = SEMS.take(16)
MX_S, MX_R = SEMS.take(1), SEMS.take(1)
MA_S, MA_R = SEMS.take(1), SEMS.take(15)
CX_S, CX_R = SEMS.take(4 * NCH), SEMS.take(4 * NCH)
RS_S, RS_R = SEMS.take(2 * NCH), SEMS.take(30 * NCH)
AG_S, AG_R = SEMS.take(2 * NCH), SEMS.take(30 * NCH)
FW_S, FW_R = SEMS.take(2 * NCH), SEMS.take(32 * NCH)
SX_S, SX_R = SEMS.take(14), SEMS.take(14)
M0_S, M0_R = SEMS.take(1), SEMS.take(31)
XW_S, XW_R = SEMS.take(1), SEMS.take(7)
XF_S, XF_R = SEMS.take(1), SEMS.take(7)
SC_S, SC_R = SEMS.take(1), SEMS.take(7)
OX_S, OX_R = SEMS.take(7), SEMS.take(56)
OF_S, OF_R = SEMS.take(1), SEMS.take(7)


class Cut(Exception):
    pass


def kernel(*refs):
    sends = []
    arrivals = []
    try:
        steps(sends, arrivals, *refs)
    except Cut:
        for wait in arrivals:
            wait()
    for wait in sends:
        wait()


def steps(
    sends, arrivals,
    lat, noi, gt, st, wmod, wup, bup, wdn, bdn, o1, o2,
    latv, noiv, wmodv, wupv, wdnv, bupv, bdnv,
    m0row, m0all, mblk, mpart, mcomb, mall, modv, modx,
    xn, xw, xm, hid, prev, slope_t,
    psend, precv, csum, rsrecv, nbuf, gbuf,
    x_all, sc_all, g_t, h_all, p_all, o_all, pg, hid_t, res,
    sem,
):
    s = lax.axis_index("section")
    t = lax.axis_index("tensor")
    x, yh = s // 2, s % 2
    z, yl, c = t // 4, (t // 2) % 2, t % 2
    q = yl * 2 + c

    def cut(k):
        if STOP == k:
            raise Cut

    def flush():
        for wait in sends:
            wait()
        sends.clear()

    def chip_at(dz, dy):
        return lax.rem(z + dz, 8), lax.rem(yl + dy, 2)

    def chip_dev(dz, dy):
        z2, y2 = chip_at(dz, dy)
        return (s, z2 * 4 + y2 * 2 + c)

    def core_dev(dz, dy, dc):
        z2, y2 = chip_at(dz, dy)
        return (s, z2 * 4 + y2 * 2 + lax.rem(c + dc, 2))

    def sect_at(dx, dy):
        return lax.rem(x + dx, 4) * 2 + lax.rem(yh + dy, 2)

    partner = (s, z * 4 + yl * 2 + (1 - c))

    def remote(src, dst, ssem, rsem, dev):
        return pltpu.make_async_remote_copy(
            src_ref=src, dst_ref=dst, send_sem=sem.at[ssem], recv_sem=sem.at[rsem],
            device_id=dev, device_id_type=MESH,
        )

    def sent(ref, k):
        sends.append(lambda: pltpu.make_async_copy(ref, ref, sem.at[k]).wait())

    if STOP < 0:
        pl.semaphore_signal(pltpu.get_barrier_semaphore(), inc=1, device_id=partner, device_id_type=MESH)
        pl.semaphore_wait(pltpu.get_barrier_semaphore(), 1)
    cut(-1)

    def load(k, src, dst):
        copy = pltpu.make_async_copy(src, dst, sem.at[LOAD + k])
        copy.start()
        arrivals.append(copy.wait)

        def wait():
            arrivals.remove(copy.wait)
            copy.wait()

        return wait

    ld_wmod = load(0, wmod, wmodv)
    ld_lat = load(1, lat, latv.at[:, 0:D])
    ld_up = [load(2, wup.at[0], wupv.at[0])]
    ld_bup = load(3, bup, bupv)
    ld_dn = [load(4, wdn.at[0], wdnv.at[0])]
    ld_bdn = load(5, bdn, bdnv.at[:, 0:D])
    ld_noi = load(6, noi, noiv.at[:, 0:D])
    for n in (1, 2):
        ld_up.append(load(5 + 2 * n, wup.at[n], wupv.at[n]))
        ld_dn.append(load(6 + 2 * n, wdn.at[n], wdnv.at[n]))

    cut(-2)
    barrier = pltpu.get_barrier_semaphore()
    for dz, dy, dc in CORES:
        pl.semaphore_signal(barrier, inc=1, device_id=core_dev(dz, dy, dc), device_id_type=MESH)
    for dx, dy in SECTS:
        pl.semaphore_signal(barrier, inc=1, device_id=(sect_at(dx, dy), t), device_id_type=MESH)

    lane = lax.broadcasted_iota(jnp.int32, (8, 128), 1).astype(f32)
    freq = jnp.exp(lane * (-math.log(10000.0) / 128))

    def embed(stamp):
        angle = stamp.astype(f32) * freq
        return jnp.concatenate([jnp.cos(angle), jnp.sin(angle)], axis=1).astype(bf16)

    emb_gen = embed(gt[s])
    emb_score = embed(st[s])
    sigma = st[s].astype(f32) / TRAIN_STEPS
    ld_wmod()
    row = lax.broadcasted_iota(jnp.int32, (8, MODC), 0)
    m0 = dot(emb_gen, wmodv[0], NT)
    m1 = dot(emb_score, wmodv[1], NT)
    m2 = dot(emb_score, wmodv[2], NT)
    m0row[...] = jnp.zeros_like(m0row)
    m0row[:, 0:MODC] = m0[0:1]
    mblk[...] = jnp.zeros_like(mblk)
    mblk[:, 0:MODC] = jnp.where(row % 4 == 1, m1, jnp.where(row % 4 == 2, m2, 0.0))
    modv[...] = jnp.zeros_like(modv)
    modx[...] = jnp.zeros_like(modx)
    latv[:, D:DP] = jnp.zeros((TOK, DP - D), bf16)
    noiv[:, D:DP] = jnp.zeros((TOK, DP - D), bf16)
    bdnv[:, D:DP] = jnp.zeros((3, DP - D), f32)
    ld_lat()

    def norm_rows(values):
        mean = jnp.mean(values, axis=1, keepdims=True)
        centred = values - mean
        var = jnp.mean(centred * centred, axis=1, keepdims=True)
        return centred * lax.rsqrt(var + 1e-06)

    def norm_body(i, _):
        rows = pl.ds(mul(i, 16), 16)
        normed = norm_rows(latv[rows, 0:D].astype(f32))
        xn[rows, :] = normed
        xw[rows, 0:D] = normed.astype(bf16)
        return 0

    lax.fori_loop(0, 8, norm_body, 0)
    xw[:, D:DP] = jnp.zeros((TOK, DP - D), bf16)
    pl.semaphore_wait(barrier, 38)
    cut(0)

    me = z * 4 + yl * 2 + c
    m0 = []
    for k, (dz, dy, dc) in enumerate(CORES):
        copy = remote(m0row, m0all.at[me], M0_S, M0_R + k, core_dev(dz, dy, dc))
        copy.start()
        m0.append(copy)
    sent(m0all.at[0:31], M0_S)
    mx = remote(mblk, mpart, MX_S, MX_R, partner)
    mx.start()
    sends.append(mx.wait_send)
    m0all[me] = m0row[...]

    def first_lane(section, half):
        return mul((19 * section) // 8 + 2 * half, 128)

    def window_copy(k):
        dev = (sect_at(*SECTS[k]), t)
        return remote(
            xw.at[:, pl.ds(first_lane(dev[0], c), 256)], x_all.at[s, :, pl.ds(mul(c, 256), 256)],
            XW_S, XW_R + k, dev,
        )

    def from_sect(k):
        dx, dy = SECTS[k]
        return sect_at((4 - dx) % 4, dy)

    def window_forward(k):
        part = x_all.at[from_sect(k), :, pl.ds(mul(c, 256), 256)]
        return remote(part, part, XF_S, XF_R + k, partner)

    def scale_copy(k):
        dev = (sect_at(*SECTS[k]), t)
        return remote(modx.at[:, pl.ds(first_lane(dev[0], 0), 512)], sc_all.at[s], SC_S, SC_R + k, dev)

    mx.wait_recv()
    row8 = lax.broadcasted_iota(jnp.int32, (8, 256), 0)
    mcomb[...] = jnp.where((row8 < 4) == (c == 0), mblk[...], mpart[...])
    chip = z * 2 + yl
    ma = []
    for k, (dz, dy) in enumerate(CHIPS):
        copy = remote(mcomb, mall.at[chip], MA_S, MA_R + k, chip_dev(dz, dy))
        copy.start()
        ma.append(copy)
        arrivals.append(copy.wait_recv)
    sent(mall.at[0:15], MA_S)
    mall[chip] = mcomb[...]
    for k in range(7 * BG):
        window_copy(k).start()
        arrivals.append(lambda k=k: window_copy(k).wait_recv())
    if BG:
        sent(x_all.at[0:7, :, 0:256], XW_S)
    x_all[s] = xw[:, pl.ds(first_lane(s, 0), 512)]
    for copy in m0:
        copy.wait_recv()
    for k in range(32):
        modv[0:1, MODC * k : MODC * (k + 1)] = m0all[k, :, 0:MODC]
    cut(1)

    def gen_body(i, _):
        rows = pl.ds(mul(i, 16), 16)
        xm[0, rows, :] = (xn[rows, :] * (1.0 + modv[0:1, D : 2 * D]) + modv[0:1, 0:D]).astype(bf16)
        return 0

    lax.fori_loop(0, 8, gen_body, 0)
    modx[0:1, 0:D] = modv[0:1, D : 2 * D]
    modx[1:2, 0:D] = modv[0:1, 0:D]
    for k in range(7 * BG):
        scale_copy(k).start()
        arrivals.append(lambda k=k: scale_copy(k).wait_recv())
    if BG:
        sent(sc_all.at[0:7], SC_S)
    sc_all[s] = modx[:, pl.ds(first_lane(s, 0), 512)]
    ld_up[0]()
    ld_bup()
    pre = dot(xm[0], wupv[0], NT) + bupv[0:1, :]
    prev[:, 0:F] = pre
    hid[0] = gelu(pre).astype(bf16)
    ld_dn[0]()
    cut(2)

    def chunk_cols(j):
        return BASES[j], min(BASES[j] + 4 * WIDTHS[j], D)

    def all_reduce(a, produce, finish, out, between, on_rows):
        def core_copy(j, i):
            col = mul(BASES[j] // 128 + (i * 2 + 1 - c) * (WIDTHS[j] // 128), 128)
            k = (a * NCH + j) * 2 + i
            return remote(
                psend.at[a, :, pl.ds(col, WIDTHS[j])], precv[a][j].at[i], CX_S + k, CX_R + k, partner
            )

        def scatter(j, k):
            z2, y2 = chip_at(*CHIPS[k])
            i = a * NCH + j
            return remote(
                csum[a][j].at[y2, pl.ds(mul(z2, 16), 16), :], rsrecv[a][j].at[k],
                RS_S + i, RS_R + i * 15 + k, chip_dev(*CHIPS[k]),
            )

        def piece(ref, j, z2, y2):
            col = mul(BASES[j] // 128 + (y2 * 2 + c) * (WIDTHS[j] // 128), 128)
            return ref.at[pl.ds(mul(z2, 16), 16), pl.ds(col, WIDTHS[j])]

        def gather(j, k):
            own = piece(out, j, z, yl)
            i = a * NCH + j
            return remote(own, own, AG_S + i, AG_R + i * 15 + k, chip_dev(*CHIPS[k]))

        def forward(j, k):
            dz, dy = CHIPS[k] if k < 15 else (0, 0)
            z2, y2 = chip_at((8 - dz) % 8, dy)
            part = piece(out, j, z2, y2)
            i = a * NCH + j
            return remote(part, part, FW_S + i, FW_R + i * 16 + k, partner)

        def send_chunk(j):
            for i in range(2):
                core_copy(j, i).wait_recv()
            for i in range(2):
                col = mul(BASES[j] // 128 + (i * 2 + c) * (WIDTHS[j] // 128), 128)
                csum[a][j][i] = (
                    psend[a, :, pl.ds(col, WIDTHS[j])].astype(f32) + precv[a][j][i].astype(f32)
                ).astype(bf16)
            for k in range(15):
                scatter(j, k).start()
            sent(rsrecv[a][j], RS_S + a * NCH + j)

        for j in range(NCH):
            produce(j)
            for i in range(2):
                core_copy(j, i).start()
                sends.append(core_copy(j, i).wait_send)
            if j >= 1:
                send_chunk(j - 1)
        send_chunk(NCH - 1)
        between()
        for j in range(NCH):
            total = csum[a][j][yl, pl.ds(mul(z, 16), 16), :].astype(f32)
            for k in reversed(range(15)):
                scatter(j, k).wait_recv()
                total = total + rsrecv[a][j][k].astype(f32)
            col = mul(BASES[j] // 128 + q * (WIDTHS[j] // 128), 128)
            piece(out, j, z, yl)[...] = finish(total, pl.ds(mul(z, 16), 16), col, WIDTHS[j])
            if STOP == 3 + 3 * a:
                continue
            for k in range(15):
                gather(j, k).start()
            sent(rsrecv[a][j], AG_S + a * NCH + j)
            forward(j, 15).start()
        cut(3 + 3 * a)

        def moves(dz):
            return [CHIPS.index((dz, dy)) if (dz, dy) != (0, 0) else 15 for dy in (0, 1)]

        def finish_rows(dz):
            for j in range(NCH):
                for k in moves(dz):
                    forward(j, k).wait_recv()
            on_rows(lax.rem(z + 8 - dz, 8), dz)

        for step, dz in enumerate(DISTANCES):
            for j in range(NCH):
                for k in moves(dz):
                    if k < 15:
                        gather(j, k).wait_recv()
                        forward(j, k).start()
            if step >= 1:
                finish_rows(DISTANCES[step - 1])
        finish_rows(DISTANCES[-1])
        for j in range(NCH):
            sent(precv[a][j], FW_S + a * NCH + j)

    def produce_gen(j):
        lo, hi = chunk_cols(j)
        psend[0, :, lo:hi] = dot(hid[0], wdnv[0, :, lo:hi], NN).astype(bf16)
        if hi < BASES[j] + 4 * WIDTHS[j]:
            psend[0, :, hi:DP] = jnp.zeros((TOK, DP - hi), bf16)

    def finish_gen(total, rows, col, width):
        cols = pl.ds(col, width)
        gate = modv[0:1, pl.ds(pl.multiple_of(2 * D + col, 128), width)]
        generated = latv[rows, cols].astype(f32) + gate * (total + bdnv[0:1, cols])
        return (
            (1.0 - sigma) * generated + sigma * noiv[rows, cols].astype(f32)
        ).astype(bf16)

    def sect_copy(part, k):
        dev = (sect_at(*SECTS[k]), t)
        i = part * 7 + k
        src = (hid_t, pg)[part]
        dst = (h_all, p_all)[part].at[:, pl.ds(mul(s, 128), 128)]
        return remote(src, dst, SX_S + i, SX_R + i, dev)

    def relay_copy(k):
        dx, dy = SECTS[k]
        part = h_all.at[:, pl.ds(mul(sect_at(0, 1), 128), 128)]
        return remote(part, part, SX_S + k, SX_R + k, (sect_at(dx, 0), t))

    direct = [k for k in range(7) if SECTS[k][1] == 0] + [SECTS.index((0, 1))]
    relayed = [k for k in range(7) if k not in direct]

    def early_sends():
        ld_bdn()
        ld_noi()
        prev[:, F:384] = jnp.zeros((TOK, 384 - F), f32)
        for b in range(3):
            height = min(128, F - 128 * b)
            block = prev[:, 128 * b : 128 * b + 128].T
            slope_t[128 * b : 128 * b + height, :] = slope(block)[0:height]
            hid_t[128 * b : 128 * b + height, :] = gelu(block)[0:height].astype(bf16)
        for k in direct if BG else []:
            sect_copy(0, k).start()
            sends.append(sect_copy(0, k).wait_send)
        h_all[:, pl.ds(mul(s, 128), 128)] = hid_t[...]
        for copy in ma:
            arrivals.remove(copy.wait_recv)
            copy.wait_recv()
        for k in range(32):
            modv[1:3, MODC * k : MODC * (k + 1)] = mall[k // 2, 4 * (k % 2) + 1 : 4 * (k % 2) + 3, 0:MODC]
        for k in reversed(range(7 * BG)):
            window_copy(k).wait_recv()
            window_forward(k).start()
        if BG:
            sent(x_all.at[0:7, :, 0:256], XF_S)

    def relay_hidden():
        if BG:
            sect_copy(0, SECTS.index((0, 1))).wait_recv()
            for k in relayed:
                relay_copy(k).start()
                sends.append(relay_copy(k).wait_send)

    def gather_inputs():
        flush()
        for k in range(7 * BG):
            window_forward(k).wait_recv()
            scale_copy(k).wait_recv()

        def body(i, _):
            values = x_all[i].astype(f32) * (1.0 + sc_all[i, 0:1, :]) + sc_all[i, 1:2, :]
            values = values.astype(bf16).astype(f32)
            for b in range(4):
                block = values[:, 128 * b : 128 * b + 128].T
                g_t[128 * b : 128 * b + 128, pl.ds(mul(i, 128), 128)] = block.astype(bf16)
            return 0

        lax.fori_loop(0, 8, body, 0)

    def score_rows(z2, dz):
        rows = pl.ds(mul(z2, 16), 16)
        normed = norm_rows(nbuf[rows, 0:D].astype(f32))
        for n in (1, 2):
            xm[n, rows, :] = (normed * (1.0 + modv[n : n + 1, D : 2 * D]) + modv[n : n + 1, 0:D]).astype(bf16)

    all_reduce(0, produce_gen, finish_gen, nbuf, early_sends, score_rows)
    relay_hidden()
    cut(4)

    for n in (1, 2):
        ld_up[n]()
        hid[n] = gelu(dot(xm[n], wupv[n], NT) + bupv[n : n + 1, :]).astype(bf16)
    for n in (1, 2):
        ld_dn[n]()
    cut(5)

    def produce_gap(j):
        lo, hi = chunk_cols(j)
        real = dot(hid[1], wdnv[1, :, lo:hi], NN) * modv[1:2, 2 * D + lo : 2 * D + hi]
        fake = dot(hid[2], wdnv[2, :, lo:hi], NN) * modv[2:3, 2 * D + lo : 2 * D + hi]
        psend[1, :, lo:hi] = (fake - real).astype(bf16)
        if hi < BASES[j] + 4 * WIDTHS[j]:
            psend[1, :, hi:DP] = jnp.zeros((TOK, DP - hi), bf16)

    def finish_gap(total, rows, col, width):
        cols = pl.ds(col, width)
        gates = modv[0:3, pl.ds(pl.multiple_of(2 * D + col, 128), width)]
        bias = gates[2:3] * bdnv[2:3, cols] - gates[1:2] * bdnv[1:2, cols]
        return ((total + bias) / 32.0 * gates[0:1]).astype(bf16)

    def slice_copy(z2, dz, k):
        dev = (sect_at(*SECTS[k]), t)
        rows = pl.ds(mul(z2, 16), 16)
        return remote(
            gbuf.at[rows, pl.ds(first_lane(dev[0], c), 256)],
            o_all.at[s, rows, pl.ds(mul(c, 256), 256)],
            OX_S + k, OX_R + 8 * k + dz, dev,
        )

    def slice_forward(k):
        part = o_all.at[from_sect(k), :, pl.ds(mul(c, 256), 256)]
        return remote(part, part, OF_S, OF_R + k, partner)

    def grad_rows(z2, dz):
        for k in range(7 * BG * (1 - LATE)):
            slice_copy(z2, dz, k).start()
            arrivals.append(lambda dz=dz, k=k: slice_copy(z, dz, k).wait_recv())
        rows = pl.ds(mul(z2, 16), 16)
        o_all[s, rows, :] = gbuf[rows, pl.ds(first_lane(s, 0), 512)]

    all_reduce(1, produce_gap, finish_gap, gbuf, gather_inputs, grad_rows)
    for k in range(7 * BG):
        sent(o_all.at[0, :, 0:256], OX_S + k)
    cut(7)

    pg[...] = (dot(wdnv[0], gbuf[:, 0:D], NT) * slope_t[...]).astype(bf16)
    for k in range(7):
        sect_copy(1, k).start()
    if LATE:
        for dz in DISTANCES:
            for k in range(7 * BG):
                slice_copy(lax.rem(z + 8 - dz, 8), dz, k).start()
    p_all[:, pl.ds(mul(s, 128), 128)] = pg[...]
    for k in reversed(range(7 * BG)):
        for dz in DISTANCES:
            slice_copy(z, dz, k).wait_recv()
        slice_forward(k).start()
    flush()
    for k in range(7):
        sends.append(sect_copy(1, k).wait_send)
    if BG:
        sent(o_all.at[0:7, :, 0:256], OF_S)
    for k in reversed(range(7 * BG)):
        (relay_copy(k) if k in relayed else sect_copy(0, k)).wait_recv() if k != SECTS.index((0, 1)) else None
        slice_forward(k).wait_recv()
    wide = dot(h_all[...], o_all[...].reshape(1024, 512), NN)
    shift = lax.rem(48 * s, 128)
    res[1] = pltpu.roll(wide, lax.rem(512 - shift, 512), 1)[:, 0:F].astype(GRAD)
    out2 = pltpu.make_async_copy(res.at[1], o2, sem.at[LOAD + 13])
    out2.start()
    for k in reversed(range(7)):
        sect_copy(1, k).wait_recv()
    res[0] = dot(g_t[pl.ds(pl.multiple_of(shift, 16), F), :], p_all[...], NT).astype(GRAD)
    out1 = pltpu.make_async_copy(res.at[0], o1, sem.at[LOAD + 12])
    out1.start()
    flush()
    out1.wait()
    out2.wait()


def shards(latent_noise, score_noise, gen_time, score_time, w_mod, w_up, b_up, w_down, b_down):
    anywhere = pl.BlockSpec(memory_space=pl.ANY)
    scalars = pl.BlockSpec(memory_space=pltpu.SMEM)
    vm = pltpu.VMEM
    per_chunk = lambda lead: [[vm((lead, TOK, w), bf16) for w in WIDTHS] for _ in range(2)]
    scratch = [
        vm((TOK, DP), bf16), vm((TOK, DP), bf16), vm((3, MODC, 256), bf16),
        vm((3, F, D), bf16), vm((3, F, D), bf16), vm((3, F), f32), vm((3, DP), f32),
        vm((1, 256), f32), vm((32, 1, 256), f32),
        vm((8, 256), f32), vm((8, 256), f32), vm((8, 256), f32), vm((16, 8, 256), f32),
        vm((8, 7424), f32), vm((8, DP), f32),
        vm((TOK, D), f32), vm((TOK, DP), bf16), vm((3, TOK, D), bf16), vm((3, TOK, F), bf16), vm((TOK, 384), f32),
        vm((F, TOK), f32),
        vm((2, TOK, DP), bf16), per_chunk(2), per_chunk(2),
        [[vm((15, 16, w), bf16) for w in WIDTHS] for _ in range(2)],
        vm((TOK, DP), bf16), vm((TOK, DP), bf16),
        vm((8, TOK, 512), bf16), vm((8, 8, 512), f32), vm((512, 1024), bf16),
        vm((F, 1024), bf16), vm((F, 1024), bf16), vm((8, TOK, 512), bf16),
        vm((F, TOK), bf16), vm((F, TOK), bf16), vm((2, F, F), GRAD),
        pltpu.SemaphoreType.DMA((SEMS.count,)),
    ]
    out = jax.ShapeDtypeStruct((F, F), GRAD)
    grads = pl.pallas_call(
        kernel,
        out_shape=(out, out),
        in_specs=[anywhere, anywhere, scalars, scalars] + [anywhere] * 5,
        out_specs=(anywhere, anywhere),
        scratch_shapes=scratch,
        cost_estimate=pl.CostEstimate(flops=1_700_000_000, bytes_accessed=11_000_000, transcendentals=300_000),
        compiler_params=pltpu.CompilerParams(
            collective_id=0, has_side_effects=True, vmem_limit_bytes=56 * 2**20
        ),
    )(
        latent_noise.reshape(TOK, D), score_noise.reshape(TOK, D), gen_time, score_time,
        w_mod.transpose(0, 2, 1), w_up.transpose(0, 2, 1), b_up, w_down, b_down,
    )
    if COPY_OUT:
        return tuple(grad.astype(f32) for grad in grads)
    return grads


def solution(mesh):
    placed = (
        P(None, "section", None),
        P(None, "section", None),
        P(),
        P(),
        P(None, None, "tensor"),
        P(None, None, "tensor"),
        P(None, "tensor"),
        P(None, "tensor", None),
        P(),
    )
    return jax.shard_map(
        shards,
        mesh=mesh,
        in_specs=placed,
        out_specs=(P("section", "tensor"), P("tensor", "section")),
        check_vma=False,
    )
```

```python
import functools
import math

import jax
import jax.numpy as jnp
from jax import lax
from jax.experimental import pallas as pl
from jax.experimental.pallas import tpu as pltpu
from jax.sharding import PartitionSpec as P

TRAIN_STEPS = 1000
MESH = pl.DeviceIdType.MESH
f32 = jnp.float32
bf16 = jnp.bfloat16

NT = (((1,), (1,)), ((), ()))
NN = (((1,), (0,)), ((), ()))

tanh_scale = math.sqrt(2.0 / math.pi)
cubic_term = 0.044715

TOK = 128
D = 2432
DP = 2560
F = 304
MODC = 228
W = DP // 4
STOP = 99
BG = 1

FAR = (4, 3, 5, 2, 6, 1, 7, 0)
CORES = [(dz, dy, dc) for dz in FAR for dy in (1, 0) for dc in (0, 1) if (dz, dy, dc) != (0, 0, 0)]
CHIPS = [(dz, dy) for dz in FAR for dy in (1, 0) if (dz, dy) != (0, 0)]
SECTS = [(2, 1), (1, 1), (3, 1), (2, 0), (0, 1), (1, 0), (3, 0)]


def mul(value, factor):
    return pl.multiple_of(value * factor, factor)


def dot(a, b, dims):
    return lax.dot_general(a, b, dims, preferred_element_type=f32)


def gelu(v):
    return 0.5 * v * (1.0 + jnp.tanh(tanh_scale * (v + cubic_term * v * v * v)))


def slope(v):
    bent = jnp.tanh(tanh_scale * (v + cubic_term * v * v * v))
    return 0.5 * (1.0 + bent) + 0.5 * v * (1.0 - bent * bent) * tanh_scale * (
        1.0 + 3.0 * cubic_term * v * v
    )


class Sems:
    def __init__(self):
        self.count = 0

    def take(self, n):
        first = self.count
        self.count += n
        return first


SEMS = Sems()
LOAD = SEMS.take(16)
MX_S, MX_R = SEMS.take(1), SEMS.take(1)
MA_S, MA_R = SEMS.take(1), SEMS.take(15)
CX_S, CX_R = SEMS.take(8), SEMS.take(8)
RS_S, RS_R = SEMS.take(2), SEMS.take(32)
AG_S, AG_R = SEMS.take(2), SEMS.take(32)
FW_S, FW_R = SEMS.take(2), SEMS.take(32)
SX_S, SX_R = SEMS.take(21), SEMS.take(21)
M0_S, M0_R = SEMS.take(1), SEMS.take(31)
XW_S, XW_R = SEMS.take(1), SEMS.take(7)
XF_S, XF_R = SEMS.take(1), SEMS.take(7)
SC_S, SC_R = SEMS.take(1), SEMS.take(7)
OX_S, OX_R = SEMS.take(7), SEMS.take(56)
OF_S, OF_R = SEMS.take(1), SEMS.take(7)


HALVES = ((0, 160), (160, F))


class Cut(Exception):
    pass


def kernel(*refs):
    sends = []
    arrivals = []
    try:
        steps(sends, arrivals, *refs)
    except Cut:
        for wait in arrivals:
            wait()
    for wait in sends:
        wait()


def steps(
    sends, arrivals,
    lat, noi, gt, st, wmod, wup, bup, wdn, bdn, out,
    latv, noiv, wmodv, wupv, wdnv, bupv, bdnv,
    m0row, m0all, mblk, mpart, mcomb, mall, modv, modx,
    xn, xw, xm, hid, prev, slope_t,
    psend, precv, csum, rsrecv, nbuf, gbuf,
    x_all, sc_all, g_t, h_all, p_all, o_all, pg, hid_t, res,
    sem,
):
    s = lax.axis_index("section")
    t = lax.axis_index("tensor")
    x, yh = s // 2, s % 2
    z, yl, c = t // 4, (t // 2) % 2, t % 2
    q = yl * 2 + c

    def cut(k):
        if STOP == k:
            raise Cut

    def flush():
        for wait in sends:
            wait()
        sends.clear()

    def chip_at(dz, dy):
        return lax.rem(z + dz, 8), lax.rem(yl + dy, 2)

    def chip_dev(dz, dy):
        z2, y2 = chip_at(dz, dy)
        return (s, z2 * 4 + y2 * 2 + c)

    def core_dev(dz, dy, dc):
        z2, y2 = chip_at(dz, dy)
        return (s, z2 * 4 + y2 * 2 + lax.rem(c + dc, 2))

    def sect_at(dx, dy):
        return lax.rem(x + dx, 4) * 2 + lax.rem(yh + dy, 2)

    partner = (s, z * 4 + yl * 2 + (1 - c))

    def remote(src, dst, ssem, rsem, dev):
        return pltpu.make_async_remote_copy(
            src_ref=src, dst_ref=dst, send_sem=sem.at[ssem], recv_sem=sem.at[rsem],
            device_id=dev, device_id_type=MESH,
        )

    def sent(ref, k):
        sends.append(lambda: pltpu.make_async_copy(ref, ref, sem.at[k]).wait())

    if STOP < 0:
        pl.semaphore_signal(pltpu.get_barrier_semaphore(), inc=1, device_id=partner, device_id_type=MESH)
        pl.semaphore_wait(pltpu.get_barrier_semaphore(), 1)
    cut(-1)

    def row_of(z2):
        return mul((z2 % 2) * 4 + z2 // 2, 16)

    def load_tokens(k, src, dst):
        for b in range(8):
            row = 16 * ((b % 2) * 4 + b // 2)
            pltpu.make_async_copy(src.at[16 * b : 16 * b + 16, :], dst.at[row : row + 16, 0:D], sem.at[LOAD + k]).start()
        whole = pltpu.make_async_copy(dst.at[:, 0:D], dst.at[:, 0:D], sem.at[LOAD + k])
        arrivals.append(whole.wait)

        def wait():
            arrivals.remove(whole.wait)
            whole.wait()

        return wait

    def load(k, src, dst):
        copy = pltpu.make_async_copy(src, dst, sem.at[LOAD + k])
        copy.start()
        arrivals.append(copy.wait)

        def wait():
            arrivals.remove(copy.wait)
            copy.wait()

        return wait

    ld_wmod = load(0, wmod, wmodv)
    ld_lat = load_tokens(1, lat, latv)
    ld_up = [load(2, wup.at[0], wupv.at[0])]
    ld_bup = load(3, bup, bupv)
    ld_dn = [load(4, wdn.at[0], wdnv.at[0])]
    ld_bdn = load(5, bdn, bdnv.at[:, 0:D])
    ld_noi = load_tokens(6, noi, noiv)
    for n in (1, 2):
        ld_up.append(load(5 + 2 * n, wup.at[n], wupv.at[n]))
        ld_dn.append(load(6 + 2 * n, wdn.at[n], wdnv.at[n]))

    cut(-2)
    barrier = pltpu.get_barrier_semaphore()
    for dz, dy, dc in CORES:
        pl.semaphore_signal(barrier, inc=1, device_id=core_dev(dz, dy, dc), device_id_type=MESH)
    for dx, dy in SECTS:
        pl.semaphore_signal(barrier, inc=1, device_id=(sect_at(dx, dy), t), device_id_type=MESH)

    lane = lax.broadcasted_iota(jnp.int32, (8, 128), 1).astype(f32)
    freq = jnp.exp(lane * (-math.log(10000.0) / 128))

    def embed(stamp):
        angle = stamp.astype(f32) * freq
        return jnp.concatenate([jnp.cos(angle), jnp.sin(angle)], axis=1).astype(bf16)

    emb_gen = embed(gt[s])
    emb_score = embed(st[s])
    sigma = st[s].astype(f32) / TRAIN_STEPS
    ld_wmod()
    row = lax.broadcasted_iota(jnp.int32, (8, MODC), 0)
    m0 = dot(emb_gen, wmodv[0], NT)
    m1 = dot(emb_score, wmodv[1], NT)
    m2 = dot(emb_score, wmodv[2], NT)
    m0row[...] = jnp.zeros_like(m0row)
    m0row[:, 0:MODC] = m0[0:1]
    mblk[...] = jnp.zeros_like(mblk)
    mblk[:, 0:MODC] = jnp.where(row % 4 == 1, m1, jnp.where(row % 4 == 2, m2, 0.0))
    modv[...] = jnp.zeros_like(modv)
    modx[...] = jnp.zeros_like(modx)
    latv[:, D:DP] = jnp.zeros((TOK, DP - D), bf16)
    noiv[:, D:DP] = jnp.zeros((TOK, DP - D), bf16)
    bdnv[:, D:DP] = jnp.zeros((3, DP - D), f32)
    for a in range(2):
        psend[a, :, D:DP] = jnp.zeros((TOK, DP - D), bf16)
    ld_lat()

    def norm_rows(values):
        mean = jnp.mean(values, axis=1, keepdims=True)
        centred = values - mean
        var = jnp.mean(centred * centred, axis=1, keepdims=True)
        return centred * lax.rsqrt(var + 1e-06)

    def norm_body(i, _):
        rows = pl.ds(mul(i, 16), 16)
        normed = norm_rows(latv[rows, 0:D].astype(f32))
        xn[rows, :] = normed
        xw[rows, 0:D] = normed.astype(bf16)
        return 0

    lax.fori_loop(0, 8, norm_body, 0)
    xw[:, D:DP] = jnp.zeros((TOK, DP - D), bf16)
    pl.semaphore_wait(barrier, 38)
    cut(0)

    me = z * 4 + yl * 2 + c
    m0 = []
    for k, (dz, dy, dc) in enumerate(CORES):
        copy = remote(m0row, m0all.at[me], M0_S, M0_R + k, core_dev(dz, dy, dc))
        copy.start()
        m0.append(copy)
    sent(m0all.at[0:31], M0_S)
    mx = remote(mblk, mpart, MX_S, MX_R, partner)
    mx.start()
    sends.append(mx.wait_send)
    m0all[me] = m0row[...]

    def first_lane(section, half):
        return mul((19 * section) // 8 + 2 * half, 128)

    def window_copy(k):
        dev = (sect_at(*SECTS[k]), t)
        return remote(
            xw.at[:, pl.ds(first_lane(dev[0], c), 256)], x_all.at[s, :, pl.ds(mul(c, 256), 256)],
            XW_S, XW_R + k, dev,
        )

    def from_sect(k):
        dx, dy = SECTS[k]
        return sect_at((4 - dx) % 4, dy)

    def window_forward(k):
        part = x_all.at[from_sect(k), :, pl.ds(mul(c, 256), 256)]
        return remote(part, part, XF_S, XF_R + k, partner)

    def scale_copy(k):
        dev = (sect_at(*SECTS[k]), t)
        return remote(modx.at[:, pl.ds(first_lane(dev[0], 0), 512)], sc_all.at[s], SC_S, SC_R + k, dev)

    mx.wait_recv()
    row8 = lax.broadcasted_iota(jnp.int32, (8, 256), 0)
    mcomb[...] = jnp.where((row8 < 4) == (c == 0), mblk[...], mpart[...])
    chip = z * 2 + yl
    ma = []
    for k, (dz, dy) in enumerate(CHIPS):
        copy = remote(mcomb, mall.at[chip], MA_S, MA_R + k, chip_dev(dz, dy))
        copy.start()
        ma.append(copy)
        arrivals.append(copy.wait_recv)
    sent(mall.at[0:15], MA_S)
    mall[chip] = mcomb[...]
    for k in range(7 * BG):
        window_copy(k).start()
        arrivals.append(lambda k=k: window_copy(k).wait_recv())
    if BG:
        sent(x_all.at[0:7, :, 0:256], XW_S)
    x_all[s] = xw[:, pl.ds(first_lane(s, 0), 512)]
    for copy in m0:
        copy.wait_recv()
    for k in range(32):
        modv[0:1, MODC * k : MODC * (k + 1)] = m0all[k, :, 0:MODC]
    cut(1)

    def gen_body(i, _):
        rows = pl.ds(mul(i, 16), 16)
        xm[0, rows, :] = (xn[rows, :] * (1.0 + modv[0:1, D : 2 * D]) + modv[0:1, 0:D]).astype(bf16)
        return 0

    lax.fori_loop(0, 8, gen_body, 0)
    modx[0:1, 0:D] = modv[0:1, D : 2 * D]
    modx[1:2, 0:D] = modv[0:1, 0:D]
    for k in range(7 * BG):
        scale_copy(k).start()
        arrivals.append(lambda k=k: scale_copy(k).wait_recv())
    if BG:
        sent(sc_all.at[0:7], SC_S)
    sc_all[s] = modx[:, pl.ds(first_lane(s, 0), 512)]
    ld_up[0]()
    ld_bup()
    pre = dot(xm[0], wupv[0], NT) + bupv[0:1, :]
    prev[:, 0:F] = pre
    hid[0] = gelu(pre).astype(bf16)
    ld_dn[0]()
    cut(2)

    def quarter(y2, core):
        return pl.ds(mul((y2 * 2 + core) * (W // 128), 128), W)

    def core_copy(a, h, i):
        rows = pl.ds(64 * h, 64)
        k = (a * 2 + h) * 2 + i
        return remote(
            psend.at[a, rows, quarter(i, 1 - c)], precv.at[a, i, rows, :], CX_S + k, CX_R + k, partner
        )

    def core_send(a, h):
        for i in range(2):
            core_copy(a, h, i).start()
            sends.append(core_copy(a, h, i).wait_send)

    def start_scatter(a, h):
        rows = pl.ds(64 * h, 64)
        for i in range(2):
            core_copy(a, h, i).wait_recv()
        for i in range(2):
            csum[a, i, rows, :] = (
                psend[a, rows, quarter(i, c)].astype(f32) + precv[a, i, rows, :].astype(f32)
            ).astype(bf16)
        odd = lax.rem(z + h, 2)
        for m in (2, 1, 3, 0):
            for dy in (1, 0):
                dz = 2 * m + odd
                z2, y2 = chip_at(dz, dy)
                copy = remote(
                    csum.at[a, y2, pl.ds(row_of(z2), 16), :], rsrecv.at[a, dz * 2 + dy],
                    RS_S + a, RS_R + a * 16 + dz * 2 + dy, chip_dev(dz, dy),
                )
                if (m, dy) == (0, 0):
                    pl.when(odd == 1)(copy.start)
                else:
                    copy.start()

    def piece(out, z2, y2):
        return out.at[pl.ds(row_of(z2), 16), quarter(y2, c)]

    def forward(a, out, dz, dy):
        z2, y2 = chip_at(8 - dz, dy)
        part = piece(out, z2, y2)
        return remote(part, part, FW_S + a, FW_R + a * 16 + dz * 2 + dy, partner)

    def gather(a, out, dz, dy):
        own = piece(out, z, yl)
        return remote(own, own, AG_S + a, AG_R + a * 16 + dz * 2 + dy, chip_dev(dz, dy))

    def reduce(a, finish, out):
        rows = pl.ds(row_of(z), 16)
        total = csum[a, yl, rows, :].astype(f32)
        for dz, dy in reversed(CHIPS):
            slot = rsrecv.at[a, dz * 2 + dy]
            remote(slot, slot, RS_S + a, RS_R + a * 16 + dz * 2 + dy, partner).wait_recv()
            total = total + slot[...].astype(f32)
        sent(rsrecv.at[a, 0:15], RS_S + a)
        piece(out, z, yl)[...] = finish(total, rows, mul(q * (W // 128), 128), W)
        for dz, dy in CHIPS:
            gather(a, out, dz, dy).start()
        forward(a, out, 0, 0).start()
        sent(rsrecv.at[a, 0:15], AG_S + a)

    def gather_rows(a, h, out, on_rows):
        odd = lax.rem(z + h, 2)

        def complete(m):
            dz = 2 * m + odd
            for dy in (0, 1):
                forward(a, out, dz, dy).wait_recv()
            on_rows(lax.rem(z + 8 - dz, 8), dz)

        before = None
        for m in (0, 3, 1, 2):
            dz = 2 * m + odd
            for dy in (0, 1):

                def pass_on():
                    gather(a, out, dz, dy).wait_recv()
                    forward(a, out, dz, dy).start()

                if (m, dy) == (0, 0):
                    pl.when(odd == 1)(pass_on)
                else:
                    pass_on()
            if before is not None:
                complete(before)
            before = m
        complete(before)
        if h == 1:
            sent(precv.at[a], FW_S + a)

    def produce_gen(h):
        rows = slice(64 * h, 64 * h + 64)
        psend[0, rows, 0:D] = dot(hid[0, rows], wdnv[0], NN).astype(bf16)

    def finish_gen(total, rows, col, width):
        cols = pl.ds(col, width)
        gate = modv[0:1, pl.ds(pl.multiple_of(2 * D + col, 128), width)]
        generated = latv[rows, cols].astype(f32) + gate * (total + bdnv[0:1, cols])
        return (
            (1.0 - sigma) * generated + sigma * noiv[rows, cols].astype(f32)
        ).astype(bf16)

    def sect_copy(part, k):
        dev = (sect_at(*SECTS[k]), t)
        i = part * 7 + k
        cols = pl.ds(mul(s, 128), 128)
        if part == 0:
            src, dst = hid_t, h_all.at[:, cols]
        else:
            lo, hi = HALVES[part - 1]
            src, dst = pg.at[lo:hi, :], p_all.at[lo:hi, cols]
        return remote(src, dst, SX_S + i, SX_R + i, dev)

    def relay_copy(k):
        dx, dy = SECTS[k]
        part = h_all.at[:, pl.ds(mul(sect_at(0, 1), 128), 128)]
        return remote(part, part, SX_S + k, SX_R + k, (sect_at(dx, 0), t))

    direct = [k for k in range(7) if SECTS[k][1] == 0] + [SECTS.index((0, 1))]
    relayed = [k for k in range(7) if k not in direct]

    def early_sends():
        ld_bdn()
        ld_noi()
        prev[:, F:384] = jnp.zeros((TOK, 384 - F), f32)
        for b in range(3):
            height = min(128, F - 128 * b)
            block = prev[:, 128 * b : 128 * b + 128].T
            slope_t[128 * b : 128 * b + height, :] = slope(block)[0:height]
            hid_t[128 * b : 128 * b + height, :] = gelu(block)[0:height].astype(bf16)
        for k in direct if BG else []:
            sect_copy(0, k).start()
            sends.append(sect_copy(0, k).wait_send)
        h_all[:, pl.ds(mul(s, 128), 128)] = hid_t[...]
        for copy in ma:
            arrivals.remove(copy.wait_recv)
            copy.wait_recv()
        for k in range(32):
            modv[1:3, MODC * k : MODC * (k + 1)] = mall[k // 2, 4 * (k % 2) + 1 : 4 * (k % 2) + 3, 0:MODC]
        for k in reversed(range(7 * BG)):
            window_copy(k).wait_recv()
            window_forward(k).start()
        if BG:
            sent(x_all.at[0:7, :, 0:256], XF_S)

    def relay_hidden():
        if BG:
            sect_copy(0, SECTS.index((0, 1))).wait_recv()
            for k in relayed:
                relay_copy(k).start()
                sends.append(relay_copy(k).wait_send)

    def gather_inputs():
        flush()
        for k in range(7 * BG):
            window_forward(k).wait_recv()
            scale_copy(k).wait_recv()

        def body(i, _):
            values = x_all[i].astype(f32) * (1.0 + sc_all[i, 0:1, :]) + sc_all[i, 1:2, :]
            values = values.astype(bf16).astype(f32)
            for b in range(4):
                block = values[:, 128 * b : 128 * b + 128].T
                g_t[128 * b : 128 * b + 128, pl.ds(mul(i, 128), 128)] = block.astype(bf16)
            return 0

        lax.fori_loop(0, 8, body, 0)

    def score_rows(z2, dz):
        rows = pl.ds(row_of(z2), 16)
        normed = norm_rows(nbuf[rows, 0:D].astype(f32))
        for n in (1, 2):
            xm[n, rows, :] = (normed * (1.0 + modv[n : n + 1, D : 2 * D]) + modv[n : n + 1, 0:D]).astype(bf16)

    for h in range(2):
        produce_gen(h)
        core_send(0, h)
    for h in range(2):
        start_scatter(0, h)
    early_sends()
    reduce(0, finish_gen, nbuf)
    relay_hidden()

    def score_hidden(h):
        rows = slice(64 * h, 64 * h + 64)
        for n in (1, 2):
            hid[n, rows] = gelu(dot(xm[n, rows], wupv[n], NT) + bupv[n : n + 1, :]).astype(bf16)

    def produce_gap(h):
        rows = slice(64 * h, 64 * h + 64)
        real = dot(hid[1, rows], wdnv[1], NN) * modv[1:2, 2 * D : 3 * D]
        fake = dot(hid[2, rows], wdnv[2], NN) * modv[2:3, 2 * D : 3 * D]
        psend[1, rows, 0:D] = (fake - real).astype(bf16)

    for wait in ld_up[1:] + ld_dn[1:]:
        wait()
    gather_rows(0, 0, nbuf, score_rows)
    score_hidden(0)
    produce_gap(0)
    core_send(1, 0)
    gather_rows(0, 1, nbuf, score_rows)
    start_scatter(1, 0)
    score_hidden(1)
    produce_gap(1)
    core_send(1, 1)
    start_scatter(1, 1)

    def finish_gap(total, rows, col, width):
        cols = pl.ds(col, width)
        gates = modv[0:3, pl.ds(pl.multiple_of(2 * D + col, 128), width)]
        bias = gates[2:3] * bdnv[2:3, cols] - gates[1:2] * bdnv[1:2, cols]
        return ((total + bias) / 32.0 * gates[0:1]).astype(bf16)

    def slice_copy(z2, dz, k):
        dev = (sect_at(*SECTS[k]), t)
        rows = pl.ds(row_of(z2), 16)
        return remote(
            gbuf.at[rows, pl.ds(first_lane(dev[0], c), 256)],
            o_all.at[s, rows, pl.ds(mul(c, 256), 256)],
            OX_S + k, OX_R + 8 * k + dz, dev,
        )

    def slice_forward(k):
        part = o_all.at[from_sect(k), :, pl.ds(mul(c, 256), 256)]
        return remote(part, part, OF_S, OF_R + k, partner)

    def grad_rows(z2, dz):
        for k in range(7 * BG):
            slice_copy(z2, dz, k).start()
            arrivals.append(lambda dz=dz, k=k: slice_copy(z, dz, k).wait_recv())
        rows = pl.ds(row_of(z2), 16)
        o_all[s, rows, :] = gbuf[rows, pl.ds(first_lane(s, 0), 512)]

    gather_inputs()
    reduce(1, finish_gap, gbuf)
    for h in range(2):
        gather_rows(1, h, gbuf, grad_rows)
    for k in range(7 * BG):
        sent(o_all.at[0, :, 0:256], OX_S + k)
    cut(7)

    for part, (lo, hi) in enumerate(HALVES):
        pg[lo:hi, :] = (dot(wdnv[0, lo:hi], gbuf[:, 0:D], NT) * slope_t[lo:hi, :]).astype(bf16)
        for k in range(7):
            sect_copy(1 + part, k).start()
    p_all[:, pl.ds(mul(s, 128), 128)] = pg[...]
    for k in reversed(range(7 * BG)):
        for dz in reversed(FAR):
            slice_copy(z, dz, k).wait_recv()
        slice_forward(k).start()
    flush()
    for k in range(7):
        for part in (1, 2):
            sends.append(sect_copy(part, k).wait_send)
    if BG:
        sent(o_all.at[0:7, :, 0:256], OF_S)
    for k in reversed(range(7 * BG)):
        (relay_copy(k) if k in relayed else sect_copy(0, k)).wait_recv() if k != SECTS.index((0, 1)) else None
        slice_forward(k).wait_recv()
    wide = dot(h_all[...], o_all[...].reshape(1024, 512), NN)
    shift = lax.rem(48 * s, 128)
    res[1] = pltpu.roll(wide, lax.rem(512 - shift, 512), 1)[:, 0:F].astype(bf16)
    out2 = pltpu.make_async_copy(res.at[1], out.at[1], sem.at[LOAD + 13])
    out2.start()
    for k in reversed(range(7)):
        for part in (1, 2):
            sect_copy(part, k).wait_recv()
    res[0] = dot(g_t[pl.ds(pl.multiple_of(shift, 16), F), :], p_all[...], NT).astype(bf16)
    out1 = pltpu.make_async_copy(res.at[0], out.at[0], sem.at[LOAD + 12])
    out1.start()
    flush()
    out1.wait()
    out2.wait()


def shards(latent_noise, score_noise, gen_time, score_time, w_mod, w_up, b_up, w_down, b_down):
    anywhere = pl.BlockSpec(memory_space=pl.ANY)
    scalars = pl.BlockSpec(memory_space=pltpu.SMEM)
    vm = pltpu.VMEM
    scratch = [
        vm((TOK, DP), bf16), vm((TOK, DP), bf16), vm((3, MODC, 256), bf16),
        vm((3, F, D), bf16), vm((3, F, D), bf16), vm((3, F), f32), vm((3, DP), f32),
        vm((1, 256), f32), vm((32, 1, 256), f32),
        vm((8, 256), f32), vm((8, 256), f32), vm((8, 256), f32), vm((16, 8, 256), f32),
        vm((8, 7424), f32), vm((8, DP), f32),
        vm((TOK, D), f32), vm((TOK, DP), bf16), vm((3, TOK, D), bf16), vm((3, TOK, F), bf16), vm((TOK, 384), f32),
        vm((F, TOK), f32),
        vm((2, TOK, DP), bf16), vm((2, 2, TOK, W), bf16), vm((2, 2, TOK, W), bf16),
        vm((2, 16, 16, W), bf16),
        vm((TOK, DP), bf16), vm((TOK, DP), bf16),
        vm((8, TOK, 512), bf16), vm((8, 8, 512), f32), vm((512, 1024), bf16),
        vm((F, 1024), bf16), vm((F, 1024), bf16), vm((8, TOK, 512), bf16),
        vm((F, TOK), bf16), vm((F, TOK), bf16), vm((2, F, F), bf16),
        pltpu.SemaphoreType.DMA((SEMS.count,)),
    ]
    grads_shape = jax.ShapeDtypeStruct((2, F, F), bf16)
    grads = pl.pallas_call(
        kernel,
        out_shape=grads_shape,
        in_specs=[anywhere, anywhere, scalars, scalars] + [anywhere] * 5,
        out_specs=anywhere,
        scratch_shapes=scratch,
        cost_estimate=pl.CostEstimate(flops=1_700_000_000, bytes_accessed=11_000_000, transcendentals=300_000),
        compiler_params=pltpu.CompilerParams(
            collective_id=0, has_side_effects=True, vmem_limit_bytes=56 * 2**20
        ),
    )(
        latent_noise.reshape(TOK, D), score_noise.reshape(TOK, D), gen_time, score_time,
        w_mod.transpose(0, 2, 1), w_up.transpose(0, 2, 1), b_up, w_down, b_down,
    )
    return grads[0].astype(f32), grads[1].astype(f32)


def solution(mesh):
    placed = (
        P(None, "section", None),
        P(None, "section", None),
        P(),
        P(),
        P(None, None, "tensor"),
        P(None, None, "tensor"),
        P(None, "tensor"),
        P(None, "tensor", None),
        P(),
    )
    return jax.shard_map(
        shards,
        mesh=mesh,
        in_specs=placed,
        out_specs=(P("section", "tensor"), P("tensor", "section")),
        check_vma=False,
    )
```

```python
import functools
import math

import jax
import jax.numpy as jnp
from jax import lax
from jax.experimental import pallas as pl
from jax.experimental.pallas import tpu as pltpu
from jax.sharding import PartitionSpec as P

TRAIN_STEPS = 1000
MESH = pl.DeviceIdType.MESH
f32 = jnp.float32
bf16 = jnp.bfloat16

NT = (((1,), (1,)), ((), ()))
NN = (((1,), (0,)), ((), ()))

tanh_scale = math.sqrt(2.0 / math.pi)
cubic_term = 0.044715

TOK = 128
D = 2432
DP = 2560
F = 304
MODC = 228
W = DP // 4

FAR = (4, 3, 5, 2, 6, 1, 7, 0)
CORES = [(dz, dy, dc) for dz in FAR for dy in (1, 0) for dc in (0, 1) if (dz, dy, dc) != (0, 0, 0)]
CHIPS = [(dz, dy) for dz in FAR for dy in (1, 0) if (dz, dy) != (0, 0)]
NEAR = (0, 3, 1, 2)
SECTS = [(2, 1), (1, 1), (3, 1), (2, 0), (0, 1), (1, 0), (3, 0)]


def mul(value, factor):
    return pl.multiple_of(value * factor, factor)


def dot(a, b, dims):
    return lax.dot_general(a, b, dims, preferred_element_type=f32)


def gelu(v):
    return 0.5 * v * (1.0 + jnp.tanh(tanh_scale * (v + cubic_term * v * v * v)))


def slope(v):
    bent = jnp.tanh(tanh_scale * (v + cubic_term * v * v * v))
    return 0.5 * (1.0 + bent) + 0.5 * v * (1.0 - bent * bent) * tanh_scale * (
        1.0 + 3.0 * cubic_term * v * v
    )


class Sems:
    def __init__(self):
        self.count = 0

    def take(self, n):
        first = self.count
        self.count += n
        return first


SEMS = Sems()
LOAD = SEMS.take(16)
MX_S, MX_R = SEMS.take(1), SEMS.take(1)
MA_S, MA_R = SEMS.take(1), SEMS.take(15)
CX_S, CX_R = SEMS.take(8), SEMS.take(8)
RS_S, RS_R = SEMS.take(2), SEMS.take(32)
AG_S, AG_R = SEMS.take(2), SEMS.take(32)
FW_S, FW_R = SEMS.take(2), SEMS.take(32)
SX_S, SX_R = SEMS.take(9), SEMS.take(21)
M0_S, M0_R = SEMS.take(1), SEMS.take(31)
XW_S, XW_R = SEMS.take(1), SEMS.take(7)
XF_S, XF_R = SEMS.take(1), SEMS.take(7)
SC_S, SC_R = SEMS.take(1), SEMS.take(7)
OX_S, OX_R = SEMS.take(7), SEMS.take(56)
OY_S, OY_R = SEMS.take(7), SEMS.take(56)
OF_S, OF_R = SEMS.take(1), SEMS.take(14)


SPLIT = 160


def kernel(*refs):
    sends = []
    steps(sends, *refs)
    for wait in sends:
        wait()


def steps(
    sends,
    lat, noi, gt, st, wmod, wup, bup, wdn, bdn, out,
    latv, noiv, wmodv, wupv, wdnv, bupv, bdnv,
    m0row, m0all, mblk, mpart, mcomb, mall, modv, modx,
    xn, xw, xm, hid, prev, slope_t,
    psend, precv, csum, rsrecv, nbuf, gbuf,
    x_all, sc_all, g_t, h_all, p_all, o_all, pg, hid_t,
    sem,
):
    s = lax.axis_index("section")
    t = lax.axis_index("tensor")
    x, yh = s // 2, s % 2
    z, yl, c = t // 4, (t // 2) % 2, t % 2
    q = yl * 2 + c

    def flush():
        for wait in sends:
            wait()
        sends.clear()

    def chip_at(dz, dy):
        return lax.rem(z + dz, 8), lax.rem(yl + dy, 2)

    def chip_dev(dz, dy):
        z2, y2 = chip_at(dz, dy)
        return (s, z2 * 4 + y2 * 2 + c)

    def core_dev(dz, dy, dc):
        z2, y2 = chip_at(dz, dy)
        return (s, z2 * 4 + y2 * 2 + lax.rem(c + dc, 2))

    def sect_at(dx, dy):
        return lax.rem(x + dx, 4) * 2 + lax.rem(yh + dy, 2)

    partner = (s, z * 4 + yl * 2 + (1 - c))

    def remote(src, dst, ssem, rsem, dev):
        return pltpu.make_async_remote_copy(
            src_ref=src, dst_ref=dst, send_sem=sem.at[ssem], recv_sem=sem.at[rsem],
            device_id=dev, device_id_type=MESH,
        )

    def sent(ref, k):
        sends.append(lambda: pltpu.make_async_copy(ref, ref, sem.at[k]).wait())

    barrier = pltpu.get_barrier_semaphore()
    for dz, dy, dc in CORES:
        pl.semaphore_signal(barrier, inc=1, device_id=core_dev(dz, dy, dc), device_id_type=MESH)
    for dx, dy in SECTS:
        pl.semaphore_signal(barrier, inc=1, device_id=(sect_at(dx, dy), t), device_id_type=MESH)

    pair = z // 2

    def owner(b, y2, h):
        return 2 * b + lax.rem(y2 + h, 2)

    def block_rows(h, b):
        return pl.ds(mul(4 * h + lax.rem(b, 2) * 2 + b // 2, 16), 16)

    def rows_of(z2, y2):
        return block_rows(lax.rem(z2 + y2, 2), z2 // 2)

    def load(k, src, dst):
        copy = pltpu.make_async_copy(src, dst, sem.at[LOAD + k])
        copy.start()
        return copy.wait

    ld_wmod = load(0, wmod, wmodv)
    ld_lat = load(1, lat, latv.at[:, 0:D])
    ld_up = [load(2, wup.at[0], wupv.at[0])]
    ld_bup = load(3, bup, bupv)
    ld_dn = [load(4, wdn.at[0], wdnv.at[0])]
    ld_bdn = load(5, bdn, bdnv.at[:, 0:D])
    ld_noi = load(6, noi, noiv.at[:, 0:D])
    for n in (1, 2):
        ld_up.append(load(5 + 2 * n, wup.at[n], wupv.at[n]))
        ld_dn.append(load(6 + 2 * n, wdn.at[n], wdnv.at[n]))

    lane = lax.broadcasted_iota(jnp.int32, (8, 128), 1).astype(f32)
    freq = jnp.exp(lane * (-math.log(10000.0) / 128))

    def embed(stamp):
        angle = stamp.astype(f32) * freq
        return jnp.concatenate([jnp.cos(angle), jnp.sin(angle)], axis=1).astype(bf16)

    emb_gen = embed(gt[s])
    emb_score = embed(st[s])
    sigma = st[s].astype(f32) / TRAIN_STEPS
    ld_wmod()
    row = lax.broadcasted_iota(jnp.int32, (8, MODC), 0)
    m0 = dot(emb_gen, wmodv[0], NT)
    m1 = dot(emb_score, wmodv[1], NT)
    m2 = dot(emb_score, wmodv[2], NT)
    m0row[...] = jnp.zeros_like(m0row)
    m0row[:, 0:MODC] = m0[0:1]
    mblk[...] = jnp.zeros_like(mblk)
    mblk[:, 0:MODC] = jnp.where(row % 4 == 1, m1, jnp.where(row % 4 == 2, m2, 0.0))
    modv[...] = jnp.zeros_like(modv)
    modx[...] = jnp.zeros_like(modx)
    latv[:, D:DP] = jnp.zeros((TOK, DP - D), bf16)
    noiv[:, D:DP] = jnp.zeros((TOK, DP - D), bf16)
    bdnv[:, D:DP] = jnp.zeros((3, DP - D), f32)
    for a in range(2):
        psend[a, :, D:DP] = jnp.zeros((TOK, DP - D), bf16)
    ld_lat()

    def norm_rows(values):
        mean = jnp.mean(values, axis=1, keepdims=True)
        centred = values - mean
        var = jnp.mean(centred * centred, axis=1, keepdims=True)
        return centred * lax.rsqrt(var + 1e-06)

    def norm_body(i, _):
        rows = pl.ds(mul(i, 16), 16)
        normed = norm_rows(latv[rows, 0:D].astype(f32))
        xn[rows, :] = normed
        xw[rows, 0:D] = normed.astype(bf16)
        return 0

    lax.fori_loop(0, 8, norm_body, 0)
    xw[:, D:DP] = jnp.zeros((TOK, DP - D), bf16)
    pl.semaphore_wait(barrier, 38)

    me = z * 4 + yl * 2 + c
    m0 = []
    for k, (dz, dy, dc) in enumerate(CORES):
        copy = remote(m0row, m0all.at[me], M0_S, M0_R + k, core_dev(dz, dy, dc))
        copy.start()
        m0.append(copy)
    sent(m0all.at[0:31], M0_S)
    mx = remote(mblk, mpart, MX_S, MX_R, partner)
    mx.start()
    sends.append(mx.wait_send)
    m0all[me] = m0row[...]

    def first_lane(section, half):
        return mul((19 * section) // 8 + 2 * half, 128)

    def window_copy(k):
        dev = (sect_at(*SECTS[k]), t)
        return remote(
            xw.at[:, pl.ds(first_lane(dev[0], c), 256)], x_all.at[s, :, pl.ds(mul(c, 256), 256)],
            XW_S, XW_R + k, dev,
        )

    def from_sect(k):
        dx, dy = SECTS[k]
        return sect_at((4 - dx) % 4, dy)

    def window_forward(k):
        part = x_all.at[from_sect(k), :, pl.ds(mul(c, 256), 256)]
        return remote(part, part, XF_S, XF_R + k, partner)

    def scale_copy(k):
        dev = (sect_at(*SECTS[k]), t)
        return remote(modx.at[:, pl.ds(first_lane(dev[0], 0), 512)], sc_all.at[s], SC_S, SC_R + k, dev)

    mx.wait_recv()
    row8 = lax.broadcasted_iota(jnp.int32, (8, 256), 0)
    mcomb[...] = jnp.where((row8 < 4) == (c == 0), mblk[...], mpart[...])
    chip = z * 2 + yl
    ma = []
    for k, (dz, dy) in enumerate(CHIPS):
        copy = remote(mcomb, mall.at[chip], MA_S, MA_R + k, chip_dev(dz, dy))
        copy.start()
        ma.append(copy)
    sent(mall.at[0:15], MA_S)
    mall[chip] = mcomb[...]
    for k in range(7):
        window_copy(k).start()
    sent(x_all.at[0:7, :, 0:256], XW_S)
    x_all[s] = xw[:, pl.ds(first_lane(s, 0), 512)]
    for copy in m0:
        copy.wait_recv()
    for k in range(32):
        modv[0:1, MODC * k : MODC * (k + 1)] = m0all[k, :, 0:MODC]

    def gen_body(i, _):
        rows = pl.ds(mul(i, 16), 16)
        xm[0, rows, :] = (xn[rows, :] * (1.0 + modv[0:1, D : 2 * D]) + modv[0:1, 0:D]).astype(bf16)
        return 0

    lax.fori_loop(0, 8, gen_body, 0)
    modx[0:1, 0:D] = modv[0:1, D : 2 * D]
    modx[1:2, 0:D] = modv[0:1, 0:D]
    for k in range(7):
        scale_copy(k).start()
    sent(sc_all.at[0:7], SC_S)
    sc_all[s] = modx[:, pl.ds(first_lane(s, 0), 512)]
    ld_up[0]()
    ld_bup()
    pre = dot(xm[0], wupv[0], NT) + bupv[0:1, :]
    prev[:, 0:F] = pre
    hid[0] = gelu(pre).astype(bf16)
    ld_dn[0]()

    def quarter(y2, core):
        return pl.ds(mul((y2 * 2 + core) * (W // 128), 128), W)

    def core_copy(a, h, i):
        rows = pl.ds(64 * h, 64)
        k = (a * 2 + h) * 2 + i
        return remote(
            psend.at[a, rows, quarter(i, 1 - c)], precv.at[a, i, rows, :], CX_S + k, CX_R + k, partner
        )

    def core_send(a, h):
        for i in range(2):
            core_copy(a, h, i).start()
            sends.append(core_copy(a, h, i).wait_send)

    def start_scatter(a, h):
        rows = pl.ds(64 * h, 64)
        for i in range(2):
            core_copy(a, h, i).wait_recv()
        for i in range(2):
            csum[a, i, rows, :] = (
                psend[a, rows, quarter(i, c)].astype(f32) + precv[a, i, rows, :].astype(f32)
            ).astype(bf16)
        for m in (2, 1, 3, 0):
            for dy in (1, 0):
                y2 = lax.rem(yl + dy, 2)
                z2 = owner(lax.rem(pair + m, 4), y2, h)
                dz = lax.rem(z2 + 8 - z, 8)
                copy = remote(
                    csum.at[a, y2, rows_of(z2, y2), :], rsrecv.at[a, dz * 2 + dy],
                    RS_S + a, RS_R + a * 16 + dz * 2 + dy, chip_dev(dz, dy),
                )
                if (m, dy) == (0, 0):
                    pl.when(dz != 0)(copy.start)
                else:
                    copy.start()

    def piece(out, z2, y2):
        return out.at[rows_of(z2, y2), quarter(y2, c)]

    def forward(a, out, dz, dy):
        z2, y2 = chip_at(8 - dz, dy)
        part = piece(out, z2, y2)
        return remote(part, part, FW_S + a, FW_R + a * 16 + dz * 2 + dy, partner)

    def gather(a, out, dz, dy):
        own = piece(out, z, yl)
        return remote(own, own, AG_S + a, AG_R + a * 16 + dz * 2 + dy, chip_dev(dz, dy))

    def reduce(a, finish, out):
        rows = rows_of(z, yl)
        total = csum[a, yl, rows, :].astype(f32)
        for dz, dy in reversed(CHIPS):
            slot = rsrecv.at[a, dz * 2 + dy]
            remote(slot, slot, RS_S + a, RS_R + a * 16 + dz * 2 + dy, partner).wait_recv()
            total = total + slot[...].astype(f32)
        sent(rsrecv.at[a, 0:15], RS_S + a)
        piece(out, z, yl)[...] = finish(total, rows, mul(q * (W // 128), 128), W)
        for dz, dy in CHIPS:
            gather(a, out, dz, dy).start()
        forward(a, out, 0, 0).start()
        sent(rsrecv.at[a, 0:15], AG_S + a)

    def source(h, m, dy):
        z2 = owner(lax.rem(pair + 4 - m, 4), lax.rem(yl + dy, 2), h)
        return lax.rem(z + 8 - z2, 8)

    def pass_on(a, h, out, m):
        for dy in (0, 1):
            dz = source(h, m, dy)

            def step():
                gather(a, out, dz, dy).wait_recv()
                forward(a, out, dz, dy).start()

            if (m, dy) == (0, 0):
                pl.when(dz != 0)(step)
            else:
                step()

    def complete(a, h, out, m, on_rows):
        for dy in (0, 1):
            forward(a, out, source(h, m, dy), dy).wait_recv()
        on_rows(h, m, block_rows(h, lax.rem(pair + 4 - m, 4)))

    def gather_first(a, out, on_rows):
        for step, m in enumerate(NEAR):
            pass_on(a, 0, out, m)
            if step > 0:
                complete(a, 0, out, NEAR[step - 1], on_rows)
        complete(a, 0, out, NEAR[-1], on_rows)

    def complete_second(a, out, on_rows):
        for m in NEAR:
            complete(a, 1, out, m, lambda h, m, rows: None)
        for m in NEAR:
            on_rows(1, m, block_rows(1, lax.rem(pair + 4 - m, 4)))

    def produce_gen(h):
        rows = slice(64 * h, 64 * h + 64)
        psend[0, rows, 0:D] = dot(hid[0, rows], wdnv[0], NN).astype(bf16)

    def finish_gen(total, rows, col, width):
        cols = pl.ds(col, width)
        gate = modv[0:1, pl.ds(pl.multiple_of(2 * D + col, 128), width)]
        generated = latv[rows, cols].astype(f32) + gate * (total + bdnv[0:1, cols])
        return (
            (1.0 - sigma) * generated + sigma * noiv[rows, cols].astype(f32)
        ).astype(bf16)

    def hidden_copy(k):
        cols = pl.ds(mul(s, 128), 128)
        return remote(hid_t, h_all.at[:, cols], SX_S + k, SX_R + k, (sect_at(*SECTS[k]), t))

    def relay_copy(k):
        dx, dy = SECTS[k]
        part = h_all.at[:, pl.ds(mul(sect_at(0, 1), 128), 128)]
        return remote(part, part, SX_S + k, SX_R + k, (sect_at(dx, 0), t))

    direct = [k for k in range(7) if SECTS[k][1] == 0] + [SECTS.index((0, 1))]
    relayed = [k for k in range(7) if k not in direct]

    def turn_hidden():
        prev[:, F:384] = jnp.zeros((TOK, 384 - F), f32)
        for b in range(3):
            height = min(128, F - 128 * b)
            block = prev[:, 128 * b : 128 * b + 128].T
            slope_t[128 * b : 128 * b + height, :] = slope(block)[0:height]
            hid_t[128 * b : 128 * b + height, :] = gelu(block)[0:height].astype(bf16)
        for k in direct:
            hidden_copy(k).start()
            sends.append(hidden_copy(k).wait_send)
        h_all[:, pl.ds(mul(s, 128), 128)] = hid_t[...]

    def other_modulation():
        ld_bdn()
        ld_noi()
        for copy in ma:
            copy.wait_recv()
        for k in range(32):
            modv[1:3, MODC * k : MODC * (k + 1)] = mall[k // 2, 4 * (k % 2) + 1 : 4 * (k % 2) + 3, 0:MODC]

    def pass_windows():
        for k in reversed(range(7)):
            window_copy(k).wait_recv()
            window_forward(k).start()
        sent(x_all.at[0:7, :, 0:256], XF_S)

    def relay_hidden():
        hidden_copy(SECTS.index((0, 1))).wait_recv()
        for k in relayed:
            relay_copy(k).start()
            sends.append(relay_copy(k).wait_send)

    def gather_inputs():
        flush()
        for k in range(7):
            window_forward(k).wait_recv()
            scale_copy(k).wait_recv()

        def body(i, _):
            values = x_all[i].astype(f32) * (1.0 + sc_all[i, 0:1, :]) + sc_all[i, 1:2, :]
            values = values.astype(bf16).astype(f32)
            low = lax.broadcasted_iota(jnp.int32, (128, 128), 1) < 64
            for b in range(4):
                block = values[:, 128 * b : 128 * b + 128].T
                turned = pltpu.roll(block, 64, 1)
                at = (slice(128 * b, 128 * b + 128), pl.ds(mul(i, 128), 128))
                for h, r, value in ((0, 0, block), (0, 1, turned), (1, 0, turned), (1, 1, block)):
                    g_t[h, r, at[0], at[1]] = jnp.where(low == (r == 0), value, 0.0).astype(bf16)
            return 0

        lax.fori_loop(0, 8, body, 0)

    def score_rows(h, m, rows):
        normed = norm_rows(nbuf[rows, 0:D].astype(f32))
        for n in (1, 2):
            xm[n, rows, :] = (normed * (1.0 + modv[n : n + 1, D : 2 * D]) + modv[n : n + 1, 0:D]).astype(bf16)

    produce_gen(0)
    core_send(0, 0)
    turn_hidden()
    start_scatter(0, 0)
    produce_gen(1)
    core_send(0, 1)
    other_modulation()
    start_scatter(0, 1)
    pass_windows()
    reduce(0, finish_gen, nbuf)
    relay_hidden()

    def score_hidden(h):
        rows = slice(64 * h, 64 * h + 64)
        for n in (1, 2):
            hid[n, rows] = gelu(dot(xm[n, rows], wupv[n], NT) + bupv[n : n + 1, :]).astype(bf16)

    def produce_gap(h):
        rows = slice(64 * h, 64 * h + 64)
        real = dot(hid[1, rows], wdnv[1], NN) * modv[1:2, 2 * D : 3 * D]
        fake = dot(hid[2, rows], wdnv[2], NN) * modv[2:3, 2 * D : 3 * D]
        psend[1, rows, 0:D] = (fake - real).astype(bf16)

    for wait in ld_up[1:] + ld_dn[1:]:
        wait()
    gather_first(0, nbuf, score_rows)
    score_hidden(0)
    for m in NEAR:
        pass_on(0, 1, nbuf, m)
    produce_gap(0)
    core_send(1, 0)
    complete_second(0, nbuf, score_rows)
    sent(precv.at[0], FW_S)
    start_scatter(1, 0)
    score_hidden(1)
    produce_gap(1)
    core_send(1, 1)
    start_scatter(1, 1)

    def finish_gap(total, rows, col, width):
        cols = pl.ds(col, width)
        gates = modv[0:3, pl.ds(pl.multiple_of(2 * D + col, 128), width)]
        bias = gates[2:3] * bdnv[2:3, cols] - gates[1:2] * bdnv[1:2, cols]
        return ((total + bias) / 32.0 * gates[0:1]).astype(bf16)

    def slice_copy(h, m, k, last):
        dev = (sect_at(*SECTS[k]), t)
        rows = block_rows(h, lax.rem(pair + 4 - m, 4))
        lo, hi, base, recv = (384, 512, OY_S, OY_R) if last else (0, 384, OX_S, OX_R)
        return remote(
            gbuf.at[rows, pl.ds(pl.multiple_of(first_lane(dev[0], 0) + lo, 128), hi - lo)],
            o_all.at[s, rows, lo:hi], base + k, recv + 8 * k + 4 * h + m, dev,
        )

    def is_wide(section):
        return (section == 2) | (section == 5)

    def grad_rows(h, m, rows):
        o_all[s, rows, :] = gbuf[rows, pl.ds(first_lane(s, 0), 512)]

        @pl.when(c == m % 2)
        def _():
            for k in range(7):
                slice_copy(h, m, k, False).start()
                pl.when(is_wide(sect_at(*SECTS[k])))(lambda: slice_copy(h, m, k, True).start())

    def slice_forward(h, k):
        rows = pl.ds(mul(2 * h + lax.rem(pair + c, 2), 32), 32)
        part = o_all.at[from_sect(k), rows, :]
        return remote(part, part, OF_S, OF_R + 7 * h + k, partner)

    def pass_slices(h):
        for k in reversed(range(7)):
            for u in (0, 1):
                slice_copy(h, c + 2 * u, k, False).wait_recv()
                pl.when(is_wide(s))(lambda: slice_copy(h, c + 2 * u, k, True).wait_recv())
            slice_forward(h, k).start()

    def grad_copy(h, k):
        dev = (sect_at(*SECTS[k]), t)
        return remote(
            pg.at[h], p_all.at[h, :, pl.ds(mul(s, 128), 128)], SX_S + 7 + h, SX_R + 7 * (1 + h) + k, dev
        )

    def hidden_grad(h):
        rows = slice(64 * h, 64 * h + 64)
        value = dot(wdnv[0], gbuf[rows, 0:D], NT) * slope_t[:, rows]
        rest = jnp.concatenate([value[SPLIT:], jnp.zeros((2 * SPLIT - F, 64), f32)], axis=0)
        pg[h] = jnp.concatenate([value[0:SPLIT], rest], axis=1).astype(bf16)
        for k in range(7):
            grad_copy(h, k).start()
        p_all[h, :, pl.ds(mul(s, 128), 128)] = pg[h]

    gather_inputs()
    reduce(1, finish_gap, gbuf)
    gather_first(1, gbuf, grad_rows)
    for m in NEAR:
        pass_on(1, 1, gbuf, m)
    hidden_grad(0)
    complete_second(1, gbuf, grad_rows)
    hidden_grad(1)
    sent(precv.at[1], FW_S + 1)
    for k in range(7):
        sent(o_all.at[0, 0:64, 0:384], OX_S + k)

    pass_slices(0)
    flush()
    sent(p_all.at[0, :, 0:896], SX_S + 7)
    for k in reversed(range(7)):
        if k != SECTS.index((0, 1)):
            (relay_copy(k) if k in relayed else hidden_copy(k)).wait_recv()
    pass_slices(1)
    for k in range(7):

        @pl.when(is_wide(sect_at(*SECTS[k])))
        def _():
            last = o_all.at[0, 0:64, 384:512]
            pltpu.make_async_copy(last, last, sem.at[OY_S + k]).wait()

    flush()
    sent(o_all.at[0:7, 0:64, :], OF_S)
    shift = pl.multiple_of(lax.rem(48 * s, 128), 16)
    rows = pl.ds(shift, F)

    def first_grad(h):
        for k in reversed(range(7)):
            grad_copy(h, k).wait_recv()
        return [dot(g_t[h, r, rows, :], p_all[h], NT) for r in range(2)]

    def second_grad():
        for h in range(2):
            for k in reversed(range(7)):
                slice_forward(h, k).wait_recv()
        wide = dot(h_all[...], o_all[...].reshape(1024, 512), NN)
        out[1] = pltpu.roll(wide, lax.rem(512 - shift, 512), 1)[:, 0:F]

    early = first_grad(0)
    second_grad()
    sent(p_all.at[1, :, 0:896], SX_S + 8)
    late = first_grad(1)
    out[0] = jnp.concatenate([early[0] + late[0], (early[1] + late[1])[:, 0 : F - SPLIT]], axis=1)
    flush()


def shards(latent_noise, score_noise, gen_time, score_time, w_mod, w_up, b_up, w_down, b_down):
    anywhere = pl.BlockSpec(memory_space=pl.ANY)
    scalars = pl.BlockSpec(memory_space=pltpu.SMEM)
    vm = pltpu.VMEM
    scratch = [
        vm((TOK, DP), bf16), vm((TOK, DP), bf16), vm((3, MODC, 256), bf16),
        vm((3, F, D), bf16), vm((3, F, D), bf16), vm((3, F), f32), vm((3, DP), f32),
        vm((1, 256), f32), vm((32, 1, 256), f32),
        vm((8, 256), f32), vm((8, 256), f32), vm((8, 256), f32), vm((16, 8, 256), f32),
        vm((8, 7424), f32), vm((8, DP), f32),
        vm((TOK, D), f32), vm((TOK, DP), bf16), vm((3, TOK, D), bf16), vm((3, TOK, F), bf16), vm((TOK, 384), f32),
        vm((F, TOK), f32),
        vm((2, TOK, DP), bf16), vm((2, 2, TOK, W), bf16), vm((2, 2, TOK, W), bf16),
        vm((2, 16, 16, W), bf16),
        vm((TOK, DP), bf16), vm((TOK, DP), bf16),
        vm((8, TOK, 512), bf16), vm((8, 8, 512), f32), vm((2, 2, 512, 1024), bf16),
        vm((F, 1024), bf16), vm((2, SPLIT, 1024), bf16), vm((8, TOK, 512), bf16),
        vm((2, SPLIT, TOK), bf16), vm((F, TOK), bf16),
        pltpu.SemaphoreType.DMA((SEMS.count,)),
    ]
    grads = pl.pallas_call(
        kernel,
        out_shape=vm((2, F, F), f32),
        in_specs=[anywhere, anywhere, scalars, scalars] + [anywhere] * 5,
        out_specs=pl.BlockSpec(memory_space=pltpu.VMEM),
        scratch_shapes=scratch,
        cost_estimate=pl.CostEstimate(flops=1_700_000_000, bytes_accessed=11_000_000, transcendentals=300_000),
        compiler_params=pltpu.CompilerParams(
            collective_id=0, has_side_effects=True, vmem_limit_bytes=56 * 2**20
        ),
    )(
        latent_noise.reshape(TOK, D), score_noise.reshape(TOK, D), gen_time, score_time,
        w_mod.transpose(0, 2, 1), w_up.transpose(0, 2, 1), b_up, w_down, b_down,
    )
    return grads[0], grads[1]


def solution(mesh):
    placed = (
        P(None, "section", None),
        P(None, "section", None),
        P(),
        P(),
        P(None, None, "tensor"),
        P(None, None, "tensor"),
        P(None, "tensor"),
        P(None, "tensor", None),
        P(),
    )
    return jax.shard_map(
        shards,
        mesh=mesh,
        in_specs=placed,
        out_specs=(P("section", "tensor"), P("tensor", "section")),
        check_vma=False,
    )
```

```python
import functools
import math

import jax
import jax.numpy as jnp
from jax import lax
from jax.experimental import pallas as pl
from jax.experimental.pallas import tpu as pltpu
from jax.sharding import PartitionSpec as P

TRAIN_STEPS = 1000
MESH = pl.DeviceIdType.MESH
f32 = jnp.float32
bf16 = jnp.bfloat16

NT = (((1,), (1,)), ((), ()))
NN = (((1,), (0,)), ((), ()))

tanh_scale = math.sqrt(2.0 / math.pi)
cubic_term = 0.044715

TOK = 128
D = 2432
DP = 2560
F = 304
MODC = 228
W = DP // 4

FAR = (4, 3, 5, 2, 6, 1, 7, 0)
CORES = [(dz, dy, dc) for dz in FAR for dy in (1, 0) for dc in (0, 1) if (dz, dy, dc) != (0, 0, 0)]
CHIPS = [(dz, dy) for dz in FAR for dy in (1, 0) if (dz, dy) != (0, 0)]
NEAR = (0, 3, 1, 2)
SECTS = [(2, 1), (1, 1), (3, 1), (2, 0), (0, 1), (1, 0), (3, 0)]


def mul(value, factor):
    return pl.multiple_of(value * factor, factor)


def dot(a, b, dims):
    return lax.dot_general(a, b, dims, preferred_element_type=f32)


def gelu(v):
    return 0.5 * v * (1.0 + jnp.tanh(tanh_scale * (v + cubic_term * v * v * v)))


def slope(v):
    bent = jnp.tanh(tanh_scale * (v + cubic_term * v * v * v))
    return 0.5 * (1.0 + bent) + 0.5 * v * (1.0 - bent * bent) * tanh_scale * (
        1.0 + 3.0 * cubic_term * v * v
    )


class Sems:
    def __init__(self):
        self.count = 0

    def take(self, n):
        first = self.count
        self.count += n
        return first


SEMS = Sems()
LOAD = SEMS.take(16)
MX_S, MX_R = SEMS.take(1), SEMS.take(1)
MA_S, MA_R = SEMS.take(1), SEMS.take(15)
CX_S, CX_R = SEMS.take(8), SEMS.take(8)
RS_S, RS_R = SEMS.take(2), SEMS.take(32)
AG_S, AG_R = SEMS.take(2), SEMS.take(32)
FW_S, FW_R = SEMS.take(2), SEMS.take(32)
SX_S, SX_R = SEMS.take(9), SEMS.take(21)
M0_S, M0_R = SEMS.take(1), SEMS.take(31)
XW_S, XW_R = SEMS.take(7), SEMS.take(7)
XV_S, XV_R = SEMS.take(7), SEMS.take(7)
XF_S, XF_R = SEMS.take(1), SEMS.take(7)
SC_S, SC_R = SEMS.take(1), SEMS.take(7)
OX_S, OX_R = SEMS.take(7), SEMS.take(56)
OY_S, OY_R = SEMS.take(7), SEMS.take(56)
OF_S, OF_R = SEMS.take(1), SEMS.take(14)


SPLIT = 160


def kernel(*refs):
    sends = []
    steps(sends, *refs)
    for wait in sends:
        wait()


def steps(
    sends,
    lat, noi, gt, st, wmod, wup, bup, wdn, bdn, out,
    latv, noiv, wmodv, wupv, wdnv, bupv, bdnv,
    m0row, m0all, mblk, mpart, mcomb, mall, modv, modx,
    xn, xw, xm, hid, prev, slope_t,
    psend, precv, csum, rsrecv, nbuf, gbuf,
    x_all, sc_all, g_t, h_all, h_t, p_all, o_all, pg, hid_t,
    sem,
):
    s = lax.axis_index("section")
    t = lax.axis_index("tensor")
    x, yh = s // 2, s % 2
    z, yl, c = t // 4, (t // 2) % 2, t % 2
    q = yl * 2 + c

    def flush():
        for wait in sends:
            wait()
        sends.clear()

    def chip_at(dz, dy):
        return lax.rem(z + dz, 8), lax.rem(yl + dy, 2)

    def chip_dev(dz, dy):
        z2, y2 = chip_at(dz, dy)
        return (s, z2 * 4 + y2 * 2 + c)

    def core_dev(dz, dy, dc):
        z2, y2 = chip_at(dz, dy)
        return (s, z2 * 4 + y2 * 2 + lax.rem(c + dc, 2))

    def sect_at(dx, dy):
        return lax.rem(x + dx, 4) * 2 + lax.rem(yh + dy, 2)

    partner = (s, z * 4 + yl * 2 + (1 - c))

    def remote(src, dst, ssem, rsem, dev):
        return pltpu.make_async_remote_copy(
            src_ref=src, dst_ref=dst, send_sem=sem.at[ssem], recv_sem=sem.at[rsem],
            device_id=dev, device_id_type=MESH,
        )

    def sent(ref, k):
        sends.append(lambda: pltpu.make_async_copy(ref, ref, sem.at[k]).wait())

    barrier = pltpu.get_barrier_semaphore()
    for dz, dy, dc in CORES:
        pl.semaphore_signal(barrier, inc=1, device_id=core_dev(dz, dy, dc), device_id_type=MESH)
    for dx, dy in SECTS:
        pl.semaphore_signal(barrier, inc=1, device_id=(sect_at(dx, dy), t), device_id_type=MESH)

    pair = z // 2

    def owner(b, y2, h):
        return 2 * b + lax.rem(y2 + h, 2)

    def block_rows(h, b):
        return pl.ds(mul(4 * h + lax.rem(b, 2) * 2 + b // 2, 16), 16)

    def rows_of(z2, y2):
        return block_rows(lax.rem(z2 + y2, 2), z2 // 2)

    def load(k, src, dst):
        copy = pltpu.make_async_copy(src, dst, sem.at[LOAD + k])
        copy.start()
        return copy.wait

    ld_wmod = load(0, wmod, wmodv)
    ld_lat = load(1, lat, latv.at[:, 0:D])
    ld_up = [load(2, wup.at[0], wupv.at[0])]
    ld_bup = load(3, bup, bupv)
    ld_dn = [load(4, wdn.at[0], wdnv.at[0, :, 0:D])]
    ld_bdn = load(5, bdn, bdnv.at[:, 0:D])
    ld_noi = load(6, noi, noiv.at[:, 0:D])
    for n in (1, 2):
        ld_up.append(load(5 + 2 * n, wup.at[n], wupv.at[n]))
        ld_dn.append(load(6 + 2 * n, wdn.at[n], wdnv.at[n, :, 0:D]))

    lane = lax.broadcasted_iota(jnp.int32, (8, 128), 1).astype(f32)
    freq = jnp.exp(lane * (-math.log(10000.0) / 128))

    def embed(stamp):
        angle = stamp.astype(f32) * freq
        return jnp.concatenate([jnp.cos(angle), jnp.sin(angle)], axis=1).astype(bf16)

    emb_gen = embed(gt[s])
    emb_score = embed(st[s])
    sigma = st[s].astype(f32) / TRAIN_STEPS
    ld_wmod()
    row = lax.broadcasted_iota(jnp.int32, (8, MODC), 0)
    m0 = dot(emb_gen, wmodv[0], NT)
    m1 = dot(emb_score, wmodv[1], NT)
    m2 = dot(emb_score, wmodv[2], NT)
    m0row[...] = jnp.zeros_like(m0row)
    m0row[:, 0:MODC] = m0[0:1]
    mblk[...] = jnp.zeros_like(mblk)
    mblk[:, 0:MODC] = jnp.where(row % 4 == 1, m1, jnp.where(row % 4 == 2, m2, 0.0))
    modv[...] = jnp.zeros_like(modv)
    modx[...] = jnp.zeros_like(modx)
    latv[:, D:DP] = jnp.zeros((TOK, DP - D), bf16)
    noiv[:, D:DP] = jnp.zeros((TOK, DP - D), bf16)
    bdnv[:, D:DP] = jnp.zeros((3, DP - D), f32)
    for n in range(3):
        wdnv[n, :, D:DP] = jnp.zeros((F, DP - D), bf16)
    ld_lat()

    def norm_rows(values):
        mean = jnp.mean(values, axis=1, keepdims=True)
        centred = values - mean
        var = jnp.mean(centred * centred, axis=1, keepdims=True)
        return centred * lax.rsqrt(var + 1e-06)

    def norm_body(i, _):
        rows = pl.ds(mul(i, 16), 16)
        normed = norm_rows(latv[rows, 0:D].astype(f32))
        xn[rows, :] = normed
        xw[rows, 0:D] = normed.astype(bf16)
        return 0

    lax.fori_loop(0, 8, norm_body, 0)
    xw[:, D:DP] = jnp.zeros((TOK, DP - D), bf16)
    pl.semaphore_wait(barrier, 38)

    me = z * 4 + yl * 2 + c
    m0 = []
    for k, (dz, dy, dc) in enumerate(CORES):
        copy = remote(m0row, m0all.at[me], M0_S, M0_R + k, core_dev(dz, dy, dc))
        copy.start()
        m0.append(copy)
    sent(m0all.at[0:31], M0_S)
    mx = remote(mblk, mpart, MX_S, MX_R, partner)
    mx.start()
    sends.append(mx.wait_send)
    m0all[me] = m0row[...]

    def first_lane(section):
        return mul((19 * section) // 8, 128)

    def is_wide(section):
        return (section == 2) | (section == 5)

    mine = pl.ds(mul(c, 64), 64)

    def window_copy(k, last):
        dev = (sect_at(*SECTS[k]), t)
        lo, hi, base, recv = (384, 512, XV_S, XV_R) if last else (0, 384, XW_S, XW_R)
        return remote(
            xw.at[mine, pl.ds(pl.multiple_of(first_lane(dev[0]) + lo, 128), hi - lo)],
            x_all.at[s, mine, lo:hi], base + k, recv + k, dev,
        )

    def from_sect(k):
        dx, dy = SECTS[k]
        return sect_at((4 - dx) % 4, dy)

    def window_forward(k):
        part = x_all.at[from_sect(k), mine, :]
        return remote(part, part, XF_S, XF_R + k, partner)

    def scale_copy(k):
        dev = (sect_at(*SECTS[k]), t)
        return remote(modx.at[:, pl.ds(first_lane(dev[0]), 512)], sc_all.at[s], SC_S, SC_R + k, dev)

    mx.wait_recv()
    row8 = lax.broadcasted_iota(jnp.int32, (8, 256), 0)
    mcomb[...] = jnp.where((row8 < 4) == (c == 0), mblk[...], mpart[...])
    chip = z * 2 + yl
    ma = []
    for k, (dz, dy) in enumerate(CHIPS):
        copy = remote(mcomb, mall.at[chip], MA_S, MA_R + k, chip_dev(dz, dy))
        copy.start()
        ma.append(copy)
    sent(mall.at[0:15], MA_S)
    mall[chip] = mcomb[...]
    for k in range(7):
        window_copy(k, False).start()
        pl.when(is_wide(sect_at(*SECTS[k])))(lambda: window_copy(k, True).start())
        sends.append(window_copy(k, False).wait_send)
    x_all[s] = xw[:, pl.ds(first_lane(s), 512)]
    for copy in m0:
        copy.wait_recv()
    for k in range(32):
        modv[0:1, MODC * k : MODC * (k + 1)] = m0all[k, :, 0:MODC]

    def gen_body(i, _):
        rows = pl.ds(mul(i, 16), 16)
        xm[0, rows, :] = (xn[rows, :] * (1.0 + modv[0:1, D : 2 * D]) + modv[0:1, 0:D]).astype(bf16)
        return 0

    lax.fori_loop(0, 8, gen_body, 0)
    modx[0:1, 0:D] = modv[0:1, D : 2 * D]
    modx[1:2, 0:D] = modv[0:1, 0:D]
    for k in range(7):
        scale_copy(k).start()
    sent(sc_all.at[0:7], SC_S)
    sc_all[s] = modx[:, pl.ds(first_lane(s), 512)]
    ld_up[0]()
    ld_bup()
    ld_dn[0]()

    def gen_hidden(h):
        rows = slice(64 * h, 64 * h + 64)
        pre = dot(xm[0, rows], wupv[0], NT) + bupv[0:1, :]
        prev[rows, 0:F] = pre
        hid[0, rows] = gelu(pre).astype(bf16)

    def quarter(y2, core):
        return pl.ds(mul((y2 * 2 + core) * (W // 128), 128), W)

    def core_copy(a, h, i):
        rows = pl.ds(64 * h, 64)
        k = (a * 2 + h) * 2 + i
        return remote(
            psend.at[a, rows, quarter(i, 1 - c)], precv.at[a, i, rows, :], CX_S + k, CX_R + k, partner
        )

    def produce(a, h, value):
        rows = slice(64 * h, 64 * h + 64)
        for core in (1 - c, c):
            for i in range(2):
                cols = quarter(i, core)
                psend[a, rows, cols] = value(rows, cols).astype(bf16)
                if core is not c:
                    core_copy(a, h, i).start()
                    sends.append(core_copy(a, h, i).wait_send)

    def start_scatter(a, h):
        rows = pl.ds(64 * h, 64)
        for i in range(2):
            core_copy(a, h, i).wait_recv()
        for i in range(2):
            csum[a, i, rows, :] = (
                psend[a, rows, quarter(i, c)].astype(f32) + precv[a, i, rows, :].astype(f32)
            ).astype(bf16)
        for m in (2, 1, 3, 0):
            for dy in (1, 0):
                y2 = lax.rem(yl + dy, 2)
                z2 = owner(lax.rem(pair + m, 4), y2, h)
                dz = lax.rem(z2 + 8 - z, 8)
                copy = remote(
                    csum.at[a, y2, rows_of(z2, y2), :], rsrecv.at[a, dz * 2 + dy],
                    RS_S + a, RS_R + a * 16 + dz * 2 + dy, chip_dev(dz, dy),
                )
                if (m, dy) == (0, 0):
                    pl.when(dz != 0)(copy.start)
                else:
                    copy.start()

    def piece(out, z2, y2):
        return out.at[rows_of(z2, y2), quarter(y2, c)]

    def forward(a, out, dz, dy):
        z2, y2 = chip_at(8 - dz, dy)
        part = piece(out, z2, y2)
        return remote(part, part, FW_S + a, FW_R + a * 16 + dz * 2 + dy, partner)

    def gather(a, out, dz, dy):
        own = piece(out, z, yl)
        return remote(own, own, AG_S + a, AG_R + a * 16 + dz * 2 + dy, chip_dev(dz, dy))

    def reduce(a, finish, out):
        rows = rows_of(z, yl)
        total = csum[a, yl, rows, :].astype(f32)
        for dz, dy in reversed(CHIPS):
            slot = rsrecv.at[a, dz * 2 + dy]
            remote(slot, slot, RS_S + a, RS_R + a * 16 + dz * 2 + dy, partner).wait_recv()
            total = total + slot[...].astype(f32)
        sent(rsrecv.at[a, 0:15], RS_S + a)
        piece(out, z, yl)[...] = finish(total, rows, mul(q * (W // 128), 128), W)
        for dz, dy in CHIPS:
            gather(a, out, dz, dy).start()
        forward(a, out, 0, 0).start()
        sent(rsrecv.at[a, 0:15], AG_S + a)

    def source(h, m, dy):
        z2 = owner(lax.rem(pair + 4 - m, 4), lax.rem(yl + dy, 2), h)
        return lax.rem(z + 8 - z2, 8)

    def pass_on(a, h, out, m):
        for dy in (0, 1):
            dz = source(h, m, dy)

            def step():
                gather(a, out, dz, dy).wait_recv()
                forward(a, out, dz, dy).start()

            if (m, dy) == (0, 0):
                pl.when(dz != 0)(step)
            else:
                step()

    def complete(a, h, out, m, on_rows):
        for dy in (0, 1):
            forward(a, out, source(h, m, dy), dy).wait_recv()
        on_rows(h, m, block_rows(h, lax.rem(pair + 4 - m, 4)))

    def gather_first(a, out, on_rows):
        for step, m in enumerate(NEAR):
            pass_on(a, 0, out, m)
            if step > 0:
                complete(a, 0, out, NEAR[step - 1], on_rows)
        complete(a, 0, out, NEAR[-1], on_rows)

    def complete_second(a, out, on_rows):
        for m in NEAR:
            complete(a, 1, out, m, lambda h, m, rows: None)
        for m in NEAR:
            on_rows(1, m, block_rows(1, lax.rem(pair + 4 - m, 4)))

    def gen_value(rows, cols):
        return dot(hid[0, rows], wdnv[0, :, cols], NN)

    def finish_gen(total, rows, col, width):
        cols = pl.ds(col, width)
        gate = modv[0:1, pl.ds(pl.multiple_of(2 * D + col, 128), width)]
        generated = latv[rows, cols].astype(f32) + gate * (total + bdnv[0:1, cols])
        return (
            (1.0 - sigma) * generated + sigma * noiv[rows, cols].astype(f32)
        ).astype(bf16)

    def hidden_copy(k):
        cols = pl.ds(mul(s, 128), 128)
        return remote(hid_t, h_all.at[:, cols], SX_S + k, SX_R + k, (sect_at(*SECTS[k]), t))

    def relay_copy(k):
        dx, dy = SECTS[k]
        part = h_all.at[:, pl.ds(mul(sect_at(0, 1), 128), 128)]
        return remote(part, part, SX_S + k, SX_R + k, (sect_at(dx, 0), t))

    direct = [k for k in range(7) if SECTS[k][1] == 0] + [SECTS.index((0, 1))]
    relayed = [k for k in range(7) if k not in direct]

    def turn_hidden():
        prev[:, F:384] = jnp.zeros((TOK, 384 - F), f32)
        for b in range(3):
            height = min(128, F - 128 * b)
            block = prev[:, 128 * b : 128 * b + 128].T
            slope_t[128 * b : 128 * b + height, :] = slope(block)[0:height]
            hid_t[128 * b : 128 * b + height, :] = gelu(block)[0:height].astype(bf16)
        for k in direct:
            hidden_copy(k).start()
            sends.append(hidden_copy(k).wait_send)
        h_all[:, pl.ds(mul(s, 128), 128)] = hid_t[...]

    def other_modulation():
        ld_bdn()
        ld_noi()
        for copy in ma:
            copy.wait_recv()
        for k in range(32):
            modv[1:3, MODC * k : MODC * (k + 1)] = mall[k // 2, 4 * (k % 2) + 1 : 4 * (k % 2) + 3, 0:MODC]

    def pass_windows():
        for k in reversed(range(7)):
            window_copy(k, False).wait_recv()
            pl.when(is_wide(s))(lambda: window_copy(k, True).wait_recv())
            window_forward(k).start()
        sent(x_all.at[0:7, 0:64, :], XF_S)

    def relay_hidden():
        hidden_copy(SECTS.index((0, 1))).wait_recv()
        for k in relayed:
            relay_copy(k).start()
            sends.append(relay_copy(k).wait_send)

    def gather_inputs():
        for k in range(7):
            window_forward(k).wait_recv()
            scale_copy(k).wait_recv()

        def body(i, _):
            values = x_all[i].astype(f32) * (1.0 + sc_all[i, 0:1, :]) + sc_all[i, 1:2, :]
            values = values.astype(bf16).astype(f32)
            low = lax.broadcasted_iota(jnp.int32, (128, 128), 1) < 64
            for b in range(4):
                block = values[:, 128 * b : 128 * b + 128].T
                turned = pltpu.roll(block, 64, 1)
                at = (slice(128 * b, 128 * b + 128), pl.ds(mul(i, 128), 128))
                for h, r, value in ((0, 0, block), (0, 1, turned), (1, 0, turned), (1, 1, block)):
                    g_t[h, r, at[0], at[1]] = jnp.where(low == (r == 0), value, 0.0).astype(bf16)
            return 0

        lax.fori_loop(0, 8, body, 0)
        for k in range(7):
            if k != SECTS.index((0, 1)):
                (relay_copy(k) if k in relayed else hidden_copy(k)).wait_recv()
        for i in range(4):
            low = lax.broadcasted_iota(jnp.int32, (F, 128), 1) < 64
            first = h_all[:, 256 * i : 256 * i + 128].astype(f32)
            second = h_all[:, 256 * i + 128 : 256 * i + 256].astype(f32)
            cols = slice(128 * i, 128 * i + 128)
            h_t[0, :, cols] = jnp.where(low, first, pltpu.roll(second, 64, 1)).astype(bf16)
            h_t[1, :, cols] = jnp.where(low, pltpu.roll(first, 64, 1), second).astype(bf16)

    def score_rows(h, m, rows):
        normed = norm_rows(nbuf[rows, 0:D].astype(f32))
        for n in (1, 2):
            xm[n, rows, :] = (normed * (1.0 + modv[n : n + 1, D : 2 * D]) + modv[n : n + 1, 0:D]).astype(bf16)

    gen_hidden(0)
    produce(0, 0, gen_value)
    gen_hidden(1)
    start_scatter(0, 0)
    produce(0, 1, gen_value)
    turn_hidden()
    other_modulation()
    start_scatter(0, 1)
    pass_windows()
    reduce(0, finish_gen, nbuf)
    relay_hidden()

    def score_hidden(h):
        rows = slice(64 * h, 64 * h + 64)
        for n in (1, 2):
            hid[n, rows] = gelu(dot(xm[n, rows], wupv[n], NT) + bupv[n : n + 1, :]).astype(bf16)

    def gap_value(rows, cols):
        gates = pl.ds(pl.multiple_of(2 * D + cols.start, 128), W)
        real = dot(hid[1, rows], wdnv[1, :, cols], NN) * modv[1:2, gates]
        fake = dot(hid[2, rows], wdnv[2, :, cols], NN) * modv[2:3, gates]
        return fake - real

    for wait in ld_up[1:] + ld_dn[1:]:
        wait()
    gather_first(0, nbuf, score_rows)
    score_hidden(0)
    for m in NEAR:
        pass_on(0, 1, nbuf, m)
    produce(1, 0, gap_value)
    complete_second(0, nbuf, score_rows)
    sent(precv.at[0], FW_S)
    start_scatter(1, 0)
    score_hidden(1)
    produce(1, 1, gap_value)
    start_scatter(1, 1)

    def finish_gap(total, rows, col, width):
        cols = pl.ds(col, width)
        gates = modv[0:3, pl.ds(pl.multiple_of(2 * D + col, 128), width)]
        bias = gates[2:3] * bdnv[2:3, cols] - gates[1:2] * bdnv[1:2, cols]
        return ((total + bias) / 32.0 * gates[0:1]).astype(bf16)

    def slice_copy(h, m, k, last):
        dev = (sect_at(*SECTS[k]), t)
        rows = block_rows(h, lax.rem(pair + 4 - m, 4))
        lo, hi, base, recv = (384, 512, OY_S, OY_R) if last else (0, 384, OX_S, OX_R)
        return remote(
            gbuf.at[rows, pl.ds(pl.multiple_of(first_lane(dev[0]) + lo, 128), hi - lo)],
            o_all.at[s, rows, lo:hi], base + k, recv + 8 * k + 4 * h + m, dev,
        )

    def grad_rows(h, m, rows):
        o_all[s, rows, :] = gbuf[rows, pl.ds(first_lane(s), 512)]

        @pl.when(c == m % 2)
        def _():
            for k in range(7):
                slice_copy(h, m, k, False).start()
                pl.when(is_wide(sect_at(*SECTS[k])))(lambda: slice_copy(h, m, k, True).start())

    def slice_forward(h, k):
        rows = pl.ds(mul(2 * h + lax.rem(pair + c, 2), 32), 32)
        part = o_all.at[from_sect(k), rows, :]
        return remote(part, part, OF_S, OF_R + 7 * h + k, partner)

    def pass_slices(h):
        for k in reversed(range(7)):
            for u in (0, 1):
                slice_copy(h, c + 2 * u, k, False).wait_recv()
                pl.when(is_wide(s))(lambda: slice_copy(h, c + 2 * u, k, True).wait_recv())
            slice_forward(h, k).start()

    def grad_copy(h, k):
        dev = (sect_at(*SECTS[k]), t)
        return remote(
            pg.at[h], p_all.at[h, :, pl.ds(mul(s, 128), 128)], SX_S + 7 + h, SX_R + 7 * (1 + h) + k, dev
        )

    def hidden_grad(h):
        rows = slice(64 * h, 64 * h + 64)
        value = dot(wdnv[0, :, 0:D], gbuf[rows, 0:D], NT) * slope_t[:, rows]
        rest = jnp.concatenate([value[SPLIT:], jnp.zeros((2 * SPLIT - F, 64), f32)], axis=0)
        pg[h] = jnp.concatenate([value[0:SPLIT], rest], axis=1).astype(bf16)
        for k in range(7):
            grad_copy(h, k).start()
        p_all[h, :, pl.ds(mul(s, 128), 128)] = pg[h]

    flush()
    reduce(1, finish_gap, gbuf)
    gather_inputs()
    gather_first(1, gbuf, grad_rows)
    for m in NEAR:
        pass_on(1, 1, gbuf, m)
    hidden_grad(0)
    complete_second(1, gbuf, grad_rows)
    hidden_grad(1)
    sent(precv.at[1], FW_S + 1)
    for k in range(7):
        sent(o_all.at[0, 0:64, 0:384], OX_S + k)

    shift = pl.multiple_of(lax.rem(48 * s, 128), 16)

    def second_grad(h):
        for k in reversed(range(7)):
            slice_forward(h, k).wait_recv()
        return dot(h_t[h], o_all[:, 64 * h : 64 * h + 64, :].reshape(512, 512), NN)

    def store_second(wide):
        out[1] = pltpu.roll(wide, lax.rem(512 - shift, 512), 1)[:, 0:F]

    pass_slices(0)
    flush()
    sent(p_all.at[0, :, 0:896], SX_S + 7)
    wide_first = second_grad(0)
    pass_slices(1)
    for k in range(7):

        @pl.when(is_wide(sect_at(*SECTS[k])))
        def _():
            window_copy(k, True).wait_send()
            last = o_all.at[0, 0:64, 384:512]
            pltpu.make_async_copy(last, last, sem.at[OY_S + k]).wait()

    flush()
    sent(o_all.at[0:7, 0:64, :], OF_S)
    rows = pl.ds(shift, F)

    def first_grad(h):
        for k in reversed(range(7)):
            grad_copy(h, k).wait_recv()
        return [dot(g_t[h, r, rows, :], p_all[h], NT) for r in range(2)]

    early = first_grad(0)
    store_second(wide_first + second_grad(1))
    sent(p_all.at[1, :, 0:896], SX_S + 8)
    late = first_grad(1)
    out[0] = jnp.concatenate([early[0] + late[0], (early[1] + late[1])[:, 0 : F - SPLIT]], axis=1)
    flush()


def shards(latent_noise, score_noise, gen_time, score_time, w_mod, w_up, b_up, w_down, b_down):
    anywhere = pl.BlockSpec(memory_space=pl.ANY)
    scalars = pl.BlockSpec(memory_space=pltpu.SMEM)
    vm = pltpu.VMEM
    scratch = [
        vm((TOK, DP), bf16), vm((TOK, DP), bf16), vm((3, MODC, 256), bf16),
        vm((3, F, D), bf16), vm((3, F, DP), bf16), vm((3, F), f32), vm((3, DP), f32),
        vm((1, 256), f32), vm((32, 1, 256), f32),
        vm((8, 256), f32), vm((8, 256), f32), vm((8, 256), f32), vm((16, 8, 256), f32),
        vm((8, 7424), f32), vm((8, DP), f32),
        vm((TOK, D), f32), vm((TOK, DP), bf16), vm((3, TOK, D), bf16), vm((3, TOK, F), bf16), vm((TOK, 384), f32),
        vm((F, TOK), f32),
        vm((2, TOK, DP), bf16), vm((2, 2, TOK, W), bf16), vm((2, 2, TOK, W), bf16),
        vm((2, 16, 16, W), bf16),
        vm((TOK, DP), bf16), vm((TOK, DP), bf16),
        vm((8, TOK, 512), bf16), vm((8, 8, 512), f32), vm((2, 2, 512, 1024), bf16),
        vm((F, 1024), bf16), vm((2, F, 512), bf16), vm((2, SPLIT, 1024), bf16), vm((8, TOK, 512), bf16),
        vm((2, SPLIT, TOK), bf16), vm((F, TOK), bf16),
        pltpu.SemaphoreType.DMA((SEMS.count,)),
    ]
    grads = pl.pallas_call(
        kernel,
        out_shape=vm((2, F, F), f32),
        in_specs=[anywhere, anywhere, scalars, scalars] + [anywhere] * 5,
        out_specs=pl.BlockSpec(memory_space=pltpu.VMEM),
        scratch_shapes=scratch,
        cost_estimate=pl.CostEstimate(flops=1_700_000_000, bytes_accessed=11_000_000, transcendentals=300_000),
        compiler_params=pltpu.CompilerParams(
            collective_id=0, has_side_effects=True, vmem_limit_bytes=56 * 2**20
        ),
    )(
        latent_noise.reshape(TOK, D), score_noise.reshape(TOK, D), gen_time, score_time,
        w_mod.transpose(0, 2, 1), w_up.transpose(0, 2, 1), b_up, w_down, b_down,
    )
    return grads[0], grads[1]


def solution(mesh):
    placed = (
        P(None, "section", None),
        P(None, "section", None),
        P(),
        P(),
        P(None, None, "tensor"),
        P(None, None, "tensor"),
        P(None, "tensor"),
        P(None, "tensor", None),
        P(),
    )
    return jax.shard_map(
        shards,
        mesh=mesh,
        in_specs=placed,
        out_specs=(P("section", "tensor"), P("tensor", "section")),
        check_vma=False,
    )
```

```python
import functools
import math

import jax
import jax.numpy as jnp
from jax import lax
from jax.experimental import pallas as pl
from jax.experimental.pallas import tpu as pltpu
from jax.sharding import PartitionSpec as P

TRAIN_STEPS = 1000
MESH = pl.DeviceIdType.MESH
f32 = jnp.float32
bf16 = jnp.bfloat16

NT = (((1,), (1,)), ((), ()))
NN = (((1,), (0,)), ((), ()))

tanh_scale = math.sqrt(2.0 / math.pi)
cubic_term = 0.044715

TOK = 128
D = 2432
DP = 2560
F = 304
MODC = 228
W = DP // 4

FAR = (4, 3, 5, 2, 6, 1, 7, 0)
CORES = [(dz, dy, dc) for dz in FAR for dy in (1, 0) for dc in (0, 1) if (dz, dy, dc) != (0, 0, 0)]
CHIPS = [(dz, dy) for dz in FAR for dy in (1, 0) if (dz, dy) != (0, 0)]
NEAR = (0, 3, 1, 2)
SECTS = [(2, 1), (1, 1), (3, 1), (2, 0), (0, 1), (1, 0), (3, 0)]


def mul(value, factor):
    return pl.multiple_of(value * factor, factor)


def dot(a, b, dims):
    return lax.dot_general(a, b, dims, preferred_element_type=f32)


def gelu(v):
    return 0.5 * v * (1.0 + jnp.tanh(tanh_scale * (v + cubic_term * v * v * v)))


def slope(v):
    bent = jnp.tanh(tanh_scale * (v + cubic_term * v * v * v))
    return 0.5 * (1.0 + bent) + 0.5 * v * (1.0 - bent * bent) * tanh_scale * (
        1.0 + 3.0 * cubic_term * v * v
    )


class Sems:
    def __init__(self):
        self.count = 0

    def take(self, n):
        first = self.count
        self.count += n
        return first


SEMS = Sems()
LOAD = SEMS.take(16)
MX_S, MX_R = SEMS.take(1), SEMS.take(1)
MA_S, MA_R = SEMS.take(1), SEMS.take(15)
CX_S, CX_R = SEMS.take(8), SEMS.take(8)
RS_S, RS_R = SEMS.take(2), SEMS.take(32)
AG_S, AG_R = SEMS.take(2), SEMS.take(32)
FW_S, FW_R = SEMS.take(2), SEMS.take(32)
SX_S, SX_R = SEMS.take(8), SEMS.take(14)
M0_S, M0_R = SEMS.take(1), SEMS.take(31)
XW_S, XW_R = SEMS.take(7), SEMS.take(7)
XV_S, XV_R = SEMS.take(7), SEMS.take(7)
XF_S, XF_R = SEMS.take(1), SEMS.take(7)
SC_S, SC_R = SEMS.take(1), SEMS.take(7)
OX_S, OX_R = SEMS.take(7), SEMS.take(56)
OY_S, OY_R = SEMS.take(7), SEMS.take(56)
OF_S, OF_R = SEMS.take(1), SEMS.take(14)
ZX_S, ZX_R = SEMS.take(1), SEMS.take(7)
PA_S, PA_R = SEMS.take(2), SEMS.take(14)


SPLIT = 160


def kernel(*refs):
    sends = []
    steps(sends, *refs)
    for wait in sends:
        wait()


def steps(
    sends,
    lat, noi, gt, st, wmod, wup, bup, wdn, bdn, out,
    latv, noiv, wmodv, wupv, wdnv, bupv, bdnv,
    m0row, m0all, mblk, mpart, mcomb, mall, modv, modx,
    xn, xw, xm, hid, prev, slope_t,
    psend, precv, csum, rsrecv, nbuf, gbuf,
    x_all, sc_all, g_t, h_all, h_t, p_all, o_all, pg, hid_t,
    sem,
):
    s = lax.axis_index("section")
    t = lax.axis_index("tensor")
    x, yh = s // 2, s % 2
    z, yl, c = t // 4, (t // 2) % 2, t % 2
    q = c * 2 + yl

    def flush():
        for wait in sends:
            wait()
        sends.clear()

    def chip_at(dz, dy):
        return lax.rem(z + dz, 8), lax.rem(yl + dy, 2)

    def chip_dev(dz, dy):
        z2, y2 = chip_at(dz, dy)
        return (s, z2 * 4 + y2 * 2 + c)

    def core_dev(dz, dy, dc):
        z2, y2 = chip_at(dz, dy)
        return (s, z2 * 4 + y2 * 2 + lax.rem(c + dc, 2))

    def sect_at(dx, dy):
        return lax.rem(x + dx, 4) * 2 + lax.rem(yh + dy, 2)

    partner = (s, z * 4 + yl * 2 + (1 - c))

    def remote(src, dst, ssem, rsem, dev):
        return pltpu.make_async_remote_copy(
            src_ref=src, dst_ref=dst, send_sem=sem.at[ssem], recv_sem=sem.at[rsem],
            device_id=dev, device_id_type=MESH,
        )

    def sent(ref, k):
        sends.append(lambda: pltpu.make_async_copy(ref, ref, sem.at[k]).wait())

    barrier = pltpu.get_barrier_semaphore()
    for dz, dy, dc in CORES:
        pl.semaphore_signal(barrier, inc=1, device_id=core_dev(dz, dy, dc), device_id_type=MESH)
    for dx, dy in SECTS:
        pl.semaphore_signal(barrier, inc=1, device_id=(sect_at(dx, dy), t), device_id_type=MESH)

    pair = z // 2

    def owner(b, y2, h):
        return 2 * b + lax.rem(y2 + h, 2)

    def block_rows(h, b):
        return pl.ds(mul(4 * h + lax.rem(b, 2) * 2 + b // 2, 16), 16)

    def rows_of(z2, y2):
        return block_rows(lax.rem(z2 + y2, 2), z2 // 2)

    def load(k, src, dst):
        copy = pltpu.make_async_copy(src, dst, sem.at[LOAD + k])
        copy.start()
        return copy.wait

    ld_wmod = load(0, wmod, wmodv)
    ld_lat = load(1, lat, latv.at[:, 0:D])
    ld_up = [load(2, wup.at[0], wupv.at[0])]
    ld_bup = load(3, bup, bupv)
    ld_dn = [load(4, wdn.at[0], wdnv.at[0, :, 0:D])]
    ld_bdn = load(5, bdn, bdnv.at[:, 0:D])
    ld_noi = load(6, noi, noiv.at[:, 0:D])
    for n in (1, 2):
        ld_up.append(load(5 + 2 * n, wup.at[n], wupv.at[n]))
        ld_dn.append(load(6 + 2 * n, wdn.at[n], wdnv.at[n, :, 0:D]))

    lane = lax.broadcasted_iota(jnp.int32, (8, 128), 1).astype(f32)
    freq = jnp.exp(lane * (-math.log(10000.0) / 128))

    def embed(stamp):
        angle = stamp.astype(f32) * freq
        return jnp.concatenate([jnp.cos(angle), jnp.sin(angle)], axis=1).astype(bf16)

    emb_gen = embed(gt[s])
    emb_score = embed(st[s])
    sigma = st[s].astype(f32) / TRAIN_STEPS
    ld_wmod()
    row = lax.broadcasted_iota(jnp.int32, (8, MODC), 0)
    m0 = dot(emb_gen, wmodv[0], NT)
    m1 = dot(emb_score, wmodv[1], NT)
    m2 = dot(emb_score, wmodv[2], NT)
    m0row[...] = jnp.zeros_like(m0row)
    m0row[:, 0:MODC] = m0[0:1]
    mblk[...] = jnp.zeros_like(mblk)
    mblk[:, 0:MODC] = jnp.where(row % 4 == 1, m1, jnp.where(row % 4 == 2, m2, 0.0))
    modv[...] = jnp.zeros_like(modv)
    modx[...] = jnp.zeros_like(modx)
    latv[:, D:DP] = jnp.zeros((TOK, DP - D), bf16)
    noiv[:, D:DP] = jnp.zeros((TOK, DP - D), bf16)
    bdnv[:, D:DP] = jnp.zeros((3, DP - D), f32)
    for n in range(3):
        wdnv[n, :, D:DP] = jnp.zeros((F, DP - D), bf16)
    ld_lat()

    def norm_rows(values):
        mean = jnp.mean(values, axis=1, keepdims=True)
        centred = values - mean
        var = jnp.mean(centred * centred, axis=1, keepdims=True)
        return centred * lax.rsqrt(var + 1e-06)

    def norm_body(i, _):
        rows = pl.ds(mul(i, 16), 16)
        normed = norm_rows(latv[rows, 0:D].astype(f32))
        xn[rows, :] = normed
        xw[rows, 0:D] = normed.astype(bf16)
        return 0

    lax.fori_loop(0, 8, norm_body, 0)
    xw[:, D:DP] = jnp.zeros((TOK, DP - D), bf16)
    pl.semaphore_wait(barrier, 38)

    me = z * 4 + yl * 2 + c
    m0 = []
    for k, (dz, dy, dc) in enumerate(CORES):
        copy = remote(m0row, m0all.at[me], M0_S, M0_R + k, core_dev(dz, dy, dc))
        copy.start()
        m0.append(copy)
    sent(m0all.at[0:31], M0_S)
    mx = remote(mblk, mpart, MX_S, MX_R, partner)
    mx.start()
    sends.append(mx.wait_send)
    m0all[me] = m0row[...]

    def first_lane(section):
        return mul((19 * section) // 8, 128)

    def is_wide(section):
        return (section == 2) | (section == 5)

    mine = pl.ds(mul(c, 64), 64)

    def window_copy(k, last):
        dev = (sect_at(*SECTS[k]), t)
        lo, hi, base, recv = (384, 512, XV_S, XV_R) if last else (0, 384, XW_S, XW_R)
        return remote(
            xw.at[mine, pl.ds(pl.multiple_of(first_lane(dev[0]) + lo, 128), hi - lo)],
            x_all.at[s, mine, lo:hi], base + k, recv + k, dev,
        )

    def from_sect(k):
        dx, dy = SECTS[k]
        return sect_at((4 - dx) % 4, dy)

    def window_forward(k):
        part = x_all.at[from_sect(k), mine, :]
        return remote(part, part, XF_S, XF_R + k, partner)

    def scale_copy(k):
        dev = (sect_at(*SECTS[k]), t)
        return remote(modx.at[:, pl.ds(first_lane(dev[0]), 512)], sc_all.at[s], SC_S, SC_R + k, dev)

    mx.wait_recv()
    row8 = lax.broadcasted_iota(jnp.int32, (8, 256), 0)
    mcomb[...] = jnp.where((row8 < 4) == (c == 0), mblk[...], mpart[...])
    chip = z * 2 + yl
    ma = []
    for k, (dz, dy) in enumerate(CHIPS):
        copy = remote(mcomb, mall.at[chip], MA_S, MA_R + k, chip_dev(dz, dy))
        copy.start()
        ma.append(copy)
    sent(mall.at[0:15], MA_S)
    mall[chip] = mcomb[...]
    for k in range(7):
        window_copy(k, False).start()
        pl.when(is_wide(sect_at(*SECTS[k])))(lambda: window_copy(k, True).start())
        sends.append(window_copy(k, False).wait_send)
    x_all[s] = xw[:, pl.ds(first_lane(s), 512)]
    for copy in m0:
        copy.wait_recv()
    for k in range(32):
        modv[0:1, MODC * k : MODC * (k + 1)] = m0all[k, :, 0:MODC]

    def gen_body(i, _):
        rows = pl.ds(mul(i, 16), 16)
        xm[0, rows, :] = (xn[rows, :] * (1.0 + modv[0:1, D : 2 * D]) + modv[0:1, 0:D]).astype(bf16)
        return 0

    lax.fori_loop(0, 8, gen_body, 0)
    modx[0:1, 0:D] = modv[0:1, D : 2 * D]
    modx[1:2, 0:D] = modv[0:1, 0:D]
    for k in range(7):
        scale_copy(k).start()
    sent(sc_all.at[0:7], SC_S)
    sc_all[s] = modx[:, pl.ds(first_lane(s), 512)]
    ld_up[0]()
    ld_bup()
    ld_dn[0]()

    def gen_hidden(h):
        rows = slice(64 * h, 64 * h + 64)
        pre = dot(xm[0, rows], wupv[0], NT) + bupv[0:1, :]
        prev[rows, 0:F] = pre
        hid[0, rows] = gelu(pre).astype(bf16)

    def quarter(y2, core):
        return pl.ds(mul((core * 2 + y2) * (W // 128), 128), W)

    def core_copy(a, h, i):
        rows = pl.ds(64 * h, 64)
        k = (a * 2 + h) * 2 + i
        return remote(
            psend.at[a, rows, quarter(i, 1 - c)], precv.at[a, i, rows, :], CX_S + k, CX_R + k, partner
        )

    def produce(a, h, value):
        rows = slice(64 * h, 64 * h + 64)
        for core in (1 - c, c):
            cols = pl.ds(mul(core * (2 * W // 128), 128), 2 * W)
            psend[a, rows, cols] = value(rows, cols).astype(bf16)
            for i in range(2) if core is not c else []:
                core_copy(a, h, i).start()
                sends.append(core_copy(a, h, i).wait_send)

    def start_scatter(a, h):
        rows = pl.ds(64 * h, 64)
        for i in range(2):
            core_copy(a, h, i).wait_recv()
        for i in range(2):
            csum[a, i, rows, :] = (
                psend[a, rows, quarter(i, c)].astype(f32) + precv[a, i, rows, :].astype(f32)
            ).astype(bf16)
        for m in (2, 1, 3, 0):
            for dy in (1, 0):
                y2 = lax.rem(yl + dy, 2)
                z2 = owner(lax.rem(pair + m, 4), y2, h)
                dz = lax.rem(z2 + 8 - z, 8)
                copy = remote(
                    csum.at[a, y2, rows_of(z2, y2), :], rsrecv.at[a, dz * 2 + dy],
                    RS_S + a, RS_R + a * 16 + dz * 2 + dy, chip_dev(dz, dy),
                )
                if (m, dy) == (0, 0):
                    pl.when(dz != 0)(copy.start)
                else:
                    copy.start()

    def piece(out, z2, y2):
        return out.at[rows_of(z2, y2), quarter(y2, c)]

    def forward(a, out, dz, dy):
        z2, y2 = chip_at(8 - dz, dy)
        part = piece(out, z2, y2)
        return remote(part, part, FW_S + a, FW_R + a * 16 + dz * 2 + dy, partner)

    def gather(a, out, dz, dy):
        own = piece(out, z, yl)
        return remote(own, own, AG_S + a, AG_R + a * 16 + dz * 2 + dy, chip_dev(dz, dy))

    def reduce(a, finish, out):
        rows = rows_of(z, yl)
        total = csum[a, yl, rows, :].astype(f32)
        for dz, dy in reversed(CHIPS):
            slot = rsrecv.at[a, dz * 2 + dy]
            remote(slot, slot, RS_S + a, RS_R + a * 16 + dz * 2 + dy, partner).wait_recv()
            total = total + slot[...].astype(f32)
        sent(rsrecv.at[a, 0:15], RS_S + a)
        piece(out, z, yl)[...] = finish(total, rows, mul(q * (W // 128), 128), W)
        for dz, dy in CHIPS:
            gather(a, out, dz, dy).start()
        forward(a, out, 0, 0).start()
        sent(rsrecv.at[a, 0:15], AG_S + a)

    def source(h, m, dy):
        z2 = owner(lax.rem(pair + 4 - m, 4), lax.rem(yl + dy, 2), h)
        return lax.rem(z + 8 - z2, 8)

    def pass_on(a, h, out, m):
        for dy in (0, 1):
            dz = source(h, m, dy)

            def step():
                gather(a, out, dz, dy).wait_recv()
                forward(a, out, dz, dy).start()

            if (m, dy) == (0, 0):
                pl.when(dz != 0)(step)
            else:
                step()

    def complete(a, h, out, m, on_rows):
        for dy in (0, 1):
            forward(a, out, source(h, m, dy), dy).wait_recv()
        on_rows(h, m, block_rows(h, lax.rem(pair + 4 - m, 4)))

    def gather_first(a, out, on_rows):
        for step, m in enumerate(NEAR):
            pass_on(a, 0, out, m)
            if step > 0:
                complete(a, 0, out, NEAR[step - 1], on_rows)
        complete(a, 0, out, NEAR[-1], on_rows)

    def complete_second(a, out, on_rows):
        for m in NEAR:
            complete(a, 1, out, m, lambda h, m, rows: None)
        for m in NEAR:
            on_rows(1, m, block_rows(1, lax.rem(pair + 4 - m, 4)))

    def gen_value(rows, cols):
        return dot(hid[0, rows], wdnv[0, :, cols], NN)

    def finish_gen(total, rows, col, width):
        cols = pl.ds(col, width)
        gate = modv[0:1, pl.ds(pl.multiple_of(2 * D + col, 128), width)]
        generated = latv[rows, cols].astype(f32) + gate * (total + bdnv[0:1, cols])
        return (
            (1.0 - sigma) * generated + sigma * noiv[rows, cols].astype(f32)
        ).astype(bf16)

    def hidden_copy(k):
        cols = pl.ds(mul(s, 128), 128)
        return remote(hid_t, h_all.at[:, cols], SX_S + k, SX_R + k, (sect_at(*SECTS[k]), t))

    def relay_copy(k):
        dx, dy = SECTS[k]
        part = h_all.at[:, pl.ds(mul(sect_at(0, 1), 128), 128)]
        return remote(part, part, SX_S + k, SX_R + k, (sect_at(dx, 0), t))

    direct = [k for k in range(7) if SECTS[k][1] == 0] + [SECTS.index((0, 1))]
    relayed = [k for k in range(7) if k not in direct]

    def turn_hidden():
        prev[:, F:384] = jnp.zeros((TOK, 384 - F), f32)
        for b in range(3):
            height = min(128, F - 128 * b)
            block = prev[:, 128 * b : 128 * b + 128].T
            slope_t[128 * b : 128 * b + height, :] = slope(block)[0:height]
            hid_t[128 * b : 128 * b + height, :] = gelu(block)[0:height].astype(bf16)
        for k in direct:
            hidden_copy(k).start()
            sends.append(hidden_copy(k).wait_send)
        h_all[:, pl.ds(mul(s, 128), 128)] = hid_t[...]

    def other_modulation():
        ld_bdn()
        ld_noi()
        for copy in ma:
            copy.wait_recv()
        for k in range(32):
            modv[1:3, MODC * k : MODC * (k + 1)] = mall[k // 2, 4 * (k % 2) + 1 : 4 * (k % 2) + 3, 0:MODC]

    def pass_windows():
        for k in reversed(range(7)):
            window_copy(k, False).wait_recv()
            pl.when(is_wide(s))(lambda: window_copy(k, True).wait_recv())
            window_forward(k).start()
        sent(x_all.at[0:7, 0:64, :], XF_S)

    def relay_hidden():
        hidden_copy(SECTS.index((0, 1))).wait_recv()
        for k in relayed:
            relay_copy(k).start()
            sends.append(relay_copy(k).wait_send)

    def gather_inputs():
        for k in range(7):
            window_forward(k).wait_recv()
            scale_copy(k).wait_recv()

        def body(i, _):
            values = x_all[i].astype(f32) * (1.0 + sc_all[i, 0:1, :]) + sc_all[i, 1:2, :]
            values = values.astype(bf16).astype(f32)
            low = lax.broadcasted_iota(jnp.int32, (128, 128), 1) < 64
            for b in range(4):
                block = values[:, 128 * b : 128 * b + 128].T
                turned = pltpu.roll(block, 64, 1)
                at = (slice(128 * b, 128 * b + 128), pl.ds(mul(i, 128), 128))
                for h, r, value in ((0, 0, block), (0, 1, turned), (1, 0, turned), (1, 1, block)):
                    g_t[h, r, at[0], at[1]] = jnp.where(low == (r == 0), value, 0.0).astype(bf16)
            return 0

        lax.fori_loop(0, 8, body, 0)
        for k in range(7):
            if k != SECTS.index((0, 1)):
                (relay_copy(k) if k in relayed else hidden_copy(k)).wait_recv()
        for i in range(4):
            low = lax.broadcasted_iota(jnp.int32, (F, 128), 1) < 64
            first = h_all[:, 256 * i : 256 * i + 128].astype(f32)
            second = h_all[:, 256 * i + 128 : 256 * i + 256].astype(f32)
            cols = slice(128 * i, 128 * i + 128)
            h_t[0, :, cols] = jnp.where(low, first, pltpu.roll(second, 64, 1)).astype(bf16)
            h_t[1, :, cols] = jnp.where(low, pltpu.roll(first, 64, 1), second).astype(bf16)

    def score_rows(h, m, rows):
        normed = norm_rows(nbuf[rows, 0:D].astype(f32))
        for n in (1, 2):
            xm[n, rows, :] = (normed * (1.0 + modv[n : n + 1, D : 2 * D]) + modv[n : n + 1, 0:D]).astype(bf16)

    gen_hidden(0)
    produce(0, 0, gen_value)
    gen_hidden(1)
    start_scatter(0, 0)
    produce(0, 1, gen_value)
    turn_hidden()
    other_modulation()
    start_scatter(0, 1)
    pass_windows()
    reduce(0, finish_gen, nbuf)
    relay_hidden()

    def score_hidden(h):
        rows = slice(64 * h, 64 * h + 64)
        for n in (1, 2):
            hid[n, rows] = gelu(dot(xm[n, rows], wupv[n], NT) + bupv[n : n + 1, :]).astype(bf16)

    def gap_value(rows, cols):
        gates = pl.ds(pl.multiple_of(2 * D + cols.start, 128), 2 * W)
        real = dot(hid[1, rows], wdnv[1, :, cols], NN) * modv[1:2, gates]
        fake = dot(hid[2, rows], wdnv[2, :, cols], NN) * modv[2:3, gates]
        return fake - real

    for wait in ld_up[1:] + ld_dn[1:]:
        wait()
    gather_first(0, nbuf, score_rows)
    score_hidden(0)
    for m in NEAR:
        pass_on(0, 1, nbuf, m)
    produce(1, 0, gap_value)
    complete_second(0, nbuf, score_rows)
    sent(precv.at[0], FW_S)
    start_scatter(1, 0)
    score_hidden(1)
    produce(1, 1, gap_value)
    start_scatter(1, 1)

    def finish_gap(total, rows, col, width):
        cols = pl.ds(col, width)
        gates = modv[0:3, pl.ds(pl.multiple_of(2 * D + col, 128), width)]
        bias = gates[2:3] * bdnv[2:3, cols] - gates[1:2] * bdnv[1:2, cols]
        return ((total + bias) / 32.0 * gates[0:1]).astype(bf16)

    def slice_copy(h, m, k, last):
        dev = (sect_at(*SECTS[k]), t)
        rows = block_rows(h, lax.rem(pair + 4 - m, 4))
        lo, hi, base, recv = (384, 512, OY_S, OY_R) if last else (0, 384, OX_S, OX_R)
        return remote(
            gbuf.at[rows, pl.ds(pl.multiple_of(first_lane(dev[0]) + lo, 128), hi - lo)],
            o_all.at[s, rows, lo:hi], base + k, recv + 8 * k + 4 * h + m, dev,
        )

    beside_of = lax.rem(z, 2)

    def slice_beside(k):
        rows = block_rows(0, lax.rem(pair + 4 - c - 2 * beside_of, 4))
        part = o_all.at[from_sect(k), rows, :]
        dev = (s, (z + 1 - 2 * beside_of) * 4 + yl * 2 + c)
        return remote(part, part, ZX_S, ZX_R + k, dev)

    def grad_rows(h, m, rows):
        o_all[s, rows, :] = gbuf[rows, pl.ds(first_lane(s), 512)]

        @pl.when(c == m % 2)
        def _():
            for k in range(7):
                slice_copy(h, m, k, False).start()
                pl.when(is_wide(sect_at(*SECTS[k])))(lambda: slice_copy(h, m, k, True).start())

    def slice_forward(h, k):
        rows = pl.ds(mul(2 * h + lax.rem(pair + c, 2), 32), 32)
        part = o_all.at[from_sect(k), rows, :]
        return remote(part, part, OF_S, OF_R + 7 * h + k, partner)

    def wait_slices(h, k, m):
        slice_copy(h, m, k, False).wait_recv()
        pl.when(is_wide(s))(lambda: slice_copy(h, m, k, True).wait_recv())

    def share_slices():
        for k in reversed(range(7)):
            wait_slices(0, k, c + 2 * beside_of)
            slice_beside(k).start()
        sent(o_all.at[0:7, 0:16, :], ZX_S)

    def pass_slices(h):
        for k in reversed(range(7)):
            wait_slices(h, k, c)
            wait_slices(h, k, c + 2)
            slice_forward(h, k).start()

    def grad_copy(k):
        cols = pl.ds(mul(s, 128), 128)
        return remote(
            pg.at[1], p_all.at[1, :, cols], SX_S + 7, SX_R + 7 + k, (sect_at(*SECTS[k]), t)
        )

    RELAY = ((0, 64), (64, SPLIT))
    across = SECTS.index((0, 1))

    def first_copy(part, k):
        rows = slice(*RELAY[part])
        cols = pl.ds(mul(s, 128), 128)
        return remote(
            pg.at[0, rows], p_all.at[0, rows, cols], PA_S + part, PA_R + 7 * part + k, (sect_at(*SECTS[k]), t)
        )

    def first_relay(part, k):
        rows = slice(*RELAY[part])
        dx = SECTS[k][0]
        origin = sect_at(0, 1) if part == 0 else sect_at((4 - dx) % 4, 0)
        dev = sect_at(dx, 0) if part == 0 else sect_at(0, 1)
        block = p_all.at[0, rows, pl.ds(mul(origin, 128), 128)]
        return remote(block, block, PA_S + part, PA_R + 7 * part + k, (dev, t))

    def relay_first():
        first_copy(0, across).wait_recv()
        for k in relayed:
            first_relay(0, k).start()
        for k in relayed:
            first_copy(1, SECTS.index((SECTS[k][0], 0))).wait_recv()
            first_relay(1, k).start()
        for part in range(2):
            sent(p_all.at[0, RELAY[part][0] : RELAY[part][1], 0:896], PA_S + part)

    def wait_first():
        for k in direct:
            if k != across:
                first_copy(0, k).wait_recv()
        first_copy(1, across).wait_recv()
        for part in range(2):
            for k in relayed:
                first_relay(part, k).wait_recv()

    def hidden_grad(h):
        rows = slice(64 * h, 64 * h + 64)
        value = dot(wdnv[0, :, 0:D], gbuf[rows, 0:D], NT) * slope_t[:, rows]
        rest = jnp.concatenate([value[SPLIT:], jnp.zeros((2 * SPLIT - F, 64), f32)], axis=0)
        pg[h] = jnp.concatenate([value[0:SPLIT], rest], axis=1).astype(bf16)
        for k in range(7) if h == 1 else []:
            grad_copy(k).start()
        for part in range(2) if h == 0 else []:
            for k in direct:
                first_copy(part, k).start()
        p_all[h, :, pl.ds(mul(s, 128), 128)] = pg[h]

    flush()
    reduce(1, finish_gap, gbuf)
    gather_inputs()
    gather_first(1, gbuf, grad_rows)
    for m in NEAR:
        pass_on(1, 1, gbuf, m)
    hidden_grad(0)
    complete_second(1, gbuf, grad_rows)
    hidden_grad(1)
    sent(precv.at[1], FW_S + 1)
    for k in range(7):
        sent(o_all.at[0, 0:64, 0:384], OX_S + k)

    shift = pl.multiple_of(lax.rem(48 * s, 128), 16)

    def second_grad(h):
        for k in reversed(range(7)):
            slice_forward(h, k).wait_recv()
        return dot(h_t[h], o_all[:, 64 * h : 64 * h + 64, :].reshape(512, 512), NN)

    def store_second(wide):
        out[1] = pltpu.roll(wide, lax.rem(512 - shift, 512), 1)[:, 0:F]

    relay_first()
    pass_slices(0)
    pass_slices(1)
    flush()
    for k in range(7):

        @pl.when(is_wide(sect_at(*SECTS[k])))
        def _():
            window_copy(k, True).wait_send()
            last = o_all.at[0, 0:64, 384:512]
            pltpu.make_async_copy(last, last, sem.at[OY_S + k]).wait()

    flush()
    sent(o_all.at[0:7, 0:64, :], OF_S)
    rows = pl.ds(shift, F)

    def first_grad(h):
        if h == 0:
            wait_first()
        else:
            for k in reversed(range(7)):
                grad_copy(k).wait_recv()
        return [dot(g_t[h, r, rows, :], p_all[h], NT) for r in range(2)]

    wide_first = second_grad(0)
    sent(p_all.at[1, :, 0:896], SX_S + 7)
    late = first_grad(1)
    store_second(wide_first + second_grad(1))
    early = first_grad(0)
    out[0] = jnp.concatenate([early[0] + late[0], (early[1] + late[1])[:, 0 : F - SPLIT]], axis=1)
    flush()


def shards(latent_noise, score_noise, gen_time, score_time, w_mod, w_up, b_up, w_down, b_down):
    anywhere = pl.BlockSpec(memory_space=pl.ANY)
    scalars = pl.BlockSpec(memory_space=pltpu.SMEM)
    vm = pltpu.VMEM
    scratch = [
        vm((TOK, DP), bf16), vm((TOK, DP), bf16), vm((3, MODC, 256), bf16),
        vm((3, F, D), bf16), vm((3, F, DP), bf16), vm((3, F), f32), vm((3, DP), f32),
        vm((1, 256), f32), vm((32, 1, 256), f32),
        vm((8, 256), f32), vm((8, 256), f32), vm((8, 256), f32), vm((16, 8, 256), f32),
        vm((8, 7424), f32), vm((8, DP), f32),
        vm((TOK, D), f32), vm((TOK, DP), bf16), vm((3, TOK, D), bf16), vm((3, TOK, F), bf16), vm((TOK, 384), f32),
        vm((F, TOK), f32),
        vm((2, TOK, DP), bf16), vm((2, 2, TOK, W), bf16), vm((2, 2, TOK, W), bf16),
        vm((2, 16, 16, W), bf16),
        vm((TOK, DP), bf16), vm((TOK, DP), bf16),
        vm((8, TOK, 512), bf16), vm((8, 8, 512), f32), vm((2, 2, 512, 1024), bf16),
        vm((F, 1024), bf16), vm((2, F, 512), bf16), vm((2, SPLIT, 1024), bf16), vm((8, TOK, 512), bf16),
        vm((2, SPLIT, TOK), bf16), vm((F, TOK), bf16),
        pltpu.SemaphoreType.DMA((SEMS.count,)),
    ]
    grads = pl.pallas_call(
        kernel,
        out_shape=vm((2, F, F), f32),
        in_specs=[anywhere, anywhere, scalars, scalars] + [anywhere] * 5,
        out_specs=pl.BlockSpec(memory_space=pltpu.VMEM),
        scratch_shapes=scratch,
        cost_estimate=pl.CostEstimate(flops=1_700_000_000, bytes_accessed=11_000_000, transcendentals=300_000),
        compiler_params=pltpu.CompilerParams(
            collective_id=0, has_side_effects=True, vmem_limit_bytes=56 * 2**20
        ),
    )(
        latent_noise.reshape(TOK, D), score_noise.reshape(TOK, D), gen_time, score_time,
        w_mod.transpose(0, 2, 1), w_up.transpose(0, 2, 1), b_up, w_down, b_down,
    )
    return grads[0], grads[1]


def solution(mesh):
    placed = (
        P(None, "section", None),
        P(None, "section", None),
        P(),
        P(),
        P(None, None, "tensor"),
        P(None, None, "tensor"),
        P(None, "tensor"),
        P(None, "tensor", None),
        P(),
    )
    return jax.shard_map(
        shards,
        mesh=mesh,
        in_specs=placed,
        out_specs=(P("section", "tensor"), P("tensor", "section")),
        check_vma=False,
    )
```

```python
import functools
import math

import jax
import jax.numpy as jnp
from jax import lax
from jax.experimental import pallas as pl
from jax.experimental.pallas import tpu as pltpu
from jax.sharding import PartitionSpec as P

TRAIN_STEPS = 1000
MESH = pl.DeviceIdType.MESH
f32 = jnp.float32
bf16 = jnp.bfloat16

NT = (((1,), (1,)), ((), ()))
NN = (((1,), (0,)), ((), ()))

tanh_scale = math.sqrt(2.0 / math.pi)
cubic_term = 0.044715

TOK = 128
D = 2432
DP = 2560
F = 304
MODC = 228
W = DP // 4

FAR = (4, 3, 5, 2, 6, 1, 7, 0)
CORES = [(dz, dy, dc) for dz in FAR for dy in (1, 0) for dc in (0, 1) if (dz, dy, dc) != (0, 0, 0)]
CHIPS = [(dz, dy) for dz in FAR for dy in (1, 0) if (dz, dy) != (0, 0)]
NEAR = (0, 3, 1, 2)
SECTS = [(2, 1), (1, 1), (3, 1), (2, 0), (0, 1), (1, 0), (3, 0)]


def mul(value, factor):
    return pl.multiple_of(value * factor, factor)


def dot(a, b, dims):
    return lax.dot_general(a, b, dims, preferred_element_type=f32)


def gelu(v):
    return 0.5 * v * (1.0 + jnp.tanh(tanh_scale * (v + cubic_term * v * v * v)))


def slope(v):
    bent = jnp.tanh(tanh_scale * (v + cubic_term * v * v * v))
    return 0.5 * (1.0 + bent) + 0.5 * v * (1.0 - bent * bent) * tanh_scale * (
        1.0 + 3.0 * cubic_term * v * v
    )


class Sems:
    def __init__(self):
        self.count = 0

    def take(self, n):
        first = self.count
        self.count += n
        return first


SEMS = Sems()
LOAD = SEMS.take(16)
MX_S, MX_R = SEMS.take(1), SEMS.take(1)
MA_S, MA_R = SEMS.take(1), SEMS.take(15)
CX_S, CX_R = SEMS.take(8), SEMS.take(8)
RS_S, RS_R = SEMS.take(2), SEMS.take(32)
AG_S, AG_R = SEMS.take(2), SEMS.take(32)
FW_S, FW_R = SEMS.take(2), SEMS.take(32)
SX_S, SX_R = SEMS.take(8), SEMS.take(14)
M0_S, M0_R = SEMS.take(1), SEMS.take(31)
XW_S, XW_R = SEMS.take(7), SEMS.take(7)
XV_S, XV_R = SEMS.take(7), SEMS.take(7)
XF_S, XF_R = SEMS.take(1), SEMS.take(7)
SC_S, SC_R = SEMS.take(1), SEMS.take(7)
OX_S, OX_R = SEMS.take(7), SEMS.take(56)
OY_S, OY_R = SEMS.take(7), SEMS.take(56)
OF_S, OF_R = SEMS.take(1), SEMS.take(14)
ZX_S, ZX_R = SEMS.take(1), SEMS.take(7)
PA_S, PA_R = SEMS.take(2), SEMS.take(14)


SPLIT = 160


def kernel(*refs):
    sends = []
    steps(sends, *refs)
    for wait in sends:
        wait()


def steps(
    sends,
    lat, noi, gt, st, wmod, wup, bup, wdn, bdn, out,
    latv, noiv, wmodv, wupv, wdnv, bupv, bdnv,
    m0row, m0all, mblk, mpart, mcomb, mall, modv, modx,
    xn, xw, xm, hid, prev, slope_t,
    psend, precv, csum, rsrecv, nbuf, gbuf,
    x_all, sc_all, g_t, h_all, h_t, p_all, o_all, pg, hid_t,
    sem,
):
    s = lax.axis_index("section")
    t = lax.axis_index("tensor")
    x, yh = s // 2, s % 2
    z, yl, c = t // 4, (t // 2) % 2, t % 2
    q = c * 2 + yl

    def flush():
        for wait in sends:
            wait()
        sends.clear()

    def chip_at(dz, dy):
        return lax.rem(z + dz, 8), lax.rem(yl + dy, 2)

    def chip_dev(dz, dy):
        z2, y2 = chip_at(dz, dy)
        return (s, z2 * 4 + y2 * 2 + c)

    def core_dev(dz, dy, dc):
        z2, y2 = chip_at(dz, dy)
        return (s, z2 * 4 + y2 * 2 + lax.rem(c + dc, 2))

    def sect_at(dx, dy):
        return lax.rem(x + dx, 4) * 2 + lax.rem(yh + dy, 2)

    partner = (s, z * 4 + yl * 2 + (1 - c))

    def remote(src, dst, ssem, rsem, dev):
        return pltpu.make_async_remote_copy(
            src_ref=src, dst_ref=dst, send_sem=sem.at[ssem], recv_sem=sem.at[rsem],
            device_id=dev, device_id_type=MESH,
        )

    def sent(ref, k):
        sends.append(lambda: pltpu.make_async_copy(ref, ref, sem.at[k]).wait())

    barrier = pltpu.get_barrier_semaphore()
    for dz, dy, dc in CORES:
        pl.semaphore_signal(barrier, inc=1, device_id=core_dev(dz, dy, dc), device_id_type=MESH)
    for dx, dy in SECTS:
        pl.semaphore_signal(barrier, inc=1, device_id=(sect_at(dx, dy), t), device_id_type=MESH)

    pair = z // 2

    def owner(b, y2, h):
        return 2 * b + lax.rem(y2 + h, 2)

    def block_rows(h, b):
        return pl.ds(mul(4 * h + lax.rem(b, 2) * 2 + b // 2, 16), 16)

    def rows_of(z2, y2):
        return block_rows(lax.rem(z2 + y2, 2), z2 // 2)

    def load(k, src, dst):
        copy = pltpu.make_async_copy(src, dst, sem.at[LOAD + k])
        copy.start()
        return copy.wait

    ld_wmod = load(0, wmod, wmodv)
    ld_lat = load(1, lat, latv.at[:, 0:D])
    ld_up = [load(2, wup.at[0], wupv.at[0])]
    ld_bup = load(3, bup, bupv)
    ld_dn = [load(4, wdn.at[0], wdnv.at[0, :, 0:D])]
    ld_bdn = load(5, bdn, bdnv.at[:, 0:D])
    ld_noi = load(6, noi, noiv.at[:, 0:D])
    for n in (1, 2):
        ld_up.append(load(5 + 2 * n, wup.at[n], wupv.at[n]))
        ld_dn.append(load(6 + 2 * n, wdn.at[n], wdnv.at[n, :, 0:D]))

    lane = lax.broadcasted_iota(jnp.int32, (8, 128), 1).astype(f32)
    freq = jnp.exp(lane * (-math.log(10000.0) / 128))

    def embed(stamp):
        angle = stamp.astype(f32) * freq
        return jnp.concatenate([jnp.cos(angle), jnp.sin(angle)], axis=1).astype(bf16)

    emb_gen = embed(gt[s])
    emb_score = embed(st[s])
    sigma = st[s].astype(f32) / TRAIN_STEPS
    ld_wmod()
    row = lax.broadcasted_iota(jnp.int32, (8, MODC), 0)
    m0 = dot(emb_gen, wmodv[0], NT)
    m1 = dot(emb_score, wmodv[1], NT)
    m2 = dot(emb_score, wmodv[2], NT)
    m0row[...] = jnp.zeros_like(m0row)
    m0row[:, 0:MODC] = m0[0:1]
    mblk[...] = jnp.zeros_like(mblk)
    mblk[:, 0:MODC] = jnp.where(row % 4 == 1, m1, jnp.where(row % 4 == 2, m2, 0.0))
    modv[...] = jnp.zeros_like(modv)
    modx[...] = jnp.zeros_like(modx)
    latv[:, D:DP] = jnp.zeros((TOK, DP - D), bf16)
    noiv[:, D:DP] = jnp.zeros((TOK, DP - D), bf16)
    bdnv[:, D:DP] = jnp.zeros((3, DP - D), f32)
    for n in range(3):
        wdnv[n, :, D:DP] = jnp.zeros((F, DP - D), bf16)
    ld_lat()

    def norm_rows(values):
        mean = jnp.mean(values, axis=1, keepdims=True)
        centred = values - mean
        var = jnp.mean(centred * centred, axis=1, keepdims=True)
        return centred * lax.rsqrt(var + 1e-06)

    def norm_body(i, _):
        rows = pl.ds(mul(i, 16), 16)
        normed = norm_rows(latv[rows, 0:D].astype(f32))
        xn[rows, :] = normed
        xw[rows, 0:D] = normed.astype(bf16)
        return 0

    lax.fori_loop(0, 8, norm_body, 0)
    xw[:, D:DP] = jnp.zeros((TOK, DP - D), bf16)
    pl.semaphore_wait(barrier, 38)

    me = z * 4 + yl * 2 + c
    m0 = []
    for k, (dz, dy, dc) in enumerate(CORES):
        copy = remote(m0row, m0all.at[me], M0_S, M0_R + k, core_dev(dz, dy, dc))
        copy.start()
        m0.append(copy)
    sent(m0all.at[0:31], M0_S)
    mx = remote(mblk, mpart, MX_S, MX_R, partner)
    mx.start()
    sends.append(mx.wait_send)
    m0all[me] = m0row[...]

    def first_lane(section):
        return mul((19 * section) // 8, 128)

    def is_wide(section):
        return (section == 2) | (section == 5)

    mine = pl.ds(mul(c, 64), 64)

    def window_copy(k, last):
        dev = (sect_at(*SECTS[k]), t)
        lo, hi, base, recv = (384, 512, XV_S, XV_R) if last else (0, 384, XW_S, XW_R)
        return remote(
            xw.at[mine, pl.ds(pl.multiple_of(first_lane(dev[0]) + lo, 128), hi - lo)],
            x_all.at[s, mine, lo:hi], base + k, recv + k, dev,
        )

    def from_sect(k):
        dx, dy = SECTS[k]
        return sect_at((4 - dx) % 4, dy)

    def window_forward(k):
        part = x_all.at[from_sect(k), mine, :]
        return remote(part, part, XF_S, XF_R + k, partner)

    def scale_copy(k):
        dev = (sect_at(*SECTS[k]), t)
        return remote(modx.at[:, pl.ds(first_lane(dev[0]), 512)], sc_all.at[s], SC_S, SC_R + k, dev)

    mx.wait_recv()
    row8 = lax.broadcasted_iota(jnp.int32, (8, 256), 0)
    mcomb[...] = jnp.where((row8 < 4) == (c == 0), mblk[...], mpart[...])
    chip = z * 2 + yl
    ma = []
    for k, (dz, dy) in enumerate(CHIPS):
        copy = remote(mcomb, mall.at[chip], MA_S, MA_R + k, chip_dev(dz, dy))
        copy.start()
        ma.append(copy)
    sent(mall.at[0:15], MA_S)
    mall[chip] = mcomb[...]
    def send_windows(dy):
        for k in range(7):
            if SECTS[k][1] == dy:
                window_copy(k, False).start()
                pl.when(is_wide(sect_at(*SECTS[k])))(lambda: window_copy(k, True).start())
                sends.append(window_copy(k, False).wait_send)

    send_windows(0)
    x_all[s] = xw[:, pl.ds(first_lane(s), 512)]
    for copy in m0:
        copy.wait_recv()
    for k in range(32):
        modv[0:1, MODC * k : MODC * (k + 1)] = m0all[k, :, 0:MODC]

    def gen_body(i, _):
        rows = pl.ds(mul(i, 16), 16)
        xm[0, rows, :] = (xn[rows, :] * (1.0 + modv[0:1, D : 2 * D]) + modv[0:1, 0:D]).astype(bf16)
        return 0

    lax.fori_loop(0, 8, gen_body, 0)
    modx[0:1, 0:D] = modv[0:1, D : 2 * D]
    modx[1:2, 0:D] = modv[0:1, 0:D]
    for k in range(7):
        scale_copy(k).start()
    sent(sc_all.at[0:7], SC_S)
    sc_all[s] = modx[:, pl.ds(first_lane(s), 512)]
    ld_up[0]()
    ld_bup()
    ld_dn[0]()

    def gen_hidden(h):
        rows = slice(64 * h, 64 * h + 64)
        pre = dot(xm[0, rows], wupv[0], NT) + bupv[0:1, :]
        prev[rows, 0:F] = pre
        hid[0, rows] = gelu(pre).astype(bf16)

    def quarter(y2, core):
        return pl.ds(mul((core * 2 + y2) * (W // 128), 128), W)

    def core_copy(a, h, i):
        rows = pl.ds(64 * h, 64)
        k = (a * 2 + h) * 2 + i
        return remote(
            psend.at[a, rows, quarter(i, 1 - c)], precv.at[a, i, rows, :], CX_S + k, CX_R + k, partner
        )

    def produce(a, h, value):
        rows = slice(64 * h, 64 * h + 64)
        for core in (1 - c, c):
            cols = pl.ds(mul(core * (2 * W // 128), 128), 2 * W)
            psend[a, rows, cols] = value(rows, cols).astype(bf16)
            for i in range(2) if core is not c else []:
                core_copy(a, h, i).start()
                sends.append(core_copy(a, h, i).wait_send)

    def start_scatter(a, h):
        rows = pl.ds(64 * h, 64)
        for i in range(2):
            core_copy(a, h, i).wait_recv()
        for i in range(2):
            csum[a, i, rows, :] = (
                psend[a, rows, quarter(i, c)].astype(f32) + precv[a, i, rows, :].astype(f32)
            ).astype(bf16)
        for m in (2, 1, 3, 0):
            for dy in (1, 0):
                y2 = lax.rem(yl + dy, 2)
                z2 = owner(lax.rem(pair + m, 4), y2, h)
                dz = lax.rem(z2 + 8 - z, 8)
                copy = remote(
                    csum.at[a, y2, rows_of(z2, y2), :], rsrecv.at[a, dz * 2 + dy],
                    RS_S + a, RS_R + a * 16 + dz * 2 + dy, chip_dev(dz, dy),
                )
                if (m, dy) == (0, 0):
                    pl.when(dz != 0)(copy.start)
                else:
                    copy.start()

    def piece(out, z2, y2):
        return out.at[rows_of(z2, y2), quarter(y2, c)]

    def forward(a, out, dz, dy):
        z2, y2 = chip_at(8 - dz, dy)
        part = piece(out, z2, y2)
        return remote(part, part, FW_S + a, FW_R + a * 16 + dz * 2 + dy, partner)

    def gather(a, out, dz, dy):
        own = piece(out, z, yl)
        return remote(own, own, AG_S + a, AG_R + a * 16 + dz * 2 + dy, chip_dev(dz, dy))

    def reduce(a, finish, out):
        rows = rows_of(z, yl)
        total = csum[a, yl, rows, :].astype(f32)
        for dz, dy in reversed(CHIPS):
            slot = rsrecv.at[a, dz * 2 + dy]
            remote(slot, slot, RS_S + a, RS_R + a * 16 + dz * 2 + dy, partner).wait_recv()
            total = total + slot[...].astype(f32)
        sent(rsrecv.at[a, 0:15], RS_S + a)
        piece(out, z, yl)[...] = finish(total, rows, mul(q * (W // 128), 128), W)
        for dz, dy in CHIPS:
            gather(a, out, dz, dy).start()
        forward(a, out, 0, 0).start()
        sent(rsrecv.at[a, 0:15], AG_S + a)

    def source(h, m, dy):
        z2 = owner(lax.rem(pair + 4 - m, 4), lax.rem(yl + dy, 2), h)
        return lax.rem(z + 8 - z2, 8)

    def pass_on(a, h, out, m):
        for dy in (0, 1):
            dz = source(h, m, dy)

            def step():
                gather(a, out, dz, dy).wait_recv()
                forward(a, out, dz, dy).start()

            if (m, dy) == (0, 0):
                pl.when(dz != 0)(step)
            else:
                step()

    def complete(a, h, out, m, on_rows):
        for dy in (0, 1):
            forward(a, out, source(h, m, dy), dy).wait_recv()
        on_rows(h, m, block_rows(h, lax.rem(pair + 4 - m, 4)))

    def gather_first(a, out, on_rows):
        for step, m in enumerate(NEAR):
            pass_on(a, 0, out, m)
            if step > 0:
                complete(a, 0, out, NEAR[step - 1], on_rows)
        complete(a, 0, out, NEAR[-1], on_rows)

    def complete_second(a, out, on_rows):
        for m in NEAR:
            complete(a, 1, out, m, lambda h, m, rows: None)
        for m in NEAR:
            on_rows(1, m, block_rows(1, lax.rem(pair + 4 - m, 4)))

    def gen_value(rows, cols):
        return dot(hid[0, rows], wdnv[0, :, cols], NN)

    def finish_gen(total, rows, col, width):
        cols = pl.ds(col, width)
        gate = modv[0:1, pl.ds(pl.multiple_of(2 * D + col, 128), width)]
        generated = latv[rows, cols].astype(f32) + gate * (total + bdnv[0:1, cols])
        return (
            (1.0 - sigma) * generated + sigma * noiv[rows, cols].astype(f32)
        ).astype(bf16)

    def hidden_copy(k):
        cols = pl.ds(mul(s, 128), 128)
        return remote(hid_t, h_all.at[:, cols], SX_S + k, SX_R + k, (sect_at(*SECTS[k]), t))

    def relay_copy(k):
        dx, dy = SECTS[k]
        part = h_all.at[:, pl.ds(mul(sect_at(0, 1), 128), 128)]
        return remote(part, part, SX_S + k, SX_R + k, (sect_at(dx, 0), t))

    direct = [k for k in range(7) if SECTS[k][1] == 0] + [SECTS.index((0, 1))]
    relayed = [k for k in range(7) if k not in direct]

    def turn_hidden():
        prev[:, F:384] = jnp.zeros((TOK, 384 - F), f32)
        for b in range(3):
            height = min(128, F - 128 * b)
            block = prev[:, 128 * b : 128 * b + 128].T
            slope_t[128 * b : 128 * b + height, :] = slope(block)[0:height]
            hid_t[128 * b : 128 * b + height, :] = gelu(block)[0:height].astype(bf16)
        for k in direct:
            hidden_copy(k).start()
            sends.append(hidden_copy(k).wait_send)
        h_all[:, pl.ds(mul(s, 128), 128)] = hid_t[...]

    def other_modulation():
        ld_bdn()
        ld_noi()
        for copy in ma:
            copy.wait_recv()
        for k in range(32):
            modv[1:3, MODC * k : MODC * (k + 1)] = mall[k // 2, 4 * (k % 2) + 1 : 4 * (k % 2) + 3, 0:MODC]

    def pass_windows():
        for k in reversed(range(7)):
            window_copy(k, False).wait_recv()
            pl.when(is_wide(s))(lambda: window_copy(k, True).wait_recv())
            window_forward(k).start()
        sent(x_all.at[0:7, 0:64, :], XF_S)

    def relay_hidden():
        hidden_copy(SECTS.index((0, 1))).wait_recv()
        for k in relayed:
            relay_copy(k).start()
            sends.append(relay_copy(k).wait_send)

    def gather_inputs():
        for k in range(7):
            window_forward(k).wait_recv()
            scale_copy(k).wait_recv()

        def body(i, _):
            values = x_all[i].astype(f32) * (1.0 + sc_all[i, 0:1, :]) + sc_all[i, 1:2, :]
            values = values.astype(bf16).astype(f32)
            low = lax.broadcasted_iota(jnp.int32, (128, 128), 1) < 64
            for b in range(4):
                block = values[:, 128 * b : 128 * b + 128].T
                turned = pltpu.roll(block, 64, 1)
                at = (slice(128 * b, 128 * b + 128), pl.ds(mul(i, 128), 128))
                for h, r, value in ((0, 0, block), (0, 1, turned), (1, 0, turned), (1, 1, block)):
                    g_t[h, r, at[0], at[1]] = jnp.where(low == (r == 0), value, 0.0).astype(bf16)
            return 0

        lax.fori_loop(0, 8, body, 0)
        for k in range(7):
            if k != SECTS.index((0, 1)):
                (relay_copy(k) if k in relayed else hidden_copy(k)).wait_recv()
        for i in range(4):
            low = lax.broadcasted_iota(jnp.int32, (F, 128), 1) < 64
            first = h_all[:, 256 * i : 256 * i + 128].astype(f32)
            second = h_all[:, 256 * i + 128 : 256 * i + 256].astype(f32)
            cols = slice(128 * i, 128 * i + 128)
            h_t[0, :, cols] = jnp.where(low, first, pltpu.roll(second, 64, 1)).astype(bf16)
            h_t[1, :, cols] = jnp.where(low, pltpu.roll(first, 64, 1), second).astype(bf16)

    def score_rows(h, m, rows):
        normed = norm_rows(nbuf[rows, 0:D].astype(f32))
        for n in (1, 2):
            xm[n, rows, :] = (normed * (1.0 + modv[n : n + 1, D : 2 * D]) + modv[n : n + 1, 0:D]).astype(bf16)

    gen_hidden(0)
    produce(0, 0, gen_value)
    gen_hidden(1)
    start_scatter(0, 0)
    produce(0, 1, gen_value)
    turn_hidden()
    other_modulation()
    start_scatter(0, 1)
    reduce(0, finish_gen, nbuf)
    relay_hidden()

    def score_hidden(h):
        rows = slice(64 * h, 64 * h + 64)
        for n in (1, 2):
            hid[n, rows] = gelu(dot(xm[n, rows], wupv[n], NT) + bupv[n : n + 1, :]).astype(bf16)

    def gap_value(rows, cols):
        gates = pl.ds(pl.multiple_of(2 * D + cols.start, 128), 2 * W)
        real = dot(hid[1, rows], wdnv[1, :, cols], NN) * modv[1:2, gates]
        fake = dot(hid[2, rows], wdnv[2, :, cols], NN) * modv[2:3, gates]
        return fake - real

    for wait in ld_up[1:] + ld_dn[1:]:
        wait()
    gather_first(0, nbuf, score_rows)
    send_windows(1)
    score_hidden(0)
    for m in NEAR:
        pass_on(0, 1, nbuf, m)
    produce(1, 0, gap_value)
    complete_second(0, nbuf, score_rows)
    sent(precv.at[0], FW_S)
    start_scatter(1, 0)
    score_hidden(1)
    produce(1, 1, gap_value)
    start_scatter(1, 1)

    def finish_gap(total, rows, col, width):
        cols = pl.ds(col, width)
        gates = modv[0:3, pl.ds(pl.multiple_of(2 * D + col, 128), width)]
        bias = gates[2:3] * bdnv[2:3, cols] - gates[1:2] * bdnv[1:2, cols]
        return ((total + bias) / 32.0 * gates[0:1]).astype(bf16)

    def slice_copy(h, m, k, last):
        dev = (sect_at(*SECTS[k]), t)
        rows = block_rows(h, lax.rem(pair + 4 - m, 4))
        lo, hi, base, recv = (384, 512, OY_S, OY_R) if last else (0, 384, OX_S, OX_R)
        return remote(
            gbuf.at[rows, pl.ds(pl.multiple_of(first_lane(dev[0]) + lo, 128), hi - lo)],
            o_all.at[s, rows, lo:hi], base + k, recv + 8 * k + 4 * h + m, dev,
        )

    beside_of = lax.rem(z, 2)

    def slice_beside(k):
        rows = block_rows(0, lax.rem(pair + 4 - c - 2 * beside_of, 4))
        part = o_all.at[from_sect(k), rows, :]
        dev = (s, (z + 1 - 2 * beside_of) * 4 + yl * 2 + c)
        return remote(part, part, ZX_S, ZX_R + k, dev)

    def grad_rows(h, m, rows):
        o_all[s, rows, :] = gbuf[rows, pl.ds(first_lane(s), 512)]

        @pl.when(c == m % 2)
        def _():
            for k in range(7):
                slice_copy(h, m, k, False).start()
                pl.when(is_wide(sect_at(*SECTS[k])))(lambda: slice_copy(h, m, k, True).start())

    def slice_forward(h, k):
        rows = pl.ds(mul(2 * h + lax.rem(pair + c, 2), 32), 32)
        part = o_all.at[from_sect(k), rows, :]
        return remote(part, part, OF_S, OF_R + 7 * h + k, partner)

    def wait_slices(h, k, m):
        slice_copy(h, m, k, False).wait_recv()
        pl.when(is_wide(s))(lambda: slice_copy(h, m, k, True).wait_recv())

    def share_slices():
        for k in reversed(range(7)):
            wait_slices(0, k, c + 2 * beside_of)
            slice_beside(k).start()
        sent(o_all.at[0:7, 0:16, :], ZX_S)

    def pass_slices(h):
        for k in reversed(range(7)):
            wait_slices(h, k, c)
            wait_slices(h, k, c + 2)
            slice_forward(h, k).start()

    def grad_copy(k):
        cols = pl.ds(mul(s, 128), 128)
        return remote(
            pg.at[1], p_all.at[1, :, cols], SX_S + 7, SX_R + 7 + k, (sect_at(*SECTS[k]), t)
        )

    RELAY = ((0, 64), (64, SPLIT))
    across = SECTS.index((0, 1))

    def first_copy(part, k):
        rows = slice(*RELAY[part])
        cols = pl.ds(mul(s, 128), 128)
        return remote(
            pg.at[0, rows], p_all.at[0, rows, cols], PA_S + part, PA_R + 7 * part + k, (sect_at(*SECTS[k]), t)
        )

    def first_relay(part, k):
        rows = slice(*RELAY[part])
        dx = SECTS[k][0]
        origin = sect_at(0, 1) if part == 0 else sect_at((4 - dx) % 4, 0)
        dev = sect_at(dx, 0) if part == 0 else sect_at(0, 1)
        block = p_all.at[0, rows, pl.ds(mul(origin, 128), 128)]
        return remote(block, block, PA_S + part, PA_R + 7 * part + k, (dev, t))

    def relay_first():
        first_copy(0, across).wait_recv()
        for k in relayed:
            first_relay(0, k).start()
        for k in relayed:
            first_copy(1, SECTS.index((SECTS[k][0], 0))).wait_recv()
            first_relay(1, k).start()
        for part in range(2):
            sent(p_all.at[0, RELAY[part][0] : RELAY[part][1], 0:896], PA_S + part)

    def wait_first():
        for k in direct:
            if k != across:
                first_copy(0, k).wait_recv()
        first_copy(1, across).wait_recv()
        for part in range(2):
            for k in relayed:
                first_relay(part, k).wait_recv()

    def hidden_grad(h):
        rows = slice(64 * h, 64 * h + 64)
        value = dot(wdnv[0, :, 0:D], gbuf[rows, 0:D], NT) * slope_t[:, rows]
        rest = jnp.concatenate([value[SPLIT:], jnp.zeros((2 * SPLIT - F, 64), f32)], axis=0)
        pg[h] = jnp.concatenate([value[0:SPLIT], rest], axis=1).astype(bf16)
        for k in range(7) if h == 1 else []:
            grad_copy(k).start()
        for part in range(2) if h == 0 else []:
            for k in direct:
                first_copy(part, k).start()
        p_all[h, :, pl.ds(mul(s, 128), 128)] = pg[h]

    flush()
    reduce(1, finish_gap, gbuf)
    pass_windows()
    gather_inputs()
    gather_first(1, gbuf, grad_rows)
    for m in NEAR:
        pass_on(1, 1, gbuf, m)
    hidden_grad(0)
    complete_second(1, gbuf, grad_rows)
    hidden_grad(1)
    sent(precv.at[1], FW_S + 1)
    for k in range(7):
        sent(o_all.at[0, 0:64, 0:384], OX_S + k)

    shift = pl.multiple_of(lax.rem(48 * s, 128), 16)

    def second_grad(h):
        for k in reversed(range(7)):
            slice_forward(h, k).wait_recv()
        return dot(h_t[h], o_all[:, 64 * h : 64 * h + 64, :].reshape(512, 512), NN)

    def store_second(wide):
        out[1] = pltpu.roll(wide, lax.rem(512 - shift, 512), 1)[:, 0:F]

    relay_first()
    pass_slices(0)
    pass_slices(1)
    flush()
    for k in range(7):

        @pl.when(is_wide(sect_at(*SECTS[k])))
        def _():
            window_copy(k, True).wait_send()
            last = o_all.at[0, 0:64, 384:512]
            pltpu.make_async_copy(last, last, sem.at[OY_S + k]).wait()

    flush()
    sent(o_all.at[0:7, 0:64, :], OF_S)
    rows = pl.ds(shift, F)

    def first_grad(h):
        if h == 0:
            wait_first()
        else:
            for k in reversed(range(7)):
                grad_copy(k).wait_recv()
        return [dot(g_t[h, r, rows, :], p_all[h], NT) for r in range(2)]

    wide_first = second_grad(0)
    sent(p_all.at[1, :, 0:896], SX_S + 7)
    late = first_grad(1)
    store_second(wide_first + second_grad(1))
    early = first_grad(0)
    out[0] = jnp.concatenate([early[0] + late[0], (early[1] + late[1])[:, 0 : F - SPLIT]], axis=1)
    flush()


def shards(latent_noise, score_noise, gen_time, score_time, w_mod, w_up, b_up, w_down, b_down):
    anywhere = pl.BlockSpec(memory_space=pl.ANY)
    scalars = pl.BlockSpec(memory_space=pltpu.SMEM)
    vm = pltpu.VMEM
    scratch = [
        vm((TOK, DP), bf16), vm((TOK, DP), bf16), vm((3, MODC, 256), bf16),
        vm((3, F, D), bf16), vm((3, F, DP), bf16), vm((3, F), f32), vm((3, DP), f32),
        vm((1, 256), f32), vm((32, 1, 256), f32),
        vm((8, 256), f32), vm((8, 256), f32), vm((8, 256), f32), vm((16, 8, 256), f32),
        vm((8, 7424), f32), vm((8, DP), f32),
        vm((TOK, D), f32), vm((TOK, DP), bf16), vm((3, TOK, D), bf16), vm((3, TOK, F), bf16), vm((TOK, 384), f32),
        vm((F, TOK), f32),
        vm((2, TOK, DP), bf16), vm((2, 2, TOK, W), bf16), vm((2, 2, TOK, W), bf16),
        vm((2, 16, 16, W), bf16),
        vm((TOK, DP), bf16), vm((TOK, DP), bf16),
        vm((8, TOK, 512), bf16), vm((8, 8, 512), f32), vm((2, 2, 512, 1024), bf16),
        vm((F, 1024), bf16), vm((2, F, 512), bf16), vm((2, SPLIT, 1024), bf16), vm((8, TOK, 512), bf16),
        vm((2, SPLIT, TOK), bf16), vm((F, TOK), bf16),
        pltpu.SemaphoreType.DMA((SEMS.count,)),
    ]
    grads = pl.pallas_call(
        kernel,
        out_shape=vm((2, F, F), f32),
        in_specs=[anywhere, anywhere, scalars, scalars] + [anywhere] * 5,
        out_specs=pl.BlockSpec(memory_space=pltpu.VMEM),
        scratch_shapes=scratch,
        cost_estimate=pl.CostEstimate(flops=1_700_000_000, bytes_accessed=11_000_000, transcendentals=300_000),
        compiler_params=pltpu.CompilerParams(
            collective_id=0, has_side_effects=True, vmem_limit_bytes=56 * 2**20
        ),
    )(
        latent_noise.reshape(TOK, D), score_noise.reshape(TOK, D), gen_time, score_time,
        w_mod.transpose(0, 2, 1), w_up.transpose(0, 2, 1), b_up, w_down, b_down,
    )
    return grads[0], grads[1]


def solution(mesh):
    placed = (
        P(None, "section", None),
        P(None, "section", None),
        P(),
        P(),
        P(None, None, "tensor"),
        P(None, None, "tensor"),
        P(None, "tensor"),
        P(None, "tensor", None),
        P(),
    )
    return jax.shard_map(
        shards,
        mesh=mesh,
        in_specs=placed,
        out_specs=(P("section", "tensor"), P("tensor", "section")),
        check_vma=False,
    )
```
